128 devices in a mesh: gx: 8 (over x, y_lo), gy: 8 (over z, core), gz: 2 (over y_hi).
Axes of the slice: x: 4, y: 4 (y_hi: 2, y_lo: 2; y = y_hi * 2 + y_lo), z: 4, core: 2. Of those that a mesh axis runs over, the one named last changes fastest.
Arguments:
- gradient: float32 [3, 64, 256, 1024], P(None, 'gz', 'gx', 'gy'), may hold values from -6 to 6
- right_side: float32 [3, 8, 32, 128], P(None, 'gz', 'gx', 'gy'), may hold values from -6 to 6
Outputs:
- solution: float32 [3, 8, 32, 128], P(None, 'gz', 'gx', 'gy')
- residual: float32 [3, 8, 32, 128], P(None, 'gz', 'gx', 'gy')
The draws below stay inside these ranges and needn't reach their ends.
All inputs are finite; a program needn't handle non-finite values.
Results may differ from the reference program's by a relative error of at most 0.0003.
Values sent between devices are 32-bit elements; how exact they have to be, the bound alone decides.
No kernel may reach another device: no remote copies, remote signals or barrier semaphores. Data moves between devices by JAX's collectives and lax.ppermute only.
A program may use at most 64 MiB of HBM per device.

```python
import jax
import jax.numpy as jnp
from jax import lax

ITERS = 6
NX = 256
NY = 1024
NZ = 64
NLX = 32
NLY = 128
NLZ = 8


def level_of(stream_key, extent, split, smallest, top_value):
    loudness, own = 1.0, jax.random.fold_in(stream_key, 6)
    for dim, shards_of in split:
        draws = jnp.exp(jax.random.uniform(jax.random.fold_in(own, dim), (shards_of,), jnp.float32, smallest / len(split), top_value / len(split)))
        loudness = loudness * jnp.repeat(draws, extent[dim] // shards_of).reshape([-1 if axis == dim else 1 for axis in range(len(extent))])
    return loudness


def noise(key, shape, width, reach, split=(), kind=jnp.bfloat16):
    values = width * jax.random.normal(key, shape, jnp.float32)
    if split:
        values = values * level_of(key, shape, split, -0.22, 0.18)
    return jnp.clip(values, -reach, reach).astype(kind)


def setup_inputs(seed: int = 0) -> dict:
    keys = jax.random.split(jax.random.key(seed), 3)
    gradient = noise(keys[0], (3, NZ, NX, NY), 1.0, 6.0, ((1, 2), (2, 8), (3, 8)), jnp.float32)
    right_side = noise(keys[1], (3, NLZ, NLX, NLY), 1.0, 6.0, ((1, 2), (2, 8), (3, 8)), jnp.float32)
    return dict(gradient=gradient, right_side=right_side)


SMOOTHING = 0.5
DAMPING = 0.05
PRECISE = lax.Precision.HIGHEST


def spline_table(number_rows, columns, first_voxel, offset):
    voxels = jnp.arange(number_rows, dtype=jnp.int32)[:, None] + first_voxel
    cells = voxels // 8
    fraction = (voxels - 8 * cells).astype(jnp.float32) / 8.0
    rest = 1.0 - fraction
    position = jnp.arange(columns, dtype=jnp.int32)[None, :] - cells + offset
    weight_first = rest * rest * rest / 6.0
    weight_second = (3.0 * fraction ** 3 - 6.0 * fraction ** 2 + 4.0) / 6.0
    weight_third = (-3.0 * fraction ** 3 + 3.0 * fraction ** 2 + 3.0 * fraction + 1.0) / 6.0
    weight_last = fraction ** 3 / 6.0
    table = jnp.where(position == 0, weight_first, 0.0)
    table = table + jnp.where(position == 1, weight_second, 0.0)
    table = table + jnp.where(position == 2, weight_third, 0.0)
    table = table + jnp.where(position == 3, weight_last, 0.0)
    return table


def evaluate(lattice, table_z, table_x, table_y):
    along_y = jnp.einsum("czxb,yb->czxy", lattice, table_y, precision=PRECISE)
    along_x = jnp.einsum("czby,xb->czxy", along_y, table_x, precision=PRECISE)
    return jnp.einsum("cbxy,zb->czxy", along_x, table_z, precision=PRECISE)


def adjoint(field, table_z, table_x, table_y):
    along_z = jnp.einsum("czxy,zb->cbxy", field, table_z, precision=PRECISE)
    along_x = jnp.einsum("cbxy,xa->cbay", along_z, table_x, precision=PRECISE)
    return jnp.einsum("cbay,yd->cbad", along_x, table_y, precision=PRECISE)


def relief_of(beside_all):
    center = beside_all[:, 1:-1, 1:-1, 1:-1]
    beside = beside_all[:, 2:, 1:-1, 1:-1] + beside_all[:, :-2, 1:-1, 1:-1]
    beside = beside + beside_all[:, 1:-1, 2:, 1:-1] + beside_all[:, 1:-1, :-2, 1:-1]
    beside = beside + beside_all[:, 1:-1, 1:-1, 2:] + beside_all[:, 1:-1, 1:-1, :-2]
    return 6.0 * center - beside


def reference(gradient, right_side):
    table_z = spline_table(NZ, NLZ, 0, 1)
    table_x = spline_table(NX, NLX, 0, 1)
    table_y = spline_table(NY, NLY, 0, 1)

    def operate(direction):
        field = evaluate(direction, table_z, table_x, table_y)
        beside_all = jnp.pad(field, ((0, 0), (1, 1), (1, 1), (1, 1)))
        shade = jnp.sum(gradient * field, axis=0)
        weighted = gradient * shade[None] + SMOOTHING * relief_of(beside_all)
        return adjoint(weighted, table_z, table_x, table_y) + DAMPING * direction

    solution = jnp.zeros_like(right_side)
    residual = right_side
    direction = right_side
    norm_now = jnp.sum(residual * residual)
    for number in range(ITERS):
        image = operate(direction)
        step_size = norm_now / jnp.sum(direction * image)
        solution = solution + step_size * direction
        residual = residual - step_size * image
        norm_next = jnp.sum(residual * residual)
        direction = residual + (norm_next / norm_now) * direction
        norm_now = norm_next
    return solution, residual
```

```python
import functools

import jax
import jax.numpy as jnp
import ml_dtypes
import numpy as np
from jax import lax
from jax.experimental import pallas as pl
from jax.experimental.pallas import tpu as pltpu
from jax.sharding import PartitionSpec as P

ITERS = 6
SMOOTHING = 0.5
DAMPING = 0.05
HIGHEST = lax.Precision.HIGHEST

CELLS_Z, CELLS_X, CELLS_Y = 4, 4, 16
BOX_X, BOX_Y, BOX_Z = 7, 19, 6
LANES = 128
ROWS = 24
DENOMINATOR = 3072.0


def numerators(t):
    return (
        (8 - t) ** 3,
        3 * t**3 - 48 * t**2 + 2048,
        -3 * t**3 + 24 * t**2 + 192 * t + 512,
        t**3,
    )


WEIGHTS = [[n / DENOMINATOR for n in numerators(t)] for t in range(8)]


def basis(cells):
    table = np.zeros((8 * cells + 1, cells + 3 + 1))
    for voxel in range(8 * cells + 1):
        for k, n in enumerate(numerators(voxel % 8)):
            table[voxel, voxel // 8 + k] = n
    return table[:, :-1]


def mass_and_edges(cells, first, last):
    table = basis(cells) / DENOMINATOR
    own = table[:-1]
    steps = table[1:] - table[:-1]
    if last:
        steps[-1] = -table[-2]
    edges = steps.T @ steps
    if first:
        edges = edges + np.outer(table[0], table[0])
    return own.T @ own, edges


def place_z(matrix, part):
    return matrix[1:7, 1:7] if part == 0 else matrix[0:6, 0:6]


@functools.lru_cache(None)
def tables():
    bx = basis(CELLS_X)[:-1]
    expand = np.zeros((96, ROWS))
    for c in range(3):
        expand[c * 32 : c * 32 + 32, c * 8 : c * 8 + BOX_X] = bx / DENOMINATOR / DENOMINATOR
    rows_x = np.zeros((3, 144, ROWS), np.float32)
    for kind in range(3):
        mass, edges = mass_and_edges(CELLS_X, kind == 0, kind == 2)
        rows_x[kind, :96] = expand
        for c in range(3):
            at = slice(c * 8, c * 8 + BOX_X)
            rows_x[kind, 96 + c * 8 : 96 + c * 8 + BOX_X, at] = SMOOTHING * mass
            rows_x[kind, 120 + c * 8 : 120 + c * 8 + BOX_X, at] = SMOOTHING * edges
    by = basis(CELLS_Y)[:-1]
    along_y = np.zeros((2, 2, LANES, 7 * LANES))
    for part in range(2):
        for f in range(BOX_Z):
            g = f + 1 if part == 0 else f
            low = by.T.astype(ml_dtypes.bfloat16).astype(np.float64)
            at = slice(f * BOX_Y, (f + 1) * BOX_Y)
            along_y[part, 0, at, g * LANES : (g + 1) * LANES] = low
            along_y[part, 1, at, g * LANES : (g + 1) * LANES] = by.T - low
    along_y = along_y.reshape(2, 256, 7 * LANES).astype(ml_dtypes.bfloat16)
    lanes = np.zeros((2, 3, 256, LANES), np.float32)
    for part in range(2):
        mz, kz = mass_and_edges(CELLS_Z, part == 0, part == 1)
        mz, kz = place_z(mz, part), place_z(kz, part)
        for kind in range(3):
            my, ky = mass_and_edges(CELLS_Y, kind == 0, kind == 2)
            used = BOX_Z * BOX_Y
            lanes[part, kind, :used, :used] = np.kron(kz, my) + np.kron(mz, ky)
            lanes[part, kind, 128 : 128 + used, :used] = np.kron(mz, my)
    put = np.zeros((2, 4, 16, LANES), np.float32)
    for part in range(2):
        for z in range(4):
            f = z if part == 0 else z + 1
            for y in range(16):
                put[part, z, y, f * BOX_Y + 1 + y] = 1.0
    return rows_x, expand.T.astype(np.float32), along_y, lanes, put


def iotas():
    row = lax.broadcasted_iota(jnp.int32, (ROWS, LANES), 0)
    lane = lax.broadcasted_iota(jnp.int32, (ROWS, LANES), 1)
    f = jnp.zeros_like(lane)
    for k in range(1, BOX_Z + 1):
        f = f + (lane >= k * BOX_Y).astype(jnp.int32)
    return row & 7, f, lane - f * BOX_Y


def masks(where):
    (gx, nx), (gy, ny), (gz, nz) = where
    kx, f, e = iotas()
    low_x, high_x = jnp.where(gx == 0, 1, 0), jnp.where(gx == nx - 1, 4, 6)
    low_y, high_y = jnp.where(gy == 0, 1, 0), jnp.where(gy == ny - 1, 16, 18)
    high_z = jnp.where(gz == 0, 5, 4)
    inside = (kx >= low_x) & (kx <= high_x) & (e >= low_y) & (e <= high_y) & (f <= high_z)
    own_z = jnp.where(gz == 0, 0, 1)
    own = (kx >= 1) & (kx <= 4) & (e >= 1) & (e <= 16) & (f >= own_z) & (f <= own_z + 3)
    return inside.astype(jnp.float32), own.astype(jnp.float32)


def places():
    return tuple((lax.axis_index(a), lax.axis_size(a)) for a in ("gx", "gy", "gz"))


def split3(value):
    high = value.astype(jnp.bfloat16)
    rest = value - high.astype(jnp.float32)
    middle = rest.astype(jnp.bfloat16)
    low = (rest - middle.astype(jnp.float32)).astype(jnp.bfloat16)
    return jnp.concatenate([high, middle, low], axis=0)


def dot(a, b, dims=((1,), (0,)), precision=None):
    return lax.dot_general(
        a, b, (dims, ((), ())), precision=precision, preferred_element_type=jnp.float32
    )


def apply_local(vector, grad_ref, rows_ref, back_ref, along_ref, lanes_ref, field_ref, sums_ref):
    first = dot(rows_ref[...], vector, precision=HIGHEST)
    pieces = split3(first[:96])
    field = dot(jnp.concatenate([pieces, pieces], axis=1), along_ref[...])
    field_ref[...] = field[:96] + field[96:192] + field[192:]

    def column(cx, carry):
        rows = [pl.ds(pl.multiple_of(c * 32 + cx * 8, 8), 8) for c in range(3)]
        inside = pl.ds(pl.multiple_of(cx * 8, 8), 8)
        total = [[None] * 4 for _ in range(3)]
        for cz in range(CELLS_Z):
            layer = [
                [field_ref[rows[c], (cz + k) * LANES : (cz + k + 1) * LANES] for k in range(4)]
                for c in range(3)
            ]
            for t in range(8):
                weight = WEIGHTS[t]
                used = [k for k in range(4) if weight[k] != 0.0]
                slope = [grad_ref[c, cz * 8 + t, inside, :] for c in range(3)]
                shade = None
                for c in range(3):
                    value = None
                    for k in used:
                        term = weight[k] * layer[c][k]
                        value = term if value is None else value + term
                    term = slope[c] * value
                    shade = term if shade is None else shade + term
                for c in range(3):
                    value = slope[c] * shade
                    for k in used:
                        term = weight[k] * value
                        total[c][k] = term if total[c][k] is None else total[c][k] + term
            for c in range(3):
                sums_ref[rows[c], cz * LANES : (cz + 1) * LANES] = total[c][0]
                total[c] = total[c][1:] + [None]
        for c in range(3):
            for k in range(3):
                g = CELLS_Z + k
                sums_ref[rows[c], g * LANES : (g + 1) * LANES] = total[c][k]
        return carry

    lax.fori_loop(0, CELLS_X, column, 0)
    pieces = split3(sums_ref[...])
    back = dot(pieces, along_ref[...], ((1,), (1,)))
    back = back[:, :LANES] + back[:, LANES:]
    back = back[:96] + back[96:192] + back[192:]
    data = dot(back_ref[...], back, precision=HIGHEST)
    relief = dot(
        jnp.concatenate([first[96:120], first[120:144]], axis=1), lanes_ref[...], precision=HIGHEST
    )
    return data + relief


def roll(value, shift, axis):
    return pltpu.roll(value, shift, axis)


def start_kernel(right_ref, put_ref, out_ref):
    count = out_ref.shape[0]
    out_ref[0] = jnp.zeros((ROWS, LANES), jnp.float32)
    for c in range(3):
        value = None
        for z in range(CELLS_Z):
            term = dot(right_ref[c, z], put_ref[z], precision=HIGHEST)
            value = term if value is None else value + term
        out_ref[0, c * 8 + 1 : c * 8 + 5, :] = value
    whole = out_ref[0]
    for i in range(1, count):
        out_ref[i] = whole


def rows_rolled(value, shift):
    return jnp.concatenate(
        [roll(value[c * 8 : c * 8 + 8], shift, 0) for c in range(3)], axis=0
    )


def middle_kernel(in_ref, out_ref):
    (gx, nx), _, (gz, nz) = places()
    kx, f, e = iotas()
    has_low = (gx > 0).astype(jnp.int32)
    has_high = (gx < nx - 1).astype(jnp.int32)
    low = jnp.maximum(gx - 1, 0)
    high = jnp.minimum(gx + 1, nx - 1)
    take_low = (kx <= 2) & (has_low == 1)
    take_high = (kx >= 4) & (kx <= 6) & (has_high == 1)

    def along_x(part):
        value = in_ref[gx * nz + part]
        below = rows_rolled(in_ref[low * nz + part], 4)
        above = rows_rolled(in_ref[high * nz + part], 4)
        value = value + jnp.where(take_low, below, 0.0)
        return value + jnp.where(take_high, above, 0.0)

    mine = along_x(gz)
    other = along_x(1 - gz)
    other = roll(other, jnp.where(gz == 0, 3 * BOX_Y, LANES - 3 * BOX_Y), 1)
    first_f = jnp.where(gz == 0, 3, 0)
    value = mine + jnp.where((f >= first_f) & (f <= first_f + 2), other, 0.0)
    everything = in_ref[0]
    for i in range(1, in_ref.shape[0]):
        everything = everything + in_ref[i]
    value = jnp.where(kx == 7, everything, value)
    for i in range(out_ref.shape[0]):
        out_ref[i] = value


def along_y_sum(in_ref):
    _, (gy, ny), _ = places()
    kx, f, e = iotas()
    has_low = (gy > 0).astype(jnp.int32)
    has_high = (gy < ny - 1).astype(jnp.int32)
    below = roll(in_ref[jnp.maximum(gy - 1, 0)], LANES - 16, 1)
    above = roll(in_ref[jnp.minimum(gy + 1, ny - 1)], 16, 1)
    value = in_ref[gy]
    value = value + jnp.where((e <= 2) & (has_low == 1), below, 0.0)
    value = value + jnp.where((e >= 16) & (has_high == 1), above, 0.0)
    everything = in_ref[0]
    for i in range(1, in_ref.shape[0]):
        everything = everything + in_ref[i]
    return value, everything


def message(vector, image, own, out_ref):
    norm = jnp.sum(own * vector * vector, axis=0, keepdims=True)
    product = jnp.sum(vector * image, axis=0, keepdims=True)
    row = lax.broadcasted_iota(jnp.int32, (ROWS, LANES), 0)
    value = jnp.where(row == 7, norm, image)
    value = jnp.where(row == 15, product, value)
    for i in range(out_ref.shape[0]):
        out_ref[i] = value


def first_kernel(in_ref, grad_ref, rows_ref, back_ref, along_ref, lanes_ref, out_ref, residual_ref, field_ref, sums_ref):
    inside, own = masks(places())
    value, _ = along_y_sum(in_ref)
    residual = value * inside
    residual_ref[...] = residual
    image = apply_local(residual, grad_ref, rows_ref, back_ref, along_ref, lanes_ref, field_ref, sums_ref)
    message(residual, image * inside, own, out_ref)


def update(in_ref, old_ref, number):
    inside, own = masks(places())
    value, everything = along_y_sum(in_ref)
    residual = old_ref[ROWS : 2 * ROWS] if number else old_ref[...]
    image = value * inside + DAMPING * residual
    norm = jnp.sum(everything[7:8], axis=1, keepdims=True)
    product = jnp.sum(everything[15:16], axis=1, keepdims=True) + DAMPING * norm
    if number:
        ratio = norm / old_ref[4 * ROWS : 4 * ROWS + 1, 0:1]
        step = norm / (product - ratio * norm / old_ref[4 * ROWS + 1 : 4 * ROWS + 2, 0:1])
        direction = residual + ratio * old_ref[2 * ROWS : 3 * ROWS]
        image = image + ratio * old_ref[3 * ROWS : 4 * ROWS]
        solved = old_ref[0:ROWS] + step * direction
    else:
        step = norm / product
        direction = residual
        solved = step * direction
    residual = residual - step * image
    return own, inside, solved, residual, direction, image, norm, step


def step_kernel(number, in_ref, old_ref, grad_ref, rows_ref, back_ref, along_ref, lanes_ref, out_ref, new_ref, field_ref, sums_ref):
    own, inside, solved, residual, direction, image, norm, step = update(in_ref, old_ref, number)
    new_ref[0:ROWS] = solved
    new_ref[ROWS : 2 * ROWS] = residual
    new_ref[2 * ROWS : 3 * ROWS] = direction
    new_ref[3 * ROWS : 4 * ROWS] = image
    row = lax.broadcasted_iota(jnp.int32, (8, LANES), 0)
    new_ref[4 * ROWS : 4 * ROWS + 8] = jnp.where(row == 0, norm, step)
    image = apply_local(residual, grad_ref, rows_ref, back_ref, along_ref, lanes_ref, field_ref, sums_ref)
    message(residual, image * inside, own, out_ref)


def last_kernel(in_ref, old_ref, put_ref, solution_ref, residual_ref):
    _, _, solved, residual, _, _, _, _ = update(in_ref, old_ref, ITERS - 1)
    both = jnp.concatenate([solved, residual], axis=0)
    for z in range(CELLS_Z):
        value = dot(both, put_ref[z], ((1,), (1,)), precision=HIGHEST)
        for c in range(3):
            solution_ref[c, z] = value[c * 8 + 1 : c * 8 + 5]
            residual_ref[c, z] = value[ROWS + c * 8 + 1 : ROWS + c * 8 + 5]


def call(body, outs, *args, scratch=False):
    shapes = [jax.ShapeDtypeStruct(s, jnp.float32) for s in outs]
    scratch_shapes = [pltpu.VMEM((96, 7 * LANES), jnp.float32)] * 2 if scratch else []
    vmem = pl.BlockSpec(memory_space=pltpu.VMEM)
    return pl.pallas_call(
        body,
        out_shape=shapes,
        in_specs=[vmem] * len(args),
        out_specs=[vmem] * len(outs),
        scratch_shapes=scratch_shapes,
        compiler_params=pltpu.CompilerParams(vmem_limit_bytes=24 * 1024 * 1024),
    )(*args)


def kind_of(index, count):
    return jnp.where(index == 0, 0, jnp.where(index == count - 1, 2, 1))


def shards(gradient, right_side):
    (gx, nx), (gy, ny), (gz, nz) = places()
    rows_x, back_x, along_y, lanes, put = tables()
    pick = lambda table, i: lax.dynamic_index_in_dim(jnp.asarray(table), i, 0, keepdims=False)
    rows_x = pick(rows_x, kind_of(gx, nx))
    along_y = pick(along_y, gz)
    lanes = pick(lanes.reshape(6, 256, LANES), gz * 3 + kind_of(gy, ny))
    put = pick(put, gz)
    operands = (gradient, rows_x, jnp.asarray(back_x), along_y, lanes)
    group, line, box = (nx * nz, ROWS, LANES), (ny, ROWS, LANES), (ROWS, LANES)
    state = (4 * ROWS + 8, LANES)

    def exchange(sent):
        near = lax.all_to_all(sent, ("gx", "gz"), 0, 0)
        (sent,) = call(middle_kernel, [line], near)
        return lax.all_to_all(sent, "gy", 0, 0)

    (sent,) = call(start_kernel, [group], right_side, put)
    sent, old = call(first_kernel, [group, box], exchange(sent), *operands, scratch=True)
    for number in range(ITERS - 1):
        body = functools.partial(step_kernel, number)
        sent, old = call(body, [group, state], exchange(sent), old, *operands, scratch=True)
    shape = right_side.shape
    return tuple(call(last_kernel, [shape, shape], exchange(sent), old, put))


def solution(mesh):
    placed = P(None, "gz", "gx", "gy")
    return jax.shard_map(
        shards,
        mesh=mesh,
        in_specs=(placed, placed),
        out_specs=(placed, placed),
        check_vma=False,
    )
```

```python
import functools

import jax
import jax.numpy as jnp
import ml_dtypes
import numpy as np
from jax import lax
from jax.experimental import pallas as pl
from jax.experimental.pallas import tpu as pltpu
from jax.sharding import PartitionSpec as P

ITERS = 6
SMOOTHING = 0.5
DAMPING = 0.05
HIGHEST = lax.Precision.HIGHEST

CELLS_Z, CELLS_X, CELLS_Y = 4, 4, 16
BOX_X, BOX_Y, BOX_Z = 7, 19, 6
LANES = 128
ROWS = 24
DENOMINATOR = 3072.0
SCALE = 512.0
DAMP = DAMPING / SCALE
SHIFTS = (0.0, 0.95, 0.5, 0.2, 0.75)
WORST_PIVOT = 0.02


def numerators(t):
    return (
        (8 - t) ** 3,
        3 * t**3 - 48 * t**2 + 2048,
        -3 * t**3 + 24 * t**2 + 192 * t + 512,
        t**3,
    )


WEIGHTS = [[n / DENOMINATOR for n in numerators(t)] for t in range(8)]


def basis(cells):
    table = np.zeros((8 * cells + 1, cells + 3 + 1))
    for voxel in range(8 * cells + 1):
        for k, n in enumerate(numerators(voxel % 8)):
            table[voxel, voxel // 8 + k] = n
    return table[:, :-1]


def mass_and_edges(cells, first, last):
    table = basis(cells) / DENOMINATOR
    own = table[:-1]
    steps = table[1:] - table[:-1]
    if last:
        steps[-1] = -table[-2]
    edges = steps.T @ steps
    if first:
        edges = edges + np.outer(table[0], table[0])
    return own.T @ own, edges


def place_z(matrix, part):
    return matrix[1:7, 1:7] if part == 0 else matrix[0:6, 0:6]


@functools.lru_cache(None)
def tables():
    bx = basis(CELLS_X)[:-1]
    expand = np.zeros((96, ROWS))
    for c in range(3):
        expand[c * 32 : c * 32 + 32, c * 8 : c * 8 + BOX_X] = bx / DENOMINATOR / DENOMINATOR
    rows_x = np.zeros((3, 144, ROWS), np.float32)
    for kind in range(3):
        mass, edges = mass_and_edges(CELLS_X, kind == 0, kind == 2)
        rows_x[kind, :96] = expand
        for c in range(3):
            at = slice(c * 8, c * 8 + BOX_X)
            rows_x[kind, 96 + c * 8 : 96 + c * 8 + BOX_X, at] = SMOOTHING / SCALE * mass
            rows_x[kind, 120 + c * 8 : 120 + c * 8 + BOX_X, at] = SMOOTHING / SCALE * edges
    by = basis(CELLS_Y)[:-1]
    along_y = np.zeros((2, 2, LANES, 7 * LANES))
    for part in range(2):
        for f in range(BOX_Z):
            g = f + 1 if part == 0 else f
            low = by.T.astype(ml_dtypes.bfloat16).astype(np.float64)
            at = slice(f * BOX_Y, (f + 1) * BOX_Y)
            along_y[part, 0, at, g * LANES : (g + 1) * LANES] = low
            along_y[part, 1, at, g * LANES : (g + 1) * LANES] = by.T - low
    along_y = along_y.reshape(2, 256, 7 * LANES).astype(ml_dtypes.bfloat16)
    lanes = np.zeros((2, 3, 256, LANES), np.float32)
    for part in range(2):
        mz, kz = mass_and_edges(CELLS_Z, part == 0, part == 1)
        mz, kz = place_z(mz, part), place_z(kz, part)
        for kind in range(3):
            my, ky = mass_and_edges(CELLS_Y, kind == 0, kind == 2)
            used = BOX_Z * BOX_Y
            lanes[part, kind, :used, :used] = np.kron(kz, my) + np.kron(mz, ky)
            lanes[part, kind, 128 : 128 + used, :used] = np.kron(mz, my)
    put = np.zeros((2, 4, 16, LANES), np.float32)
    for part in range(2):
        for z in range(4):
            f = z if part == 0 else z + 1
            for y in range(16):
                put[part, z, y, f * BOX_Y + 1 + y] = 1.0
    return (
        rows_x,
        (expand.T / SCALE).astype(np.float32),
        along_y,
        lanes.reshape(6, 256, LANES),
        put.astype(ml_dtypes.bfloat16),
    )


def iotas():
    row = lax.broadcasted_iota(jnp.int32, (ROWS, LANES), 0)
    lane = lax.broadcasted_iota(jnp.int32, (ROWS, LANES), 1)
    f = jnp.zeros_like(lane)
    for k in range(1, BOX_Z + 1):
        f = f + (lane >= k * BOX_Y).astype(jnp.int32)
    return row & 7, f, lane - f * BOX_Y


def masks(where):
    (gx, nx), (gy, ny), (gz, nz) = where
    kx, f, e = iotas()
    low_x, high_x = jnp.where(gx == 0, 1, 0), jnp.where(gx == nx - 1, 4, 6)
    low_y, high_y = jnp.where(gy == 0, 1, 0), jnp.where(gy == ny - 1, 16, 18)
    high_z = jnp.where(gz == 0, 5, 4)
    inside = (kx >= low_x) & (kx <= high_x) & (e >= low_y) & (e <= high_y) & (f <= high_z)
    own_z = jnp.where(gz == 0, 0, 1)
    own = (kx >= 1) & (kx <= 4) & (e >= 1) & (e <= 16) & (f >= own_z) & (f <= own_z + 3)
    return inside.astype(jnp.float32), own.astype(jnp.float32)


def places():
    return tuple((lax.axis_index(a), lax.axis_size(a)) for a in ("gx", "gy", "gz"))


def split3(value):
    high = value.astype(jnp.bfloat16)
    rest = value - high.astype(jnp.float32)
    middle = rest.astype(jnp.bfloat16)
    low = (rest - middle.astype(jnp.float32)).astype(jnp.bfloat16)
    return jnp.concatenate([high, middle, low], axis=0)


def dot(a, b, dims=((1,), (0,)), precision=None):
    return lax.dot_general(
        a, b, (dims, ((), ())), precision=precision, preferred_element_type=jnp.float32
    )


def kind_of(index, count):
    return jnp.where(index == 0, 0, jnp.where(index == count - 1, 2, 1))


def apply_local(vector, grad_ref, rows_ref, back_ref, along_ref, lanes_ref, field_ref, sums_ref):
    (gx, nx), (gy, ny), (gz, _) = places()
    first = dot(rows_ref[kind_of(gx, nx)], vector, precision=HIGHEST)
    pieces = split3(first[:96])
    field = dot(jnp.concatenate([pieces, pieces], axis=1), along_ref[gz])
    field_ref[...] = field[:96] + field[96:192] + field[192:]

    def column(cx, carry):
        rows = [pl.ds(pl.multiple_of(c * 32 + cx * 8, 8), 8) for c in range(3)]
        inside = pl.ds(pl.multiple_of(cx * 8, 8), 8)
        total = [[None] * 4 for _ in range(3)]
        for cz in range(CELLS_Z):
            layer = [
                [field_ref[rows[c], (cz + k) * LANES : (cz + k + 1) * LANES] for k in range(4)]
                for c in range(3)
            ]
            for t in range(8):
                weight = WEIGHTS[t]
                used = [k for k in range(4) if weight[k] != 0.0]
                slope = [grad_ref[c, cz * 8 + t, inside, :] for c in range(3)]
                shade = None
                for c in range(3):
                    value = None
                    for k in used:
                        term = weight[k] * layer[c][k]
                        value = term if value is None else value + term
                    term = slope[c] * value
                    shade = term if shade is None else shade + term
                for c in range(3):
                    value = slope[c] * shade
                    for k in used:
                        term = weight[k] * value
                        total[c][k] = term if total[c][k] is None else total[c][k] + term
            for c in range(3):
                sums_ref[rows[c], cz * LANES : (cz + 1) * LANES] = total[c][0]
                total[c] = total[c][1:] + [None]
        for c in range(3):
            for k in range(3):
                g = CELLS_Z + k
                sums_ref[rows[c], g * LANES : (g + 1) * LANES] = total[c][k]
        return carry

    lax.fori_loop(0, CELLS_X, column, 0)
    pieces = split3(sums_ref[...])
    back = dot(pieces, along_ref[gz], ((1,), (1,)))
    back = back[:, :LANES] + back[:, LANES:]
    back = back[:96] + back[96:192] + back[192:]
    data = dot(back_ref[...], back, precision=HIGHEST)
    relief = dot(
        jnp.concatenate([first[96:120], first[120:144]], axis=1),
        lanes_ref[gz * 3 + kind_of(gy, ny)],
        precision=HIGHEST,
    )
    return data + relief


def roll(value, shift, axis):
    return pltpu.roll(value, shift, axis)


def start_kernel(right_ref, put_ref, out_ref):
    gz = lax.axis_index("gz")
    out_ref[...] = jnp.zeros((ROWS, LANES), jnp.float32)
    for c in range(3):
        value = None
        for z in range(CELLS_Z):
            rest = right_ref[c, z]
            for _ in range(3):
                piece = rest.astype(jnp.bfloat16)
                rest = rest - piece.astype(jnp.float32)
                term = dot(piece, put_ref[gz, z])
                value = term if value is None else value + term
        out_ref[c * 8 + 1 : c * 8 + 5, :] = value


def size_kernel(grad_ref, out_ref):
    def plane(z, totals):
        totals = list(totals)
        for x in range(4):
            slope = [grad_ref[c, z, x * 8 : x * 8 + 8, :] for c in range(3)]
            k = 0
            for a in range(3):
                for b in range(a, 3):
                    totals[k] = totals[k] + slope[a] * slope[b]
                    k += 1
        return tuple(totals)

    zero = jnp.zeros((8, LANES), jnp.float32)
    totals = lax.fori_loop(0, 32, plane, (zero,) * 6)
    count = 32.0 * 32.0 * 128.0
    xx, xy, xz, yy, yz, zz = [
        jnp.sum(jnp.sum(t, axis=0, keepdims=True), axis=1, keepdims=True) / count for t in totals
    ]
    aa = xx * xx + xy * xy + xz * xz
    bb = xy * xy + yy * yy + yz * yz
    cc = xz * xz + yz * yz + zz * zz
    ab = xx * xy + xy * yy + xz * yz
    ac = xx * xz + xy * yz + xz * zz
    bc = xy * xz + yy * yz + yz * zz
    norm = aa * aa + bb * bb + cc * cc + 2.0 * (ab * ab + ac * ac + bc * bc)
    size = 0.9 * jnp.sqrt(jnp.sqrt(norm)) + 0.05
    row = lax.broadcasted_iota(jnp.int32, (8, LANES), 0)
    out_ref[...] = jnp.where(row == 7, jnp.broadcast_to(size, (8, LANES)), 0.0)


def with_size(value, *others):
    row = lax.broadcasted_iota(jnp.int32, (ROWS, LANES), 0)
    return jnp.where(row == 7, functools.reduce(jnp.maximum, others), value)


def pair_sides(index, pair, other):
    even = lax.rem(index, 2) == 0
    return jnp.where(even, other, pair), jnp.where(even, pair, other)


def z_kernel(mine_ref, swap_ref, out_ref):
    gz = lax.axis_index("gz")
    _, f, _ = iotas()
    mine, swap = mine_ref[...], swap_ref[...]
    other = roll(swap, jnp.where(gz == 0, 3 * BOX_Y, LANES - 3 * BOX_Y), 1)
    first_f = jnp.where(gz == 0, 3, 0)
    value = mine + jnp.where((f >= first_f) & (f <= first_f + 2), other, 0.0)
    out_ref[...] = with_size(value, mine, swap)


def x_kernel(mine_ref, pair_ref, other_ref, *rest):
    out_ref = rest[-1]
    gx, nx = lax.axis_index("gx"), lax.axis_size("gx")
    kx, _, _ = iotas()
    mine, pair, other = mine_ref[...], pair_ref[...], other_ref[...]
    low, high = pair_sides(gx, pair, other)
    first_x, last_x = jnp.where(gx > 0, 2, -1), jnp.where(gx < nx - 1, 4, 8)
    value = mine + jnp.where(kx <= first_x, rows_rolled(low, 4), 0.0)
    value = value + jnp.where((kx >= last_x) & (kx <= 6), rows_rolled(high, 4), 0.0)
    out_ref[...] = with_size(value, mine, pair, other)


def x_first_kernel(mine_ref, size_ref, out_ref):
    out_ref[...] = mine_ref[...]
    row = lax.broadcasted_iota(jnp.int32, (8, LANES), 0)
    out_ref[0:8] = jnp.where(row == 7, size_ref[...], mine_ref[0:8])


def y_sum(mine_ref, pair_ref, other_ref):
    gy, ny = lax.axis_index("gy"), lax.axis_size("gy")
    _, _, e = iotas()
    mine, pair, other = mine_ref[...], pair_ref[...], other_ref[...]
    low, high = pair_sides(gy, pair, other)
    first_y, last_y = jnp.where(gy > 0, 2, -1), jnp.where(gy < ny - 1, 16, LANES)
    value = mine + jnp.where(e <= first_y, roll(low, LANES - 16, 1), 0.0)
    value = value + jnp.where(e >= last_y, roll(high, 16, 1), 0.0)
    return value, jnp.maximum(jnp.maximum(mine, pair), other)[7:8]


def rows_rolled(value, shift):
    return jnp.concatenate(
        [roll(value[c * 8 : c * 8 + 8], shift, 0) for c in range(3)], axis=0
    )


def middle_kernel(in_ref, out_ref):
    (gx, nx), _, (gz, nz) = places()
    kx, f, e = iotas()
    has_low = (gx > 0).astype(jnp.int32)
    has_high = (gx < nx - 1).astype(jnp.int32)
    low = jnp.maximum(gx - 1, 0)
    high = jnp.minimum(gx + 1, nx - 1)
    take_low = (kx <= 2) & (has_low == 1)
    take_high = (kx >= 4) & (kx <= 6) & (has_high == 1)

    def along_x(part):
        value = in_ref[gx * nz + part]
        below = rows_rolled(in_ref[low * nz + part], 4)
        above = rows_rolled(in_ref[high * nz + part], 4)
        value = value + jnp.where(take_low, below, 0.0)
        return value + jnp.where(take_high, above, 0.0)

    mine = along_x(gz)
    other = along_x(1 - gz)
    other = roll(other, jnp.where(gz == 0, 3 * BOX_Y, LANES - 3 * BOX_Y), 1)
    first_f = jnp.where(gz == 0, 3, 0)
    value = mine + jnp.where((f >= first_f) & (f <= first_f + 2), other, 0.0)
    everything = in_ref[0]
    for i in range(1, in_ref.shape[0]):
        everything = everything + in_ref[i]
    value = jnp.where(kx == 7, everything, value)
    for i in range(out_ref.shape[0]):
        out_ref[i] = value


def along_y_sum(in_ref):
    _, (gy, ny), _ = places()
    kx, f, e = iotas()
    has_low = (gy > 0).astype(jnp.int32)
    has_high = (gy < ny - 1).astype(jnp.int32)
    below = roll(in_ref[jnp.maximum(gy - 1, 0)], LANES - 16, 1)
    above = roll(in_ref[jnp.minimum(gy + 1, ny - 1)], 16, 1)
    value = in_ref[gy]
    value = value + jnp.where((e <= 2) & (has_low == 1), below, 0.0)
    value = value + jnp.where((e >= 16) & (has_high == 1), above, 0.0)
    everything = in_ref[0]
    for i in range(1, in_ref.shape[0]):
        everything = everything + in_ref[i]
    return value, everything


def message(vector, image, own, out_ref):
    norm = jnp.sum(own * vector * vector, axis=0, keepdims=True)
    product = jnp.sum(vector * image, axis=0, keepdims=True)
    row = lax.broadcasted_iota(jnp.int32, (ROWS, LANES), 0)
    value = jnp.where(row == 7, norm, image)
    value = jnp.where(row == 15, product, value)
    for i in range(out_ref.shape[0]):
        out_ref[i] = value


def basis_kernel(number, mine_ref, pair_ref, other_ref, *refs):
    past = refs[:number]
    operands = refs[number : number + 5]
    out_ref, *new_refs, field_ref, sums_ref = refs[number + 5 :]
    inside, own = masks(places())
    value, size = y_sum(mine_ref, pair_ref, other_ref)
    value = value * inside
    if number:
        value = value + DAMP * past[-1][...]
    if number == 3:
        inverse = 1.0 / size
        one, two = past[1][...], past[2][...]
        second = inverse * two - SHIFTS[1] * one
        value = inverse * (inverse * value - SHIFTS[1] * two) - SHIFTS[2] * second
        new_refs[1][...] = second
    elif number > 3:
        value = value / size - SHIFTS[number - 1] * past[-1][...]
    new_refs[0][...] = value
    image = apply_local(value, *operands, field_ref, sums_ref) * inside
    if number < 5:
        out_ref[...] = with_size(image, jnp.broadcast_to(size, (ROWS, LANES)))
        return
    new_refs[1][...] = jnp.broadcast_to(size, (8, LANES))
    vectors = [ref[...] for ref in past] + [value]
    products = []
    for i in range(6):
        mine = own * vectors[i]
        for j in range(i, 6):
            products.append(mine * vectors[j])
    products.append(value * image + DAMP * own * value * value)
    sums = [jnp.sum(p, axis=0, keepdims=True) for p in products]
    sums = jnp.concatenate(sums + [jnp.zeros((2, LANES), jnp.float32)], axis=0)
    sums = jnp.sum(sums, axis=1, keepdims=True)
    row = lax.broadcasted_iota(jnp.int32, (ROWS, LANES), 0)
    lane = lax.broadcasted_iota(jnp.int32, (ROWS, LANES), 1)
    line = jnp.sum(jnp.where(row == lane, sums, 0.0), axis=0, keepdims=True)
    image = jnp.where(row == 7, line, image)
    for i in range(out_ref.shape[0]):
        out_ref[i] = image


def add(a, b):
    return b if a is None else a if b is None else a + b


def times(a, b):
    return None if a is None or b is None else a * b


def form(left, table, right):
    total = None
    for i, a in enumerate(left):
        inner = None
        for j, b in enumerate(right):
            inner = add(inner, times(table[i][j], b))
        total = add(total, times(a, inner))
    return total


def fast_kernel(in_ref, *refs):
    vectors = [ref[...] for ref in refs[:6]]
    size_ref, put_ref, solution_ref, residual_ref, good_ref = refs[6:]
    inside, _ = masks(places())
    value, everything = along_y_sum(in_ref)
    size = size_ref[0:1, 0:1]
    inverse = 1.0 / size
    image = (value * inside + DAMP * vectors[5]) * inverse
    line = everything[7:8]
    lane = lax.broadcasted_iota(jnp.int32, (1, LANES), 1)
    scalars = [jnp.sum(jnp.where(lane == k, line, 0.0), axis=1, keepdims=True) for k in range(22)]
    gram = [[None] * 6 for _ in range(6)]
    k = 0
    for i in range(6):
        for j in range(i, 6):
            gram[i][j] = gram[j][i] = scalars[k]
            k += 1
    factor = [inverse] + [jnp.ones_like(inverse)] * 4
    energy = [[None] * 6 for _ in range(6)]
    for i in range(5):
        for j in range(i, 6):
            energy[i][j] = energy[j][i] = factor[i] * (gram[i + 1][j] + SHIFTS[i] * gram[i][j])
    energy[5][5] = scalars[21] * inverse
    rest = [row[:] for row in gram]
    good = jnp.ones_like(inverse)
    for k in range(6):
        good = jnp.where(rest[k][k] / gram[k][k] > WORST_PIVOT, good, 0.0)
        for i in range(k + 1, 6):
            ratio = rest[i][k] / rest[k][k]
            for j in range(i, 6):
                rest[i][j] = rest[i][j] - ratio * rest[k][j]
                rest[j][i] = rest[i][j]
    good_ref[...] = jnp.broadcast_to(good, (8, LANES))
    solved = [None] * 7
    residual = [jnp.ones_like(inverse)] + [None] * 6
    direction = residual[:]
    norm = gram[0][0]
    for number in range(ITERS):
        known = number + 1
        moved = [None] * 7
        for j in range(known):
            if j == 5:
                moved[6] = add(moved[6], direction[5])
            else:
                part = factor[j] * direction[j]
                moved[j + 1] = add(moved[j + 1], part)
                moved[j] = add(moved[j], SHIFTS[j] * part)
        step = norm / form(direction[:known], energy, direction[:known])
        solved = [add(a, times(step, b)) for a, b in zip(solved, direction)]
        residual = [add(a, times(-step, b)) for a, b in zip(residual, moved)]
        if number < ITERS - 1:
            known += 1
            later = form(residual[:known], gram, residual[:known])
            ratio = later / norm
            direction = [add(a, times(ratio, b)) for a, b in zip(residual, direction)]
            norm = later
    vectors = vectors + [image]
    first, second = None, None
    for j in range(7):
        if solved[j] is not None:
            first = add(first, solved[j] * vectors[j])
        second = add(second, residual[j] * vectors[j])
    write_out(first * (inverse / SCALE), second, put_ref, solution_ref, residual_ref)


def write_out(solved, residual, put_ref, solution_ref, residual_ref):
    gz = lax.axis_index("gz")
    both = jnp.concatenate([solved, residual], axis=0)
    pieces = split3(both)
    for z in range(CELLS_Z):
        value = dot(pieces, put_ref[gz, z], ((1,), (1,)))
        value = value[:48] + value[48:96] + value[96:]
        for c in range(3):
            solution_ref[c, z] = value[c * 8 + 1 : c * 8 + 5]
            residual_ref[c, z] = value[ROWS + c * 8 + 1 : ROWS + c * 8 + 5]


def slow_kernel(vector_ref, grad_ref, rows_ref, back_ref, along_ref, lanes_ref, out_ref, field_ref, sums_ref):
    inside, own = masks(places())
    vector = vector_ref[...]
    image = apply_local(vector, grad_ref, rows_ref, back_ref, along_ref, lanes_ref, field_ref, sums_ref)
    message(vector, image * inside, own, out_ref)


def update(in_ref, old_ref, number):
    inside, own = masks(places())
    value, everything = along_y_sum(in_ref)
    residual = old_ref[ROWS : 2 * ROWS] if number else old_ref[...]
    image = value * inside + DAMP * residual
    norm = jnp.sum(everything[7:8], axis=1, keepdims=True)
    product = jnp.sum(everything[15:16], axis=1, keepdims=True) + DAMP * norm
    if number:
        ratio = norm / old_ref[4 * ROWS : 4 * ROWS + 1, 0:1]
        step = norm / (product - ratio * norm / old_ref[4 * ROWS + 1 : 4 * ROWS + 2, 0:1])
        direction = residual + ratio * old_ref[2 * ROWS : 3 * ROWS]
        image = image + ratio * old_ref[3 * ROWS : 4 * ROWS]
        solved = old_ref[0:ROWS] + step * direction
    else:
        step = norm / product
        direction = residual
        solved = step * direction
    residual = residual - step * image
    return own, inside, solved, residual, direction, image, norm, step


def step_kernel(number, in_ref, old_ref, grad_ref, rows_ref, back_ref, along_ref, lanes_ref, out_ref, new_ref, field_ref, sums_ref):
    own, inside, solved, residual, direction, image, norm, step = update(in_ref, old_ref, number)
    new_ref[0:ROWS] = solved
    new_ref[ROWS : 2 * ROWS] = residual
    new_ref[2 * ROWS : 3 * ROWS] = direction
    new_ref[3 * ROWS : 4 * ROWS] = image
    row = lax.broadcasted_iota(jnp.int32, (8, LANES), 0)
    new_ref[4 * ROWS : 4 * ROWS + 8] = jnp.where(row == 0, norm, step)
    image = apply_local(residual, grad_ref, rows_ref, back_ref, along_ref, lanes_ref, field_ref, sums_ref)
    message(residual, image * inside, own, out_ref)


def last_kernel(in_ref, old_ref, put_ref, solution_ref, residual_ref):
    _, _, solved, residual, _, _, _, _ = update(in_ref, old_ref, ITERS - 1)
    write_out(solved / SCALE, residual, put_ref, solution_ref, residual_ref)


def call(body, outs, *args, scratch=False):
    shapes = [jax.ShapeDtypeStruct(s, jnp.float32) for s in outs]
    scratch_shapes = [pltpu.VMEM((96, 7 * LANES), jnp.float32)] * 2 if scratch else []
    vmem = pl.BlockSpec(memory_space=pltpu.VMEM)
    return pl.pallas_call(
        body,
        out_shape=shapes,
        in_specs=[vmem] * len(args),
        out_specs=[vmem] * len(outs),
        scratch_shapes=scratch_shapes,
        compiler_params=pltpu.CompilerParams(vmem_limit_bytes=24 * 1024 * 1024),
    )(*args)


def swaps(axis):
    count = lax.axis_size(axis)
    pair = [(i, i ^ 1) for i in range(count)]
    other = [(i, (i + 1 if i % 2 else i - 1) % count) for i in range(count)]
    return pair, other


def shards(gradient, right_side):
    (_, nx), (_, ny), (_, nz) = places()
    rows_x, back_x, along_y, lanes, put = [jnp.asarray(t) for t in tables()]
    operands = (gradient, rows_x, back_x, along_y, lanes)
    group, line, box = (nx * nz, ROWS, LANES), (ny, ROWS, LANES), (ROWS, LANES)
    tile, state, shape = (8, LANES), (4 * ROWS + 8, LANES), right_side.shape

    def exchange_all(sent):
        near = lax.all_to_all(sent, ("gx", "gz"), 0, 0)
        (sent,) = call(middle_kernel, [line], near)
        return lax.all_to_all(sent, "gy", 0, 0)

    def exchange_near(sent, size=None):
        swapped = lax.ppermute(sent, "gz", swaps("gz")[0])
        (sent,) = call(z_kernel, [box], sent, swapped)
        if size is not None:
            (sent,) = call(x_first_kernel, [box], sent, size)
        pair, other = [lax.ppermute(sent, "gx", s) for s in swaps("gx")]
        (sent,) = call(x_kernel, [box], sent, pair, other)
        pair, other = [lax.ppermute(sent, "gy", s) for s in swaps("gy")]
        return sent, pair, other

    def slow(first):
        (sent,) = call(slow_kernel, [group], first, *operands, scratch=True)
        old = first
        for number in range(ITERS - 1):
            body = functools.partial(step_kernel, number)
            sent, old = call(body, [group, state], exchange_all(sent), old, *operands, scratch=True)
        return tuple(call(last_kernel, [shape, shape], exchange_all(sent), old, put))

    (sent,) = call(start_kernel, [box], right_side, put)
    (size,) = call(size_kernel, [tile], gradient)
    vectors = []
    for number in range(6):
        near = exchange_near(sent, size if number == 0 else None)
        outs = [group if number == 5 else box, box] + [[], [], [], [box], [], [tile]][number]
        body = functools.partial(basis_kernel, number)
        sent, vector, *extra = call(body, outs, *near, *vectors, *operands, scratch=True)
        if number == 3:
            vectors[2] = extra[0]
        vectors.append(vector)
    arrived = exchange_all(sent)
    *fast, good = call(fast_kernel, [shape, shape, tile], arrived, *vectors, extra[0], put)
    return lax.cond(good[0, 0] > 0.5, lambda first: tuple(fast), slow, vectors[0])


def solution(mesh):
    placed = P(None, "gz", "gx", "gy")
    return jax.shard_map(
        shards,
        mesh=mesh,
        in_specs=(placed, placed),
        out_specs=(placed, placed),
        check_vma=False,
    )
```

```python
import functools

import jax
import jax.numpy as jnp
import ml_dtypes
import numpy as np
from jax import lax
from jax.experimental import pallas as pl
from jax.experimental.pallas import tpu as pltpu
from jax.sharding import PartitionSpec as P

ITERS = 6
SMOOTHING = 0.5
DAMPING = 0.05
HIGHEST = lax.Precision.HIGHEST

CELLS_Z, CELLS_X, CELLS_Y = 4, 4, 16
BOX_X, BOX_Y, BOX_Z = 7, 19, 6
LANES = 128
ROWS = 24
DENOMINATOR = 3072.0
SCALE = 512.0
DAMP = DAMPING / SCALE
SHIFTS = (0.0, 0.171, 0.452, 0.776, 0.114)
WORST_PIVOT = 0.05


def numerators(t):
    return (
        (8 - t) ** 3,
        3 * t**3 - 48 * t**2 + 2048,
        -3 * t**3 + 24 * t**2 + 192 * t + 512,
        t**3,
    )


WEIGHTS = [[n / DENOMINATOR for n in numerators(t)] for t in range(8)]


def basis(cells):
    table = np.zeros((8 * cells + 1, cells + 3 + 1))
    for voxel in range(8 * cells + 1):
        for k, n in enumerate(numerators(voxel % 8)):
            table[voxel, voxel // 8 + k] = n
    return table[:, :-1]


def mass_and_edges(cells, first, last):
    table = basis(cells) / DENOMINATOR
    own = table[:-1]
    steps = table[1:] - table[:-1]
    if last:
        steps[-1] = -table[-2]
    edges = steps.T @ steps
    if first:
        edges = edges + np.outer(table[0], table[0])
    return own.T @ own, edges


def place_z(matrix, part):
    return matrix[1:7, 1:7] if part == 0 else matrix[0:6, 0:6]


@functools.lru_cache(None)
def tables():
    bx = basis(CELLS_X)[:-1]
    expand = np.zeros((96, ROWS))
    for c in range(3):
        expand[c * 32 : c * 32 + 32, c * 8 : c * 8 + BOX_X] = bx / DENOMINATOR / DENOMINATOR
    rows_x = np.zeros((3, 144, ROWS), np.float32)
    for kind in range(3):
        mass, edges = mass_and_edges(CELLS_X, kind == 0, kind == 2)
        rows_x[kind, :96] = expand
        for c in range(3):
            at = slice(c * 8, c * 8 + BOX_X)
            rows_x[kind, 96 + c * 8 : 96 + c * 8 + BOX_X, at] = SMOOTHING / SCALE * mass
            rows_x[kind, 120 + c * 8 : 120 + c * 8 + BOX_X, at] = SMOOTHING / SCALE * edges
    by = basis(CELLS_Y)[:-1]
    along_y = np.zeros((2, 2, LANES, 7 * LANES))
    for part in range(2):
        for f in range(BOX_Z):
            g = f + 1 if part == 0 else f
            low = by.T.astype(ml_dtypes.bfloat16).astype(np.float64)
            at = slice(f * BOX_Y, (f + 1) * BOX_Y)
            along_y[part, 0, at, g * LANES : (g + 1) * LANES] = low
            along_y[part, 1, at, g * LANES : (g + 1) * LANES] = by.T - low
    along_y = along_y.reshape(2, 256, 7 * LANES).astype(ml_dtypes.bfloat16)
    lanes = np.zeros((2, 3, 256, LANES), np.float32)
    for part in range(2):
        mz, kz = mass_and_edges(CELLS_Z, part == 0, part == 1)
        mz, kz = place_z(mz, part), place_z(kz, part)
        for kind in range(3):
            my, ky = mass_and_edges(CELLS_Y, kind == 0, kind == 2)
            used = BOX_Z * BOX_Y
            lanes[part, kind, :used, :used] = np.kron(kz, my) + np.kron(mz, ky)
            lanes[part, kind, 128 : 128 + used, :used] = np.kron(mz, my)
    return (
        rows_x,
        (expand.T / SCALE).astype(np.float32),
        along_y,
        lanes.reshape(6, 256, LANES),
    )


def iotas():
    row = lax.broadcasted_iota(jnp.int32, (ROWS, LANES), 0)
    lane = lax.broadcasted_iota(jnp.int32, (ROWS, LANES), 1)
    f = jnp.zeros_like(lane)
    for k in range(1, BOX_Z + 1):
        f = f + (lane >= k * BOX_Y).astype(jnp.int32)
    return row & 7, f, lane - f * BOX_Y


def masks(where):
    (gx, nx), (gy, ny), (gz, nz) = where
    kx, f, e = iotas()
    low_x, high_x = jnp.where(gx == 0, 1, 0), jnp.where(gx == nx - 1, 4, 6)
    low_y, high_y = jnp.where(gy == 0, 1, 0), jnp.where(gy == ny - 1, 16, 18)
    high_z = jnp.where(gz == 0, 5, 4)
    inside = (kx >= low_x) & (kx <= high_x) & (e >= low_y) & (e <= high_y) & (f <= high_z)
    own_z = jnp.where(gz == 0, 0, 1)
    own = (kx >= 1) & (kx <= 4) & (e >= 1) & (e <= 16) & (f >= own_z) & (f <= own_z + 3)
    return inside.astype(jnp.float32), own.astype(jnp.float32)


def places():
    return tuple((lax.axis_index(a), lax.axis_size(a)) for a in ("gx", "gy", "gz"))


def split3(value):
    high = value.astype(jnp.bfloat16)
    rest = value - high.astype(jnp.float32)
    middle = rest.astype(jnp.bfloat16)
    low = (rest - middle.astype(jnp.float32)).astype(jnp.bfloat16)
    return jnp.concatenate([high, middle, low], axis=0)


def dot(a, b, dims=((1,), (0,)), precision=None):
    return lax.dot_general(
        a, b, (dims, ((), ())), precision=precision, preferred_element_type=jnp.float32
    )


def kind_of(index, count):
    return jnp.where(index == 0, 0, jnp.where(index == count - 1, 2, 1))


def apply_local(vector, grad_ref, rows_ref, back_ref, along_ref, lanes_ref, field_ref, sums_ref):
    (gx, nx), (gy, ny), (gz, _) = places()
    first = dot(rows_ref[kind_of(gx, nx)], vector, precision=HIGHEST)
    pieces = split3(first[:96])
    field = dot(jnp.concatenate([pieces, pieces], axis=1), along_ref[gz])
    field_ref[...] = field[:96] + field[96:192] + field[192:]

    def column(cx, carry):
        rows = [pl.ds(pl.multiple_of(c * 32 + cx * 8, 8), 8) for c in range(3)]
        inside = pl.ds(pl.multiple_of(cx * 8, 8), 8)
        total = [[None] * 4 for _ in range(3)]
        for cz in range(CELLS_Z):
            layer = [
                [field_ref[rows[c], (cz + k) * LANES : (cz + k + 1) * LANES] for k in range(4)]
                for c in range(3)
            ]
            for t in range(8):
                weight = WEIGHTS[t]
                used = [k for k in range(4) if weight[k] != 0.0]
                slope = [grad_ref[c, cz * 8 + t, inside, :] for c in range(3)]
                shade = None
                for c in range(3):
                    value = None
                    for k in used:
                        term = weight[k] * layer[c][k]
                        value = term if value is None else value + term
                    term = slope[c] * value
                    shade = term if shade is None else shade + term
                for c in range(3):
                    value = slope[c] * shade
                    for k in used:
                        term = weight[k] * value
                        total[c][k] = term if total[c][k] is None else total[c][k] + term
            for c in range(3):
                sums_ref[rows[c], cz * LANES : (cz + 1) * LANES] = total[c][0]
                total[c] = total[c][1:] + [None]
        for c in range(3):
            for k in range(3):
                g = CELLS_Z + k
                sums_ref[rows[c], g * LANES : (g + 1) * LANES] = total[c][k]
        return carry

    lax.fori_loop(0, CELLS_X, column, 0)
    pieces = split3(sums_ref[...])
    back = dot(pieces, along_ref[gz], ((1,), (1,)))
    back = back[:, :LANES] + back[:, LANES:]
    back = back[:96] + back[96:192] + back[192:]
    data = dot(back_ref[...], back, precision=HIGHEST)
    relief = dot(
        jnp.concatenate([first[96:120], first[120:144]], axis=1),
        lanes_ref[gz * 3 + kind_of(gy, ny)],
        precision=HIGHEST,
    )
    return data + relief


def roll(value, shift, axis):
    return pltpu.roll(value, shift, axis)


def put(z):
    f = z + jnp.where(lax.axis_index("gz") == 0, 0, 1)
    row = lax.broadcasted_iota(jnp.int32, (16, LANES), 0)
    lane = lax.broadcasted_iota(jnp.int32, (16, LANES), 1)
    return (lane == row + (f * BOX_Y + 1)).astype(jnp.float32).astype(jnp.bfloat16)


def start_kernel(right_ref, out_ref):
    out_ref[...] = jnp.zeros((ROWS, LANES), jnp.float32)
    for c in range(3):
        value = None
        for z in range(CELLS_Z):
            rest = right_ref[c, z]
            for _ in range(3):
                piece = rest.astype(jnp.bfloat16)
                rest = rest - piece.astype(jnp.float32)
                term = dot(piece, put(z))
                value = term if value is None else value + term
        out_ref[c * 8 + 1 : c * 8 + 5, :] = value


def size_kernel(grad_ref, out_ref):
    def plane(z, totals):
        totals = list(totals)
        for x in range(4):
            slope = [grad_ref[c, z, x * 8 : x * 8 + 8, :] for c in range(3)]
            k = 0
            for a in range(3):
                for b in range(a, 3):
                    totals[k] = totals[k] + slope[a] * slope[b]
                    k += 1
        return tuple(totals)

    zero = jnp.zeros((8, LANES), jnp.float32)
    totals = lax.fori_loop(0, 32, plane, (zero,) * 6)
    count = 32.0 * 32.0 * 128.0
    xx, xy, xz, yy, yz, zz = [
        jnp.sum(jnp.sum(t, axis=0, keepdims=True), axis=1, keepdims=True) / count for t in totals
    ]
    aa = xx * xx + xy * xy + xz * xz
    bb = xy * xy + yy * yy + yz * yz
    cc = xz * xz + yz * yz + zz * zz
    ab = xx * xy + xy * yy + xz * yz
    ac = xx * xz + xy * yz + xz * zz
    bc = xy * xz + yy * yz + yz * zz
    norm = aa * aa + bb * bb + cc * cc + 2.0 * (ab * ab + ac * ac + bc * bc)
    size = 0.73 * jnp.sqrt(jnp.sqrt(norm)) + 0.04
    row = lax.broadcasted_iota(jnp.int32, (8, LANES), 0)
    out_ref[...] = jnp.where(row == 7, jnp.broadcast_to(size, (8, LANES)), 0.0)


def with_size(value, *others):
    row = lax.broadcasted_iota(jnp.int32, (ROWS, LANES), 0)
    return jnp.where(row == 7, functools.reduce(jnp.maximum, others), value)


def pair_sides(index, pair, other):
    even = lax.rem(index, 2) == 0
    return jnp.where(even, other, pair), jnp.where(even, pair, other)


def z_kernel(mine_ref, swap_ref, out_ref):
    gz = lax.axis_index("gz")
    _, f, _ = iotas()
    mine, swap = mine_ref[...], swap_ref[...]
    other = roll(swap, jnp.where(gz == 0, 3 * BOX_Y, LANES - 3 * BOX_Y), 1)
    first_f = jnp.where(gz == 0, 3, 0)
    value = mine + jnp.where((f >= first_f) & (f <= first_f + 2), other, 0.0)
    out_ref[...] = with_size(value, mine, swap)


def x_kernel(mine_ref, pair_ref, other_ref, *rest):
    out_ref = rest[-1]
    gx, nx = lax.axis_index("gx"), lax.axis_size("gx")
    kx, _, _ = iotas()
    mine, pair, other = mine_ref[...], pair_ref[...], other_ref[...]
    low, high = pair_sides(gx, pair, other)
    first_x, last_x = jnp.where(gx > 0, 2, -1), jnp.where(gx < nx - 1, 4, 8)
    value = mine + jnp.where(kx <= first_x, rows_rolled(low, 4), 0.0)
    value = value + jnp.where((kx >= last_x) & (kx <= 6), rows_rolled(high, 4), 0.0)
    out_ref[...] = with_size(value, mine, pair, other)


def x_first_kernel(mine_ref, size_ref, out_ref):
    out_ref[...] = mine_ref[...]
    row = lax.broadcasted_iota(jnp.int32, (8, LANES), 0)
    out_ref[0:8] = jnp.where(row == 7, size_ref[...], mine_ref[0:8])


def y_sum(mine_ref, pair_ref, other_ref):
    gy, ny = lax.axis_index("gy"), lax.axis_size("gy")
    _, _, e = iotas()
    mine, pair, other = mine_ref[...], pair_ref[...], other_ref[...]
    low, high = pair_sides(gy, pair, other)
    first_y, last_y = jnp.where(gy > 0, 2, -1), jnp.where(gy < ny - 1, 16, LANES)
    value = mine + jnp.where(e <= first_y, roll(low, LANES - 16, 1), 0.0)
    value = value + jnp.where(e >= last_y, roll(high, 16, 1), 0.0)
    return value, jnp.maximum(jnp.maximum(mine, pair), other)[7:8]


def rows_rolled(value, shift):
    return jnp.concatenate(
        [roll(value[c * 8 : c * 8 + 8], shift, 0) for c in range(3)], axis=0
    )


def middle_kernel(in_ref, out_ref):
    (gx, nx), _, (gz, nz) = places()
    kx, f, e = iotas()
    has_low = (gx > 0).astype(jnp.int32)
    has_high = (gx < nx - 1).astype(jnp.int32)
    low = jnp.maximum(gx - 1, 0)
    high = jnp.minimum(gx + 1, nx - 1)
    take_low = (kx <= 2) & (has_low == 1)
    take_high = (kx >= 4) & (kx <= 6) & (has_high == 1)

    def along_x(part):
        value = in_ref[gx * nz + part]
        below = rows_rolled(in_ref[low * nz + part], 4)
        above = rows_rolled(in_ref[high * nz + part], 4)
        value = value + jnp.where(take_low, below, 0.0)
        return value + jnp.where(take_high, above, 0.0)

    mine = along_x(gz)
    other = along_x(1 - gz)
    other = roll(other, jnp.where(gz == 0, 3 * BOX_Y, LANES - 3 * BOX_Y), 1)
    first_f = jnp.where(gz == 0, 3, 0)
    value = mine + jnp.where((f >= first_f) & (f <= first_f + 2), other, 0.0)
    everything = in_ref[0]
    for i in range(1, in_ref.shape[0]):
        everything = everything + in_ref[i]
    value = jnp.where(kx == 7, everything, value)
    for i in range(out_ref.shape[0]):
        out_ref[i] = value


def along_y_sum(in_ref):
    _, (gy, ny), _ = places()
    kx, f, e = iotas()
    has_low = (gy > 0).astype(jnp.int32)
    has_high = (gy < ny - 1).astype(jnp.int32)
    below = roll(in_ref[jnp.maximum(gy - 1, 0)], LANES - 16, 1)
    above = roll(in_ref[jnp.minimum(gy + 1, ny - 1)], 16, 1)
    value = in_ref[gy]
    value = value + jnp.where((e <= 2) & (has_low == 1), below, 0.0)
    value = value + jnp.where((e >= 16) & (has_high == 1), above, 0.0)
    everything = in_ref[0]
    for i in range(1, in_ref.shape[0]):
        everything = everything + in_ref[i]
    return value, everything


def message(vector, image, own, out_ref):
    norm = jnp.sum(own * vector * vector, axis=0, keepdims=True)
    product = jnp.sum(vector * image, axis=0, keepdims=True)
    row = lax.broadcasted_iota(jnp.int32, (ROWS, LANES), 0)
    value = jnp.where(row == 7, norm, image)
    value = jnp.where(row == 15, product, value)
    for i in range(out_ref.shape[0]):
        out_ref[i] = value


def spread(group, mine, next_one, opposite, previous):
    total = None
    for k in range(4):
        away = lax.rem(k - group + 4, 4)
        value = jnp.where(
            away == 0,
            mine,
            jnp.where(away == 1, next_one, jnp.where(away == 2, opposite, previous)),
        )
        total = value if total is None else total + value
    return total


def ring_line(index, mine_ref, other_ref, cross_ref, far_ref):
    odd = lax.rem(index, 2) == 1
    mine, other, cross, far = [r[7:8] for r in (mine_ref, other_ref, cross_ref, far_ref)]
    return spread(
        index // 2, mine, jnp.where(odd, other, cross), far, jnp.where(odd, cross, other)
    )


def with_line(value, line):
    row = lax.broadcasted_iota(jnp.int32, (ROWS, LANES), 0)
    return jnp.where(row == 7, line, value)


def z_last_kernel(mine_ref, swap_ref, out_ref):
    z_kernel(mine_ref, swap_ref, out_ref)
    out_ref[7:8] = mine_ref[7:8] + swap_ref[7:8]


def x_side(value, arrived, is_high):
    gx, nx = lax.axis_index("gx"), lax.axis_size("gx")
    kx, _, _ = iotas()
    there = jnp.where(is_high, gx < nx - 1, gx > 0)
    low, high = jnp.where(is_high, 4, 0), jnp.where(there, jnp.where(is_high, 6, 2), -1)
    return value + jnp.where((kx >= low) & (kx <= high), rows_rolled(arrived, 4), 0.0)


def y_side(value, arrived, is_high):
    gy, ny = lax.axis_index("gy"), lax.axis_size("gy")
    _, _, e = iotas()
    there = jnp.where(is_high, gy < ny - 1, gy > 0)
    low, high = jnp.where(is_high, 16, 0), jnp.where(there, jnp.where(is_high, 18, 2), -1)
    moved = roll(arrived, jnp.where(is_high, 16, LANES - 16), 1)
    return value + jnp.where((e >= low) & (e <= high), moved, 0.0)


def pair_kernel(axis, mine_ref, pair_ref, out_ref, line_ref):
    mine, pair = mine_ref[...], pair_ref[...]
    even = lax.rem(lax.axis_index(axis), 2) == 0
    value = (x_side if axis == "gx" else y_side)(mine, pair, even)
    out_ref[...] = with_line(value, mine[7:8] + pair[7:8])
    line_ref[...] = mine[0:8] + pair[0:8]


def x_last_kernel(mine_ref, other_ref, cross_ref, far_ref, out_ref):
    gx = lax.axis_index("gx")
    value = x_side(mine_ref[...], other_ref[...], lax.rem(gx, 2) == 1)
    out_ref[...] = with_line(value, ring_line(gx, mine_ref, other_ref, cross_ref, far_ref))


def basis_kernel(number, mine_ref, pair_ref, other_ref, *refs):
    past = refs[:number]
    operands = refs[number : number + 5]
    out_ref, *new_refs, field_ref, sums_ref = refs[number + 5 :]
    inside, own = masks(places())
    value, size = y_sum(mine_ref, pair_ref, other_ref)
    value = value * inside
    if number:
        value = value + DAMP * past[-1][...]
    if number == 3:
        inverse = 1.0 / size
        one, two = past[1][...], past[2][...]
        second = inverse * two - SHIFTS[1] * one
        value = inverse * (inverse * value - SHIFTS[1] * two) - SHIFTS[2] * second
        new_refs[1][...] = second
    elif number > 3:
        value = value / size - SHIFTS[number - 1] * past[-1][...]
    new_refs[0][...] = value
    image = apply_local(value, *operands, field_ref, sums_ref) * inside
    if number < 5:
        out_ref[...] = with_size(image, jnp.broadcast_to(size, (ROWS, LANES)))
        return
    new_refs[1][...] = jnp.broadcast_to(size, (8, LANES))
    vectors = [ref[...] for ref in past] + [value]
    products = []
    for i in range(6):
        mine = own * vectors[i]
        for j in range(i, 6):
            products.append(mine * vectors[j])
    products.append(value * image + DAMP * own * value * value)
    sums = [jnp.sum(p, axis=0, keepdims=True) for p in products]
    sums = jnp.concatenate(sums + [jnp.zeros((2, LANES), jnp.float32)], axis=0)
    sums = jnp.sum(sums, axis=1, keepdims=True)
    row = lax.broadcasted_iota(jnp.int32, (ROWS, LANES), 0)
    lane = lax.broadcasted_iota(jnp.int32, (ROWS, LANES), 1)
    line = jnp.sum(jnp.where(row == lane, sums, 0.0), axis=0, keepdims=True)
    image = jnp.where(row == 7, line, image)
    out_ref[...] = image


def add(a, b):
    return b if a is None else a if b is None else a + b


def times(a, b):
    return None if a is None or b is None else a * b


def form(left, table, right):
    total = None
    for i, a in enumerate(left):
        inner = None
        for j, b in enumerate(right):
            inner = add(inner, times(table[i][j], b))
        total = add(total, times(a, inner))
    return total


def fast_kernel(mine_ref, other_ref, cross_ref, far_ref, *refs):
    vectors = [ref[...] for ref in refs[:6]]
    size_ref, solution_ref, residual_ref, good_ref = refs[6:]
    inside, _ = masks(places())
    gy = lax.axis_index("gy")
    value = y_side(mine_ref[...], other_ref[...], lax.rem(gy, 2) == 1)
    size = size_ref[0:1, 0:1]
    inverse = 1.0 / size
    image = (value * inside + DAMP * vectors[5]) * inverse
    line = ring_line(gy, mine_ref, other_ref, cross_ref, far_ref)
    lane = lax.broadcasted_iota(jnp.int32, (1, LANES), 1)
    scalars = [jnp.sum(jnp.where(lane == k, line, 0.0), axis=1, keepdims=True) for k in range(22)]
    gram = [[None] * 6 for _ in range(6)]
    k = 0
    for i in range(6):
        for j in range(i, 6):
            gram[i][j] = gram[j][i] = scalars[k]
            k += 1
    factor = [inverse] + [jnp.ones_like(inverse)] * 4
    energy = [[None] * 6 for _ in range(6)]
    for i in range(5):
        for j in range(i, 6):
            energy[i][j] = energy[j][i] = factor[i] * (gram[i + 1][j] + SHIFTS[i] * gram[i][j])
    energy[5][5] = scalars[21] * inverse
    rest = [row[:] for row in gram]
    good = jnp.ones_like(inverse)
    for k in range(6):
        good = jnp.where(rest[k][k] / gram[k][k] > WORST_PIVOT, good, 0.0)
        for i in range(k + 1, 6):
            ratio = rest[i][k] / rest[k][k]
            for j in range(i, 6):
                rest[i][j] = rest[i][j] - ratio * rest[k][j]
                rest[j][i] = rest[i][j]
    good_ref[...] = jnp.broadcast_to(good, (8, LANES))
    solved = [None] * 7
    residual = [jnp.ones_like(inverse)] + [None] * 6
    direction = residual[:]
    norm = gram[0][0]
    for number in range(ITERS):
        known = number + 1
        moved = [None] * 7
        for j in range(known):
            if j == 5:
                moved[6] = add(moved[6], direction[5])
            else:
                part = factor[j] * direction[j]
                moved[j + 1] = add(moved[j + 1], part)
                moved[j] = add(moved[j], SHIFTS[j] * part)
        step = norm / form(direction[:known], energy, direction[:known])
        solved = [add(a, times(step, b)) for a, b in zip(solved, direction)]
        residual = [add(a, times(-step, b)) for a, b in zip(residual, moved)]
        if number < ITERS - 1:
            known += 1
            later = form(residual[:known], gram, residual[:known])
            ratio = later / norm
            direction = [add(a, times(ratio, b)) for a, b in zip(residual, direction)]
            norm = later
    vectors = vectors + [image]
    first, second = None, None
    for j in range(7):
        if solved[j] is not None:
            first = add(first, solved[j] * vectors[j])
        second = add(second, residual[j] * vectors[j])
    write_out(first * (inverse / SCALE), second, solution_ref, residual_ref)


def write_out(solved, residual, solution_ref, residual_ref):
    both = jnp.concatenate([solved, residual], axis=0)
    pieces = split3(both)
    for z in range(CELLS_Z):
        value = dot(pieces, put(z), ((1,), (1,)))
        value = value[:48] + value[48:96] + value[96:]
        for c in range(3):
            solution_ref[c, z] = value[c * 8 + 1 : c * 8 + 5]
            residual_ref[c, z] = value[ROWS + c * 8 + 1 : ROWS + c * 8 + 5]


def slow_kernel(vector_ref, grad_ref, rows_ref, back_ref, along_ref, lanes_ref, out_ref, field_ref, sums_ref):
    inside, own = masks(places())
    vector = vector_ref[...]
    image = apply_local(vector, grad_ref, rows_ref, back_ref, along_ref, lanes_ref, field_ref, sums_ref)
    message(vector, image * inside, own, out_ref)


def update(in_ref, old_ref, number):
    inside, own = masks(places())
    value, everything = along_y_sum(in_ref)
    residual = old_ref[ROWS : 2 * ROWS] if number else old_ref[...]
    image = value * inside + DAMP * residual
    norm = jnp.sum(everything[7:8], axis=1, keepdims=True)
    product = jnp.sum(everything[15:16], axis=1, keepdims=True) + DAMP * norm
    if number:
        ratio = norm / old_ref[4 * ROWS : 4 * ROWS + 1, 0:1]
        step = norm / (product - ratio * norm / old_ref[4 * ROWS + 1 : 4 * ROWS + 2, 0:1])
        direction = residual + ratio * old_ref[2 * ROWS : 3 * ROWS]
        image = image + ratio * old_ref[3 * ROWS : 4 * ROWS]
        solved = old_ref[0:ROWS] + step * direction
    else:
        step = norm / product
        direction = residual
        solved = step * direction
    residual = residual - step * image
    return own, inside, solved, residual, direction, image, norm, step


def step_kernel(number, in_ref, old_ref, grad_ref, rows_ref, back_ref, along_ref, lanes_ref, out_ref, new_ref, field_ref, sums_ref):
    own, inside, solved, residual, direction, image, norm, step = update(in_ref, old_ref, number)
    new_ref[0:ROWS] = solved
    new_ref[ROWS : 2 * ROWS] = residual
    new_ref[2 * ROWS : 3 * ROWS] = direction
    new_ref[3 * ROWS : 4 * ROWS] = image
    row = lax.broadcasted_iota(jnp.int32, (8, LANES), 0)
    new_ref[4 * ROWS : 4 * ROWS + 8] = jnp.where(row == 0, norm, step)
    image = apply_local(residual, grad_ref, rows_ref, back_ref, along_ref, lanes_ref, field_ref, sums_ref)
    message(residual, image * inside, own, out_ref)


def last_kernel(in_ref, old_ref, solution_ref, residual_ref):
    _, _, solved, residual, _, _, _, _ = update(in_ref, old_ref, ITERS - 1)
    write_out(solved / SCALE, residual, solution_ref, residual_ref)


def call(body, outs, *args, scratch=False):
    shapes = [jax.ShapeDtypeStruct(s, jnp.float32) for s in outs]
    scratch_shapes = [pltpu.VMEM((96, 7 * LANES), jnp.float32)] * 2 if scratch else []
    vmem = pl.BlockSpec(memory_space=pltpu.VMEM)
    return pl.pallas_call(
        body,
        out_shape=shapes,
        in_specs=[vmem] * len(args),
        out_specs=[vmem] * len(outs),
        scratch_shapes=scratch_shapes,
        compiler_params=pltpu.CompilerParams(vmem_limit_bytes=24 * 1024 * 1024),
    )(*args)


def swaps(axis):
    count = lax.axis_size(axis)
    pair = [(i, i ^ 1) for i in range(count)]
    other = [(i, (i + 1 if i % 2 else i - 1) % count) for i in range(count)]
    groups = range(count // 2)
    cross, far = [], []
    for i in groups:
        after = (i + 1) % len(groups)
        cross += [(2 * i, 2 * after + 1), (2 * after + 1, 2 * i)]
        far += [(2 * i + c, 2 * ((i + 2) % len(groups)) + c) for c in range(2)]
    return pair, other, cross, far


def shards(gradient, right_side):
    (_, nx), (_, ny), (_, nz) = places()
    rows_x, back_x, along_y, lanes = [jnp.asarray(t) for t in tables()]
    operands = (gradient, rows_x, back_x, along_y, lanes)
    group, line, box = (nx * nz, ROWS, LANES), (ny, ROWS, LANES), (ROWS, LANES)
    tile, state, shape = (8, LANES), (4 * ROWS + 8, LANES), right_side.shape

    def exchange_all(sent):
        near = lax.all_to_all(sent, ("gx", "gz"), 0, 0)
        (sent,) = call(middle_kernel, [line], near)
        return lax.all_to_all(sent, "gy", 0, 0)

    def exchange_near(sent, size=None):
        swapped = lax.ppermute(sent, "gz", swaps("gz")[0])
        (sent,) = call(z_kernel, [box], sent, swapped)
        if size is not None:
            (sent,) = call(x_first_kernel, [box], sent, size)
        pair, other = [lax.ppermute(sent, "gx", s) for s in swaps("gx")[:2]]
        (sent,) = call(x_kernel, [box], sent, pair, other)
        pair, other = [lax.ppermute(sent, "gy", s) for s in swaps("gy")[:2]]
        return sent, pair, other

    def exchange_last(sent):
        (sent,) = call(z_last_kernel, [box], sent, lax.ppermute(sent, "gz", swaps("gz")[0]))
        for axis in ("gx", "gy"):
            pair, other, cross, far = swaps(axis)
            arrived = lax.ppermute(sent, axis, pair)
            body = functools.partial(pair_kernel, axis)
            sent, line = call(body, [box, tile], sent, arrived)
            arrived = lax.ppermute(sent, axis, other)
            lines = [lax.ppermute(line, axis, p) for p in (cross, far)]
            if axis == "gx":
                (sent,) = call(x_last_kernel, [box], sent, arrived, *lines)
        return sent, arrived, *lines

    def slow(first):
        (sent,) = call(slow_kernel, [group], first, *operands, scratch=True)
        old = first
        for number in range(ITERS - 1):
            body = functools.partial(step_kernel, number)
            sent, old = call(body, [group, state], exchange_all(sent), old, *operands, scratch=True)
        return tuple(call(last_kernel, [shape, shape], exchange_all(sent), old))

    (sent,) = call(start_kernel, [box], right_side)
    (size,) = call(size_kernel, [tile], gradient)
    vectors = []
    for number in range(6):
        near = exchange_near(sent, size if number == 0 else None)
        outs = [box, box] + [[], [], [], [box], [], [tile]][number]
        body = functools.partial(basis_kernel, number)
        sent, vector, *extra = call(body, outs, *near, *vectors, *operands, scratch=True)
        if number == 3:
            vectors[2] = extra[0]
        vectors.append(vector)
    *fast, good = call(fast_kernel, [shape, shape, tile], *exchange_last(sent), *vectors, extra[0])
    return lax.cond(good[0, 0] > 0.5, lambda first: tuple(fast), slow, vectors[0])


def solution(mesh):
    placed = P(None, "gz", "gx", "gy")
    return jax.shard_map(
        shards,
        mesh=mesh,
        in_specs=(placed, placed),
        out_specs=(placed, placed),
        check_vma=False,
    )
```

```python
import functools

import jax
import jax.numpy as jnp
import ml_dtypes
import numpy as np
from jax import lax
from jax.experimental import pallas as pl
from jax.experimental.pallas import tpu as pltpu
from jax.sharding import PartitionSpec as P

ITERS = 6
SMOOTHING = 0.5
DAMPING = 0.05
HIGHEST = lax.Precision.HIGHEST

CELLS_Z, CELLS_X, CELLS_Y = 4, 4, 8
BOX_X, BOX_Y, BOX_Z = 7, 11, 8
LANES = 128
ROWS = 24
DENOMINATOR = 3072.0
SCALE = 512.0
DAMP = DAMPING / SCALE
SHIFTS = (0.0, 0.171, 0.452, 0.776, 0.114)
WORST_PIVOT = 0.05


def numerators(t):
    return (
        (8 - t) ** 3,
        3 * t**3 - 48 * t**2 + 2048,
        -3 * t**3 + 24 * t**2 + 192 * t + 512,
        t**3,
    )


WEIGHTS = [[n / DENOMINATOR for n in numerators(t)] for t in range(8)]


def basis(cells):
    table = np.zeros((8 * cells + 1, cells + 3 + 1))
    for voxel in range(8 * cells + 1):
        for k, n in enumerate(numerators(voxel % 8)):
            table[voxel, voxel // 8 + k] = n
    return table[:, :-1]


def mass_and_edges(cells, first, last):
    table = basis(cells) / DENOMINATOR
    own = table[:-1]
    steps = table[1:] - table[:-1]
    if last:
        steps[-1] = -table[-2]
    edges = steps.T @ steps
    if first:
        edges = edges + np.outer(table[0], table[0])
    return own.T @ own, edges


@functools.lru_cache(None)
def tables():
    bx = basis(CELLS_X)[:-1]
    expand = np.zeros((96, ROWS))
    for c in range(3):
        expand[c * 32 : c * 32 + 32, c * 8 : c * 8 + BOX_X] = bx / DENOMINATOR / DENOMINATOR
    rows_x = np.zeros((3, 144, ROWS), np.float32)
    for kind in range(3):
        mass, edges = mass_and_edges(CELLS_X, kind == 0, kind == 2)
        rows_x[kind, :96] = expand
        for c in range(3):
            at = slice(c * 8, c * 8 + BOX_X)
            rows_x[kind, 96 + c * 8 : 96 + c * 8 + BOX_X, at] = SMOOTHING / SCALE * mass
            rows_x[kind, 120 + c * 8 : 120 + c * 8 + BOX_X, at] = SMOOTHING / SCALE * edges
    by = basis(CELLS_Y)[:-1]
    low = by.T.astype(ml_dtypes.bfloat16).astype(np.float64)
    along_y = np.zeros((2, LANES, 7 * LANES))
    for half in range(2):
        for g in range(7):
            f = g - 1 + 4 * half
            if 0 <= f < BOX_Z:
                rows = slice(f * BOX_Y, (f + 1) * BOX_Y)
                at = slice(g * LANES + half * 64, g * LANES + half * 64 + 64)
                along_y[0, rows, at] = low
                along_y[1, rows, at] = by.T - low
    along_y = along_y.reshape(256, 7 * LANES).astype(ml_dtypes.bfloat16)
    mz, kz = [m[1 : 1 + BOX_Z, 1 : 1 + BOX_Z] for m in mass_and_edges(2 * CELLS_Z, True, True)]
    lanes = np.zeros((3, 256, LANES), np.float32)
    used = BOX_Z * BOX_Y
    for kind in range(3):
        my, ky = mass_and_edges(CELLS_Y, kind == 0, kind == 2)
        lanes[kind, :used, :used] = np.kron(kz, my) + np.kron(mz, ky)
        lanes[kind, 128 : 128 + used, :used] = np.kron(mz, my)
    return (
        rows_x,
        (expand.T / SCALE).astype(np.float32),
        along_y,
        lanes,
    )


def iotas():
    row = lax.broadcasted_iota(jnp.int32, (ROWS, LANES), 0)
    lane = lax.broadcasted_iota(jnp.int32, (ROWS, LANES), 1)
    f = jnp.zeros_like(lane)
    for k in range(1, BOX_Z + 1):
        f = f + (lane >= k * BOX_Y).astype(jnp.int32)
    return row & 7, f, lane - f * BOX_Y


def places():
    gx, nx = lax.axis_index("gx"), lax.axis_size("gx")
    gz, nz = lax.axis_index("gz"), lax.axis_size("gz")
    return (gx, nx), (lax.axis_index("gy") * nz + gz, lax.axis_size("gy") * nz)


def masks(where):
    (gx, nx), (q, nq) = where
    kx, f, e = iotas()
    low_x, high_x = jnp.where(gx == 0, 1, 0), jnp.where(gx == nx - 1, 4, 6)
    low_y, high_y = jnp.where(q == 0, 1, 0), jnp.where(q == nq - 1, 8, 10)
    inside = (kx >= low_x) & (kx <= high_x) & (e >= low_y) & (e <= high_y) & (f < BOX_Z)
    own = (kx >= 1) & (kx <= 4) & (e >= 1) & (e <= 8) & (f < BOX_Z)
    return inside.astype(jnp.float32), own.astype(jnp.float32)


def split3(value):
    high = value.astype(jnp.bfloat16)
    rest = value - high.astype(jnp.float32)
    middle = rest.astype(jnp.bfloat16)
    low = (rest - middle.astype(jnp.float32)).astype(jnp.bfloat16)
    return jnp.concatenate([high, middle, low], axis=0)


def dot(a, b, dims=((1,), (0,)), precision=None):
    return lax.dot_general(
        a, b, (dims, ((), ())), precision=precision, preferred_element_type=jnp.float32
    )


def kind_of(index, count):
    return jnp.where(index == 0, 0, jnp.where(index == count - 1, 2, 1))


def apply_local(vector, grad_ref, rows_ref, back_ref, along_ref, lanes_ref, field_ref, sums_ref):
    (gx, nx), (q, nq) = places()
    first = dot(rows_ref[kind_of(gx, nx)], vector, precision=HIGHEST)
    pieces = split3(first[:96])
    field = dot(jnp.concatenate([pieces, pieces], axis=1), along_ref[...])
    field_ref[...] = field[:96] + field[96:192] + field[192:]

    def column(cx, carry):
        rows = [pl.ds(pl.multiple_of(c * 32 + cx * 8, 8), 8) for c in range(3)]
        inside = pl.ds(pl.multiple_of(cx * 8, 8), 8)
        total = [[None] * 4 for _ in range(3)]
        for cz in range(CELLS_Z):
            layer = [
                [field_ref[rows[c], (cz + k) * LANES : (cz + k + 1) * LANES] for k in range(4)]
                for c in range(3)
            ]
            for t in range(8):
                weight = WEIGHTS[t]
                used = [k for k in range(4) if weight[k] != 0.0]
                slope = [grad_ref[c, cz * 8 + t, inside, :] for c in range(3)]
                shade = None
                for c in range(3):
                    value = None
                    for k in used:
                        term = weight[k] * layer[c][k]
                        value = term if value is None else value + term
                    term = slope[c] * value
                    shade = term if shade is None else shade + term
                for c in range(3):
                    value = slope[c] * shade
                    for k in used:
                        term = weight[k] * value
                        total[c][k] = term if total[c][k] is None else total[c][k] + term
            for c in range(3):
                sums_ref[rows[c], cz * LANES : (cz + 1) * LANES] = total[c][0]
                total[c] = total[c][1:] + [None]
        for c in range(3):
            for k in range(3):
                g = CELLS_Z + k
                sums_ref[rows[c], g * LANES : (g + 1) * LANES] = total[c][k]
        return carry

    lax.fori_loop(0, CELLS_X, column, 0)
    pieces = split3(sums_ref[...])
    back = dot(pieces, along_ref[...], ((1,), (1,)))
    back = back[:, :LANES] + back[:, LANES:]
    back = back[:96] + back[96:192] + back[192:]
    data = dot(back_ref[...], back, precision=HIGHEST)
    relief = dot(
        jnp.concatenate([first[96:120], first[120:144]], axis=1),
        lanes_ref[kind_of(q, nq)],
        precision=HIGHEST,
    )
    return data + relief


def roll(value, shift, axis):
    return pltpu.roll(value, shift, axis)


def put(z, half):
    f = z + CELLS_Z * lax.axis_index("gz")
    row = lax.broadcasted_iota(jnp.int32, (16, LANES), 0) - 8 * half
    lane = lax.broadcasted_iota(jnp.int32, (16, LANES), 1)
    hit = (lane == row + (f * BOX_Y + 1)) & (row >= 0) & (row < 8)
    return hit.astype(jnp.float32).astype(jnp.bfloat16)


def start_kernel(right_ref, mine_ref, theirs_ref):
    gz = lax.axis_index("gz")
    for half, out_ref in ((gz, mine_ref), (1 - gz, theirs_ref)):
        out_ref[...] = jnp.zeros((ROWS, LANES), jnp.float32)
        places_z = [put(z, half) for z in range(CELLS_Z)]
        for c in range(3):
            value = None
            for z in range(CELLS_Z):
                rest = right_ref[c, z]
                for _ in range(3):
                    piece = rest.astype(jnp.bfloat16)
                    rest = rest - piece.astype(jnp.float32)
                    term = dot(piece, places_z[z])
                    value = term if value is None else value + term
            out_ref[c * 8 + 1 : c * 8 + 5, :] = value


def pack_kernel(grad_ref, out_ref):
    first = lax.axis_index("gz") == 0
    left = lax.broadcasted_iota(jnp.int32, (32, LANES), 1) < 64

    def plane(z, carry):
        for c in range(3):
            one, two = grad_ref[c, z], grad_ref[c, z + 16]
            one = jnp.where(first, roll(one, 64, 1), one)
            two = jnp.where(first, two, roll(two, 64, 1))
            out_ref[c, z] = jnp.where(left, one, two)
        return carry

    lax.fori_loop(0, 16, plane, 0)


def unpack_kernel(grad_ref, in_ref, out_ref):
    first = lax.axis_index("gz") == 0
    left = lax.broadcasted_iota(jnp.int32, (32, LANES), 1) < 64
    keep = left == first

    def plane(z, carry):
        for c in range(3):
            arrived = in_ref[c, z]
            moved = roll(arrived, 64, 1)
            out_ref[c, z] = jnp.where(keep, grad_ref[c, z], jnp.where(first, moved, arrived))
            out_ref[c, z + 16] = jnp.where(
                keep, grad_ref[c, z + 16], jnp.where(first, arrived, moved)
            )
        return carry

    lax.fori_loop(0, 16, plane, 0)


def size_kernel(grad_ref, out_ref):
    def plane(z, totals):
        totals = list(totals)
        for x in range(4):
            slope = [grad_ref[c, z, x * 8 : x * 8 + 8, :] for c in range(3)]
            k = 0
            for a in range(3):
                for b in range(a, 3):
                    totals[k] = totals[k] + slope[a] * slope[b]
                    k += 1
        return tuple(totals)

    zero = jnp.zeros((8, LANES), jnp.float32)
    totals = lax.fori_loop(0, 32, plane, (zero,) * 6)
    count = 32.0 * 32.0 * 128.0
    xx, xy, xz, yy, yz, zz = [
        jnp.sum(jnp.sum(t, axis=0, keepdims=True), axis=1, keepdims=True) / count for t in totals
    ]
    aa = xx * xx + xy * xy + xz * xz
    bb = xy * xy + yy * yy + yz * yz
    cc = xz * xz + yz * yz + zz * zz
    ab = xx * xy + xy * yy + xz * yz
    ac = xx * xz + xy * yz + xz * zz
    bc = xy * xz + yy * yz + yz * zz
    norm = aa * aa + bb * bb + cc * cc + 2.0 * (ab * ab + ac * ac + bc * bc)
    size = 0.73 * jnp.sqrt(jnp.sqrt(norm)) + 0.04
    row = lax.broadcasted_iota(jnp.int32, (8, LANES), 0)
    out_ref[...] = jnp.where(row == 7, jnp.broadcast_to(size, (8, LANES)), 0.0)


def with_size(value, *others):
    row = lax.broadcasted_iota(jnp.int32, (ROWS, LANES), 0)
    return jnp.where(row == 7, functools.reduce(jnp.maximum, others), value)


def pair_sides(index, pair, other):
    even = lax.rem(index, 2) == 0
    return jnp.where(even, other, pair), jnp.where(even, pair, other)


def x_kernel(mine_ref, pair_ref, other_ref, *rest):
    out_ref = rest[-1]
    gx, nx = lax.axis_index("gx"), lax.axis_size("gx")
    kx, _, _ = iotas()
    mine, pair, other = mine_ref[...], pair_ref[...], other_ref[...]
    low, high = pair_sides(gx, pair, other)
    first_x, last_x = jnp.where(gx > 0, 2, -1), jnp.where(gx < nx - 1, 4, 8)
    value = mine + jnp.where(kx <= first_x, rows_rolled(low, 4), 0.0)
    value = value + jnp.where((kx >= last_x) & (kx <= 6), rows_rolled(high, 4), 0.0)
    out_ref[...] = with_size(value, mine, pair, other)


def x_first_kernel(mine_ref, theirs_ref, size_ref, far_ref, out_ref):
    out_ref[...] = mine_ref[...] + theirs_ref[...]
    out_ref[7:8] = jnp.maximum(size_ref[7:8], far_ref[7:8])


def y_sum(mine_ref, pair_ref, other_ref):
    _, (q, nq) = places()
    _, _, e = iotas()
    mine, pair, other = mine_ref[...], pair_ref[...], other_ref[...]
    low, high = pair_sides(q, pair, other)
    first_y, last_y = jnp.where(q > 0, 2, -1), jnp.where(q < nq - 1, 8, LANES)
    value = mine + jnp.where(e <= first_y, roll(low, LANES - 8, 1), 0.0)
    value = value + jnp.where(e >= last_y, roll(high, 8, 1), 0.0)
    return value, jnp.maximum(jnp.maximum(mine, pair), other)[7:8]


def rows_rolled(value, shift):
    return jnp.concatenate(
        [roll(value[c * 8 : c * 8 + 8], shift, 0) for c in range(3)], axis=0
    )


def middle_kernel(in_ref, out_ref):
    (gx, nx), _ = places()
    kx, _, _ = iotas()
    first_x, last_x = jnp.where(gx > 0, 2, -1), jnp.where(gx < nx - 1, 4, 8)
    low, high = in_ref[jnp.maximum(gx - 1, 0)], in_ref[jnp.minimum(gx + 1, nx - 1)]
    value = in_ref[gx] + jnp.where(kx <= first_x, rows_rolled(low, 4), 0.0)
    value = value + jnp.where((kx >= last_x) & (kx <= 6), rows_rolled(high, 4), 0.0)
    value = jnp.where(kx == 7, total_of(in_ref), value)
    for i in range(out_ref.shape[0]):
        out_ref[i] = value


def total_of(in_ref):
    total = in_ref[0]
    for i in range(1, in_ref.shape[0]):
        total = total + in_ref[i]
    return total


def along_y_sum(in_ref):
    _, (q, nq) = places()
    _, _, e = iotas()
    first_y, last_y = jnp.where(q > 0, 2, -1), jnp.where(q < nq - 1, 8, LANES)
    low, high = in_ref[jnp.maximum(q - 1, 0)], in_ref[jnp.minimum(q + 1, nq - 1)]
    value = in_ref[q] + jnp.where(e <= first_y, roll(low, LANES - 8, 1), 0.0)
    value = value + jnp.where(e >= last_y, roll(high, 8, 1), 0.0)
    return value, total_of(in_ref)


def message(vector, image, own, out_ref):
    norm = jnp.sum(own * vector * vector, axis=0, keepdims=True)
    product = jnp.sum(vector * image, axis=0, keepdims=True)
    row = lax.broadcasted_iota(jnp.int32, (ROWS, LANES), 0)
    value = jnp.where(row == 7, norm, image)
    value = jnp.where(row == 15, product, value)
    for i in range(out_ref.shape[0]):
        out_ref[i] = value


def basis_kernel(number, mine_ref, pair_ref, other_ref, *refs):
    past = refs[:number]
    operands = refs[number : number + 5]
    out_ref, *new_refs, field_ref, sums_ref = refs[number + 5 :]
    inside, own = masks(places())
    value, size = y_sum(mine_ref, pair_ref, other_ref)
    value = value * inside
    if number:
        value = value + DAMP * past[-1][...]
    if number == 3:
        inverse = 1.0 / size
        one, two = past[1][...], past[2][...]
        second = inverse * two - SHIFTS[1] * one
        value = inverse * (inverse * value - SHIFTS[1] * two) - SHIFTS[2] * second
        new_refs[1][...] = second
    elif number > 3:
        value = value / size - SHIFTS[number - 1] * past[-1][...]
    new_refs[0][...] = value
    image = apply_local(value, *operands, field_ref, sums_ref) * inside
    if number < 5:
        out_ref[...] = with_size(image, jnp.broadcast_to(size, (ROWS, LANES)))
        return
    new_refs[1][...] = jnp.broadcast_to(size, (8, LANES))
    vectors = [ref[...] for ref in past] + [value]
    products = []
    for i in range(6):
        mine = own * vectors[i]
        for j in range(i, 6):
            products.append(mine * vectors[j])
    products.append(value * image + DAMP * own * value * value)
    sums = [jnp.sum(p, axis=0, keepdims=True) for p in products]
    sums = jnp.concatenate(sums + [jnp.zeros((2, LANES), jnp.float32)], axis=0)
    sums = jnp.sum(sums, axis=1, keepdims=True)
    row = lax.broadcasted_iota(jnp.int32, (ROWS, LANES), 0)
    lane = lax.broadcasted_iota(jnp.int32, (ROWS, LANES), 1)
    line = jnp.sum(jnp.where(row == lane, sums, 0.0), axis=0, keepdims=True)
    image = jnp.where(row == 7, line, image)
    for i in range(out_ref.shape[0]):
        out_ref[i] = image


def add(a, b):
    return b if a is None else a if b is None else a + b


def times(a, b):
    return None if a is None or b is None else a * b


def form(left, table, right):
    total = None
    for i, a in enumerate(left):
        inner = None
        for j, b in enumerate(right):
            inner = add(inner, times(table[i][j], b))
        total = add(total, times(a, inner))
    return total


def fast_kernel(in_ref, *refs):
    vectors = [ref[...] for ref in refs[:6]]
    size_ref, both_ref, good_ref = refs[6:]
    inside, _ = masks(places())
    value, everything = along_y_sum(in_ref)
    size = size_ref[0:1, 0:1]
    inverse = 1.0 / size
    image = (value * inside + DAMP * vectors[5]) * inverse
    line = everything[7:8]
    lane = lax.broadcasted_iota(jnp.int32, (1, LANES), 1)
    scalars = [jnp.sum(jnp.where(lane == k, line, 0.0), axis=1, keepdims=True) for k in range(22)]
    gram = [[None] * 6 for _ in range(6)]
    k = 0
    for i in range(6):
        for j in range(i, 6):
            gram[i][j] = gram[j][i] = scalars[k]
            k += 1
    factor = [inverse] + [jnp.ones_like(inverse)] * 4
    energy = [[None] * 6 for _ in range(6)]
    for i in range(5):
        for j in range(i, 6):
            energy[i][j] = energy[j][i] = factor[i] * (gram[i + 1][j] + SHIFTS[i] * gram[i][j])
    energy[5][5] = scalars[21] * inverse
    rest = [row[:] for row in gram]
    good = jnp.ones_like(inverse)
    for k in range(6):
        good = jnp.where(rest[k][k] / gram[k][k] > WORST_PIVOT, good, 0.0)
        for i in range(k + 1, 6):
            ratio = rest[i][k] / rest[k][k]
            for j in range(i, 6):
                rest[i][j] = rest[i][j] - ratio * rest[k][j]
                rest[j][i] = rest[i][j]
    good_ref[...] = jnp.broadcast_to(good, (8, LANES))
    solved = [None] * 7
    residual = [jnp.ones_like(inverse)] + [None] * 6
    direction = residual[:]
    norm = gram[0][0]
    for number in range(ITERS):
        known = number + 1
        moved = [None] * 7
        for j in range(known):
            if j == 5:
                moved[6] = add(moved[6], direction[5])
            else:
                part = factor[j] * direction[j]
                moved[j + 1] = add(moved[j + 1], part)
                moved[j] = add(moved[j], SHIFTS[j] * part)
        step = norm / form(direction[:known], energy, direction[:known])
        solved = [add(a, times(step, b)) for a, b in zip(solved, direction)]
        residual = [add(a, times(-step, b)) for a, b in zip(residual, moved)]
        if number < ITERS - 1:
            known += 1
            later = form(residual[:known], gram, residual[:known])
            ratio = later / norm
            direction = [add(a, times(ratio, b)) for a, b in zip(residual, direction)]
            norm = later
    vectors = vectors + [image]
    first, second = None, None
    for j in range(7):
        if solved[j] is not None:
            first = add(first, solved[j] * vectors[j])
        second = add(second, residual[j] * vectors[j])
    both_ref[0:ROWS] = first * (inverse / SCALE)
    both_ref[ROWS:] = second


def finish_kernel(mine_ref, theirs_ref, solution_ref, residual_ref):
    gz = lax.axis_index("gz")
    mine, theirs = split3(mine_ref[...]), split3(theirs_ref[...])
    for z in range(CELLS_Z):
        value = dot(mine, put(z, gz), ((1,), (1,))) + dot(theirs, put(z, 1 - gz), ((1,), (1,)))
        value = value[:48] + value[48:96] + value[96:]
        for c in range(3):
            solution_ref[c, z] = value[c * 8 + 1 : c * 8 + 5]
            residual_ref[c, z] = value[ROWS + c * 8 + 1 : ROWS + c * 8 + 5]


def slow_kernel(vector_ref, grad_ref, rows_ref, back_ref, along_ref, lanes_ref, out_ref, field_ref, sums_ref):
    inside, own = masks(places())
    vector = vector_ref[...]
    image = apply_local(vector, grad_ref, rows_ref, back_ref, along_ref, lanes_ref, field_ref, sums_ref)
    message(vector, image * inside, own, out_ref)


def update(in_ref, old_ref, number):
    inside, own = masks(places())
    value, everything = along_y_sum(in_ref)
    residual = old_ref[ROWS : 2 * ROWS] if number else old_ref[...]
    image = value * inside + DAMP * residual
    norm = jnp.sum(everything[7:8], axis=1, keepdims=True)
    product = jnp.sum(everything[15:16], axis=1, keepdims=True) + DAMP * norm
    if number:
        ratio = norm / old_ref[4 * ROWS : 4 * ROWS + 1, 0:1]
        step = norm / (product - ratio * norm / old_ref[4 * ROWS + 1 : 4 * ROWS + 2, 0:1])
        direction = residual + ratio * old_ref[2 * ROWS : 3 * ROWS]
        image = image + ratio * old_ref[3 * ROWS : 4 * ROWS]
        solved = old_ref[0:ROWS] + step * direction
    else:
        step = norm / product
        direction = residual
        solved = step * direction
    residual = residual - step * image
    return own, inside, solved, residual, direction, image, norm, step


def step_kernel(number, in_ref, old_ref, grad_ref, rows_ref, back_ref, along_ref, lanes_ref, out_ref, new_ref, field_ref, sums_ref):
    own, inside, solved, residual, direction, image, norm, step = update(in_ref, old_ref, number)
    new_ref[0:ROWS] = solved
    new_ref[ROWS : 2 * ROWS] = residual
    new_ref[2 * ROWS : 3 * ROWS] = direction
    new_ref[3 * ROWS : 4 * ROWS] = image
    row = lax.broadcasted_iota(jnp.int32, (8, LANES), 0)
    new_ref[4 * ROWS : 4 * ROWS + 8] = jnp.where(row == 0, norm, step)
    image = apply_local(residual, grad_ref, rows_ref, back_ref, along_ref, lanes_ref, field_ref, sums_ref)
    message(residual, image * inside, own, out_ref)


def last_kernel(in_ref, old_ref, both_ref):
    _, _, solved, residual, _, _, _, _ = update(in_ref, old_ref, ITERS - 1)
    both_ref[0:ROWS] = solved / SCALE
    both_ref[ROWS:] = residual


def call(body, outs, *args, scratch=False):
    shapes = [jax.ShapeDtypeStruct(s, jnp.float32) for s in outs]
    scratch_shapes = [pltpu.VMEM((96, 7 * LANES), jnp.float32)] * 2 if scratch else []
    vmem = pl.BlockSpec(memory_space=pltpu.VMEM)
    return pl.pallas_call(
        body,
        out_shape=shapes,
        in_specs=[vmem] * len(args),
        out_specs=[vmem] * len(outs),
        scratch_shapes=scratch_shapes,
        compiler_params=pltpu.CompilerParams(vmem_limit_bytes=24 * 1024 * 1024),
    )(*args)


def swaps(count):
    pair = [(i, i ^ 1) for i in range(count)]
    other = [(i, (i + 1 if i % 2 else i - 1) % count) for i in range(count)]
    return pair, other


def shards(gradient, right_side):
    (_, nx), (_, nq) = places()
    ny, ring = lax.axis_size("gy"), ("gy", "gz")
    rows_x, back_x, along_y, lanes = [jnp.asarray(t) for t in tables()]
    group, line, box = (nx, ROWS, LANES), (nq, ROWS, LANES), (ROWS, LANES)
    tile, state, two, shape = (8, LANES), (4 * ROWS + 8, LANES), (2 * ROWS, LANES), right_side.shape
    between = [(0, 1), (1, 0)]

    def exchange_all(sent):
        near = lax.all_to_all(sent, "gx", 0, 0)
        (sent,) = call(middle_kernel, [line], near)
        return lax.all_to_all(sent, ring, 0, 0)

    def exchange_near(sent):
        pair, other = [lax.ppermute(sent, "gx", s) for s in swaps(nx)]
        (sent,) = call(x_kernel, [box], sent, pair, other)
        pair, other = [lax.ppermute(sent, ring, s) for s in swaps(nq)]
        return sent, pair, other

    (packed,) = call(pack_kernel, [(3, 16, 32, LANES)], gradient)
    packed = lax.ppermute(packed, "gz", between)
    mine, theirs = call(start_kernel, [box, box], right_side)
    theirs = lax.ppermute(theirs, "gz", between)
    (size,) = call(size_kernel, [tile], gradient)
    far = lax.ppermute(size, "gy", [(i, (i + ny // 2) % ny) for i in range(ny)])
    (sent,) = call(x_first_kernel, [box], mine, theirs, size, far)
    near = exchange_near(sent)
    (gradient,) = call(unpack_kernel, [gradient.shape], gradient, packed)
    operands = (gradient, rows_x, back_x, along_y, lanes)

    def slow(first):
        (sent,) = call(slow_kernel, [group], first, *operands, scratch=True)
        old = first
        for number in range(ITERS - 1):
            body = functools.partial(step_kernel, number)
            sent, old = call(body, [group, state], exchange_all(sent), old, *operands, scratch=True)
        return call(last_kernel, [two], exchange_all(sent), old)[0]

    vectors = []
    for number in range(6):
        if number:
            near = exchange_near(sent)
        outs = [group if number == 5 else box, box] + [[], [], [], [box], [], [tile]][number]
        body = functools.partial(basis_kernel, number)
        sent, vector, *extra = call(body, outs, *near, *vectors, *operands, scratch=True)
        if number == 3:
            vectors[2] = extra[0]
        vectors.append(vector)
    both, good = call(fast_kernel, [two, tile], exchange_all(sent), *vectors, extra[0])
    both = lax.cond(good[0, 0] > 0.5, lambda first: both, slow, vectors[0])
    return tuple(call(finish_kernel, [shape, shape], both, lax.ppermute(both, "gz", between)))


def solution(mesh):
    placed = P(None, "gz", "gx", "gy")
    return jax.shard_map(
        shards,
        mesh=mesh,
        in_specs=(placed, placed),
        out_specs=(placed, placed),
        check_vma=False,
    )
```

```python
import functools

import jax
import jax.numpy as jnp
import ml_dtypes
import numpy as np
from jax import lax
from jax.experimental import pallas as pl
from jax.experimental.pallas import tpu as pltpu
from jax.sharding import PartitionSpec as P

ITERS = 6
SMOOTHING = 0.5
DAMPING = 0.05
HIGHEST = lax.Precision.HIGHEST

CELLS_Z, CELLS_X, CELLS_Y = 4, 4, 16
BOX_X, BOX_Y, BOX_Z = 7, 19, 6
LANES = 128
ROWS = 24
DENOMINATOR = 3072.0
SCALE = 512.0
DAMP = DAMPING / SCALE
SHIFTS = (0.0, 0.171, 0.452, 0.776, 0.114)
WORST_PIVOT = 0.05


def numerators(t):
    return (
        (8 - t) ** 3,
        3 * t**3 - 48 * t**2 + 2048,
        -3 * t**3 + 24 * t**2 + 192 * t + 512,
        t**3,
    )


WEIGHTS = [[n / DENOMINATOR for n in numerators(t)] for t in range(8)]


def basis(cells):
    table = np.zeros((8 * cells + 1, cells + 3 + 1))
    for voxel in range(8 * cells + 1):
        for k, n in enumerate(numerators(voxel % 8)):
            table[voxel, voxel // 8 + k] = n
    return table[:, :-1]


def mass_and_edges(cells, first, last):
    table = basis(cells) / DENOMINATOR
    own = table[:-1]
    steps = table[1:] - table[:-1]
    if last:
        steps[-1] = -table[-2]
    edges = steps.T @ steps
    if first:
        edges = edges + np.outer(table[0], table[0])
    return own.T @ own, edges


def place_z(matrix, part):
    return matrix[1:7, 1:7] if part == 0 else matrix[0:6, 0:6]


@functools.lru_cache(None)
def tables():
    bx = basis(CELLS_X)[:-1]
    expand = np.zeros((96, ROWS))
    for c in range(3):
        expand[c * 32 : c * 32 + 32, c * 8 : c * 8 + BOX_X] = bx / DENOMINATOR / DENOMINATOR
    rows_x = np.zeros((3, 144, ROWS), np.float32)
    for kind in range(3):
        mass, edges = mass_and_edges(CELLS_X, kind == 0, kind == 2)
        rows_x[kind, :96] = expand
        for c in range(3):
            at = slice(c * 8, c * 8 + BOX_X)
            rows_x[kind, 96 + c * 8 : 96 + c * 8 + BOX_X, at] = SMOOTHING / SCALE * mass
            rows_x[kind, 120 + c * 8 : 120 + c * 8 + BOX_X, at] = SMOOTHING / SCALE * edges
    by = basis(CELLS_Y)[:-1]
    along_y = np.zeros((2, 2, LANES, 7 * LANES))
    for part in range(2):
        for f in range(BOX_Z):
            g = f + 1 if part == 0 else f
            low = by.T.astype(ml_dtypes.bfloat16).astype(np.float64)
            at = slice(f * BOX_Y, (f + 1) * BOX_Y)
            along_y[part, 0, at, g * LANES : (g + 1) * LANES] = low
            along_y[part, 1, at, g * LANES : (g + 1) * LANES] = by.T - low
    along_y = along_y.reshape(2, 256, 7 * LANES).astype(ml_dtypes.bfloat16)
    lanes = np.zeros((2, 3, 256, LANES), np.float32)
    for part in range(2):
        mz, kz = mass_and_edges(CELLS_Z, part == 0, part == 1)
        mz, kz = place_z(mz, part), place_z(kz, part)
        for kind in range(3):
            my, ky = mass_and_edges(CELLS_Y, kind == 0, kind == 2)
            used = BOX_Z * BOX_Y
            lanes[part, kind, :used, :used] = np.kron(kz, my) + np.kron(mz, ky)
            lanes[part, kind, 128 : 128 + used, :used] = np.kron(mz, my)
    return (
        rows_x,
        (expand.T / SCALE).astype(np.float32),
        along_y,
        lanes.reshape(6, 256, LANES),
    )


def iotas():
    row = lax.broadcasted_iota(jnp.int32, (ROWS, LANES), 0)
    lane = lax.broadcasted_iota(jnp.int32, (ROWS, LANES), 1)
    f = jnp.zeros_like(lane)
    for k in range(1, BOX_Z + 1):
        f = f + (lane >= k * BOX_Y).astype(jnp.int32)
    return row & 7, f, lane - f * BOX_Y


def masks(where):
    (gx, nx), (gy, ny), (gz, nz) = where
    kx, f, e = iotas()
    low_x, high_x = jnp.where(gx == 0, 1, 0), jnp.where(gx == nx - 1, 4, 6)
    low_y, high_y = jnp.where(gy == 0, 1, 0), jnp.where(gy == ny - 1, 16, 18)
    high_z = jnp.where(gz == 0, 5, 4)
    inside = (kx >= low_x) & (kx <= high_x) & (e >= low_y) & (e <= high_y) & (f <= high_z)
    own_z = jnp.where(gz == 0, 0, 1)
    own = (kx >= 1) & (kx <= 4) & (e >= 1) & (e <= 16) & (f >= own_z) & (f <= own_z + 3)
    return inside.astype(jnp.float32), own.astype(jnp.float32)


def places():
    return tuple((lax.axis_index(a), lax.axis_size(a)) for a in ("gx", "gy", "gz"))


def add(a, b):
    return b if a is None else a if b is None else a + b


def split3(value):
    high = value.astype(jnp.bfloat16)
    rest = value - high.astype(jnp.float32)
    middle = rest.astype(jnp.bfloat16)
    low = (rest - middle.astype(jnp.float32)).astype(jnp.bfloat16)
    return jnp.concatenate([high, middle, low], axis=0)


def dot(a, b, dims=((1,), (0,)), precision=None):
    return lax.dot_general(
        a, b, (dims, ((), ())), precision=precision, preferred_element_type=jnp.float32
    )


def kind_of(index, count):
    return jnp.where(index == 0, 0, jnp.where(index == count - 1, 2, 1))


def apply_local(vector, grad_ref, rows_ref, back_ref, along_ref, lanes_ref, field_ref, sums_ref):
    first = dot(rows_ref[...], vector, precision=HIGHEST)
    pieces = split3(first[:96])
    field = dot(jnp.concatenate([pieces, pieces], axis=1), along_ref[...])
    field_ref[...] = field[:96] + field[96:192] + field[192:]

    def column(cx, carry):
        rows = [pl.ds(pl.multiple_of(c * 32 + cx * 8, 8), 8) for c in range(3)]
        inside = pl.ds(pl.multiple_of(cx * 8, 8), 8)
        total = [[None] * 4 for _ in range(3)]
        for cz in range(CELLS_Z):
            layer = [
                [field_ref[rows[c], (cz + k) * LANES : (cz + k + 1) * LANES] for k in range(4)]
                for c in range(3)
            ]

            def weighted(t, values):
                slope = [grad_ref[c, cz * 8 + t, inside, :] for c in range(3)]
                shade = slope[0] * values[0] + slope[1] * values[1] + slope[2] * values[2]
                return [slope[c] * shade for c in range(3)]

            edge, near = WEIGHTS[0][0], WEIGHTS[0][1]
            value = weighted(0, [edge * (v[0] + v[2]) + near * v[1] for v in layer])
            first = [edge * v for v in value]
            second = [near * v for v in value]
            outer = [v[0] + v[3] for v in layer]
            inner = [v[1] + v[2] for v in layer]
            outer_odd = [v[0] - v[3] for v in layer]
            inner_odd = [v[1] - v[2] for v in layer]
            edge, near = WEIGHTS[4][0], WEIGHTS[4][1]
            value = weighted(4, [edge * a + near * b for a, b in zip(outer, inner)])
            sums = [[edge * v, near * v, None, None] for v in value]
            for t in (1, 2, 3):
                w = WEIGHTS[t]
                a, b, p, q = (w[0] + w[3]) / 2, (w[1] + w[2]) / 2, (w[0] - w[3]) / 2, (w[1] - w[2]) / 2
                even = [a * outer[c] + b * inner[c] for c in range(3)]
                odd = [p * outer_odd[c] + q * inner_odd[c] for c in range(3)]
                one = weighted(t, [even[c] + odd[c] for c in range(3)])
                two = weighted(8 - t, [even[c] - odd[c] for c in range(3)])
                for c in range(3):
                    plus, minus = one[c] + two[c], one[c] - two[c]
                    terms = (a * plus, b * plus, p * minus, q * minus)
                    sums[c] = [add(x, y) for x, y in zip(sums[c], terms)]
            for c in range(3):
                outside, middle, outside_odd, middle_odd = sums[c]
                parts = (
                    outside + outside_odd + first[c],
                    middle + middle_odd + second[c],
                    middle - middle_odd + first[c],
                    outside - outside_odd,
                )
                total[c] = [add(x, y) for x, y in zip(total[c], parts)]
                sums_ref[rows[c], cz * LANES : (cz + 1) * LANES] = total[c][0]
                total[c] = total[c][1:] + [None]
        for c in range(3):
            for k in range(3):
                g = CELLS_Z + k
                sums_ref[rows[c], g * LANES : (g + 1) * LANES] = total[c][k]
        return carry

    lax.fori_loop(0, CELLS_X, column, 0, unroll=True)
    pieces = split3(sums_ref[...])
    back = dot(pieces, along_ref[...], ((1,), (1,)))
    back = back[:, :LANES] + back[:, LANES:]
    back = back[:96] + back[96:192] + back[192:]
    data = dot(back_ref[...], back, precision=HIGHEST)
    relief = dot(
        jnp.concatenate([first[96:120], first[120:144]], axis=1),
        lanes_ref[...],
        precision=HIGHEST,
    )
    return data + relief


def roll(value, shift, axis):
    return pltpu.roll(value, shift, axis)


def put():
    first_f = jnp.where(lax.axis_index("gz") == 0, 0, 1)
    row = lax.broadcasted_iota(jnp.int32, (64, LANES), 0)
    lane = lax.broadcasted_iota(jnp.int32, (64, LANES), 1)
    target = ((row >> 4) + first_f) * BOX_Y + 1 + (row & 15)
    return (lane == target).astype(jnp.float32).astype(jnp.bfloat16)


def start_kernel(right_ref, out_ref):
    parts = []
    for c in range(3):
        own = jnp.concatenate([right_ref[c, z] for z in range(CELLS_Z)], axis=1)
        parts += [jnp.zeros((1, 64), jnp.float32), own, jnp.zeros((3, 64), jnp.float32)]
    value = dot(split3(jnp.concatenate(parts, axis=0)), put())
    out_ref[...] = value[:ROWS] + value[ROWS : 2 * ROWS] + value[2 * ROWS :]


def size_kernel(grad_ref, out_ref):
    def plane(z, totals):
        totals = list(totals)
        for x in range(4):
            slope = [grad_ref[c, z, x * 8 : x * 8 + 8, :] for c in range(3)]
            k = 0
            for a in range(3):
                for b in range(a, 3):
                    totals[k] = totals[k] + slope[a] * slope[b]
                    k += 1
        return tuple(totals)

    zero = jnp.zeros((8, LANES), jnp.float32)
    totals = lax.fori_loop(0, 32, plane, (zero,) * 6)
    count = 32.0 * 32.0 * 128.0
    xx, xy, xz, yy, yz, zz = [
        jnp.sum(jnp.sum(t, axis=0, keepdims=True), axis=1, keepdims=True) / count for t in totals
    ]
    aa = xx * xx + xy * xy + xz * xz
    bb = xy * xy + yy * yy + yz * yz
    cc = xz * xz + yz * yz + zz * zz
    ab = xx * xy + xy * yy + xz * yz
    ac = xx * xz + xy * yz + xz * zz
    bc = xy * xz + yy * yz + yz * zz
    norm = aa * aa + bb * bb + cc * cc + 2.0 * (ab * ab + ac * ac + bc * bc)
    size = 0.73 * jnp.sqrt(jnp.sqrt(norm)) + 0.04
    row = lax.broadcasted_iota(jnp.int32, (8, LANES), 0)
    out_ref[...] = jnp.where(row == 7, jnp.broadcast_to(size, (8, LANES)), 0.0)


def with_size(value, *others):
    row = lax.broadcasted_iota(jnp.int32, (ROWS, LANES), 0)
    return jnp.where(row == 7, functools.reduce(jnp.maximum, others), value)


def pair_sides(index, pair, other):
    even = lax.rem(index, 2) == 0
    return jnp.where(even, other, pair), jnp.where(even, pair, other)


def z_kernel(mine_ref, swap_ref, out_ref):
    gz = lax.axis_index("gz")
    _, f, _ = iotas()
    mine, swap = mine_ref[...], swap_ref[...]
    other = roll(swap, jnp.where(gz == 0, 3 * BOX_Y, LANES - 3 * BOX_Y), 1)
    first_f = jnp.where(gz == 0, 3, 0)
    value = mine + jnp.where((f >= first_f) & (f <= first_f + 2), other, 0.0)
    out_ref[...] = with_size(value, mine, swap)


def x_kernel(mine_ref, pair_ref, other_ref, *rest):
    out_ref = rest[-1]
    gx, nx = lax.axis_index("gx"), lax.axis_size("gx")
    kx, _, _ = iotas()
    mine, pair, other = mine_ref[...], pair_ref[...], other_ref[...]
    low, high = pair_sides(gx, pair, other)
    first_x, last_x = jnp.where(gx > 0, 2, -1), jnp.where(gx < nx - 1, 4, 8)
    value = mine + jnp.where(kx <= first_x, rows_rolled(low, 4), 0.0)
    value = value + jnp.where((kx >= last_x) & (kx <= 6), rows_rolled(high, 4), 0.0)
    out_ref[...] = with_size(value, mine, pair, other)


def x_first_kernel(mine_ref, size_ref, out_ref):
    out_ref[...] = mine_ref[...]
    row = lax.broadcasted_iota(jnp.int32, (8, LANES), 0)
    out_ref[0:8] = jnp.where(row == 7, size_ref[...], mine_ref[0:8])


def y_sum(mine_ref, pair_ref, other_ref):
    gy, ny = lax.axis_index("gy"), lax.axis_size("gy")
    _, _, e = iotas()
    mine, pair, other = mine_ref[...], pair_ref[...], other_ref[...]
    low, high = pair_sides(gy, pair, other)
    first_y, last_y = jnp.where(gy > 0, 2, -1), jnp.where(gy < ny - 1, 16, LANES)
    value = mine + jnp.where(e <= first_y, roll(low, LANES - 16, 1), 0.0)
    value = value + jnp.where(e >= last_y, roll(high, 16, 1), 0.0)
    return value, jnp.maximum(jnp.maximum(mine, pair), other)[7:8]


def rows_rolled(value, shift):
    return jnp.concatenate(
        [roll(value[c * 8 : c * 8 + 8], shift, 0) for c in range(3)], axis=0
    )


def middle_kernel(in_ref, out_ref):
    (gx, nx), _, (gz, nz) = places()
    kx, f, e = iotas()
    has_low = (gx > 0).astype(jnp.int32)
    has_high = (gx < nx - 1).astype(jnp.int32)
    low = jnp.maximum(gx - 1, 0)
    high = jnp.minimum(gx + 1, nx - 1)
    take_low = (kx <= 2) & (has_low == 1)
    take_high = (kx >= 4) & (kx <= 6) & (has_high == 1)

    def along_x(part):
        value = in_ref[gx * nz + part]
        below = rows_rolled(in_ref[low * nz + part], 4)
        above = rows_rolled(in_ref[high * nz + part], 4)
        value = value + jnp.where(take_low, below, 0.0)
        return value + jnp.where(take_high, above, 0.0)

    mine = along_x(gz)
    other = along_x(1 - gz)
    other = roll(other, jnp.where(gz == 0, 3 * BOX_Y, LANES - 3 * BOX_Y), 1)
    first_f = jnp.where(gz == 0, 3, 0)
    value = mine + jnp.where((f >= first_f) & (f <= first_f + 2), other, 0.0)
    everything = in_ref[0]
    for i in range(1, in_ref.shape[0]):
        everything = everything + in_ref[i]
    value = jnp.where(kx == 7, everything, value)
    for i in range(out_ref.shape[0]):
        out_ref[i] = value


def along_y_sum(in_ref):
    _, (gy, ny), _ = places()
    kx, f, e = iotas()
    has_low = (gy > 0).astype(jnp.int32)
    has_high = (gy < ny - 1).astype(jnp.int32)
    below = roll(in_ref[jnp.maximum(gy - 1, 0)], LANES - 16, 1)
    above = roll(in_ref[jnp.minimum(gy + 1, ny - 1)], 16, 1)
    value = in_ref[gy]
    value = value + jnp.where((e <= 2) & (has_low == 1), below, 0.0)
    value = value + jnp.where((e >= 16) & (has_high == 1), above, 0.0)
    everything = in_ref[0]
    for i in range(1, in_ref.shape[0]):
        everything = everything + in_ref[i]
    return value, everything


def message(vector, image, own, out_ref):
    norm = jnp.sum(own * vector * vector, axis=0, keepdims=True)
    product = jnp.sum(vector * image, axis=0, keepdims=True)
    row = lax.broadcasted_iota(jnp.int32, (ROWS, LANES), 0)
    value = jnp.where(row == 7, norm, image)
    value = jnp.where(row == 15, product, value)
    for i in range(out_ref.shape[0]):
        out_ref[i] = value


def z_last_kernel(mine_ref, swap_ref, out_ref):
    z_kernel(mine_ref, swap_ref, out_ref.at[0])
    out_ref[0, 7:8] = mine_ref[7:8] + swap_ref[7:8]
    value = out_ref[0]
    for i in range(1, out_ref.shape[0]):
        out_ref[i] = value


def total_of(in_ref):
    total = in_ref[0]
    for i in range(1, in_ref.shape[0]):
        total = total + in_ref[i]
    return total


def x_last_kernel(in_ref, out_ref):
    gx, nx = lax.axis_index("gx"), lax.axis_size("gx")
    kx, _, _ = iotas()
    first_x, last_x = jnp.where(gx > 0, 2, -1), jnp.where(gx < nx - 1, 4, 8)
    low, high = in_ref[jnp.maximum(gx - 1, 0)], in_ref[jnp.minimum(gx + 1, nx - 1)]
    value = in_ref[gx] + jnp.where(kx <= first_x, rows_rolled(low, 4), 0.0)
    value = value + jnp.where((kx >= last_x) & (kx <= 6), rows_rolled(high, 4), 0.0)
    value = jnp.where(kx == 7, total_of(in_ref), value)
    for i in range(out_ref.shape[0]):
        out_ref[i] = value


def basis_kernel(number, mine_ref, pair_ref, other_ref, *refs):
    past = refs[:number]
    operands = refs[number : number + 5]
    out_ref, *new_refs, field_ref, sums_ref = refs[number + 5 :]
    inside, own = masks(places())
    value, size = y_sum(mine_ref, pair_ref, other_ref)
    value = value * inside
    if number:
        value = value + DAMP * past[-1][...]
    if number == 3:
        inverse = 1.0 / size
        one, two = past[1][...], past[2][...]
        second = inverse * two - SHIFTS[1] * one
        value = inverse * (inverse * value - SHIFTS[1] * two) - SHIFTS[2] * second
        new_refs[1][...] = second
    elif number > 3:
        value = value / size - SHIFTS[number - 1] * past[-1][...]
    new_refs[0][...] = value
    image = apply_local(value, *operands, field_ref, sums_ref) * inside
    if number < 5:
        out_ref[...] = with_size(image, jnp.broadcast_to(size, (ROWS, LANES)))
        return
    new_refs[1][...] = jnp.broadcast_to(size, (8, LANES))
    vectors = [ref[...] for ref in past] + [value]
    products = []
    for i in range(6):
        mine = own * vectors[i]
        for j in range(i, 6):
            products.append(mine * vectors[j])
    products.append(value * image + DAMP * own * value * value)
    sums = [jnp.sum(p, axis=0, keepdims=True) for p in products]
    sums = jnp.concatenate(sums + [jnp.zeros((2, LANES), jnp.float32)], axis=0)
    sums = jnp.sum(sums, axis=1, keepdims=True)
    row = lax.broadcasted_iota(jnp.int32, (ROWS, LANES), 0)
    lane = lax.broadcasted_iota(jnp.int32, (ROWS, LANES), 1)
    line = jnp.sum(jnp.where(row == lane, sums, 0.0), axis=0, keepdims=True)
    image = jnp.where(row == 7, line, image)
    out_ref[...] = image


def times(a, b):
    return None if a is None or b is None else a * b


def form(left, table, right):
    total = None
    for i, a in enumerate(left):
        inner = None
        for j, b in enumerate(right):
            inner = add(inner, times(table[i][j], b))
        total = add(total, times(a, inner))
    return total


def fast_kernel(in_ref, *refs):
    vectors = [ref[...] for ref in refs[:6]]
    size_ref, solution_ref, residual_ref, good_ref = refs[6:]
    inside, _ = masks(places())
    value, everything = along_y_sum(in_ref)
    size = size_ref[0:1, 0:1]
    inverse = 1.0 / size
    image = (value * inside + DAMP * vectors[5]) * inverse
    line = everything[7:8]
    lane = lax.broadcasted_iota(jnp.int32, (1, LANES), 1)
    scalars = [jnp.sum(jnp.where(lane == k, line, 0.0), axis=1, keepdims=True) for k in range(22)]
    gram = [[None] * 6 for _ in range(6)]
    k = 0
    for i in range(6):
        for j in range(i, 6):
            gram[i][j] = gram[j][i] = scalars[k]
            k += 1
    factor = [inverse] + [jnp.ones_like(inverse)] * 4
    energy = [[None] * 6 for _ in range(6)]
    for i in range(5):
        for j in range(i, 6):
            energy[i][j] = energy[j][i] = factor[i] * (gram[i + 1][j] + SHIFTS[i] * gram[i][j])
    energy[5][5] = scalars[21] * inverse
    rest = [row[:] for row in gram]
    good = jnp.ones_like(inverse)
    for k in range(6):
        good = jnp.where(rest[k][k] / gram[k][k] > WORST_PIVOT, good, 0.0)
        for i in range(k + 1, 6):
            ratio = rest[i][k] / rest[k][k]
            for j in range(i, 6):
                rest[i][j] = rest[i][j] - ratio * rest[k][j]
                rest[j][i] = rest[i][j]
    good_ref[0, 0] = jnp.sum(good).astype(jnp.int32)
    solved = [None] * 7
    residual = [jnp.ones_like(inverse)] + [None] * 6
    direction = residual[:]
    norm = gram[0][0]
    for number in range(ITERS):
        known = number + 1
        moved = [None] * 7
        for j in range(known):
            if j == 5:
                moved[6] = add(moved[6], direction[5])
            else:
                part = factor[j] * direction[j]
                moved[j + 1] = add(moved[j + 1], part)
                moved[j] = add(moved[j], SHIFTS[j] * part)
        step = norm / form(direction[:known], energy, direction[:known])
        solved = [add(a, times(step, b)) for a, b in zip(solved, direction)]
        residual = [add(a, times(-step, b)) for a, b in zip(residual, moved)]
        if number < ITERS - 1:
            known += 1
            later = form(residual[:known], gram, residual[:known])
            ratio = later / norm
            direction = [add(a, times(ratio, b)) for a, b in zip(residual, direction)]
            norm = later
    vectors = vectors + [image]
    first, second = None, None
    for j in range(7):
        if solved[j] is not None:
            first = add(first, solved[j] * vectors[j])
        second = add(second, residual[j] * vectors[j])
    write_out(first * (inverse / SCALE), second, solution_ref, residual_ref)


def write_out(solved, residual, solution_ref, residual_ref):
    both = jnp.concatenate([solved, residual], axis=0)
    value = dot(split3(both), put(), ((1,), (1,)))
    value = value[:48] + value[48:96] + value[96:]
    for z in range(CELLS_Z):
        for c in range(3):
            solution_ref[c, z] = value[c * 8 + 1 : c * 8 + 5, z * 16 : z * 16 + 16]
            residual_ref[c, z] = value[ROWS + c * 8 + 1 : ROWS + c * 8 + 5, z * 16 : z * 16 + 16]


def slow_kernel(vector_ref, grad_ref, rows_ref, back_ref, along_ref, lanes_ref, out_ref, field_ref, sums_ref):
    inside, own = masks(places())
    vector = vector_ref[...]
    image = apply_local(vector, grad_ref, rows_ref, back_ref, along_ref, lanes_ref, field_ref, sums_ref)
    message(vector, image * inside, own, out_ref)


def update(in_ref, old_ref, number):
    inside, own = masks(places())
    value, everything = along_y_sum(in_ref)
    residual = old_ref[ROWS : 2 * ROWS] if number else old_ref[...]
    image = value * inside + DAMP * residual
    norm = jnp.sum(everything[7:8], axis=1, keepdims=True)
    product = jnp.sum(everything[15:16], axis=1, keepdims=True) + DAMP * norm
    if number:
        ratio = norm / old_ref[4 * ROWS : 4 * ROWS + 1, 0:1]
        step = norm / (product - ratio * norm / old_ref[4 * ROWS + 1 : 4 * ROWS + 2, 0:1])
        direction = residual + ratio * old_ref[2 * ROWS : 3 * ROWS]
        image = image + ratio * old_ref[3 * ROWS : 4 * ROWS]
        solved = old_ref[0:ROWS] + step * direction
    else:
        step = norm / product
        direction = residual
        solved = step * direction
    residual = residual - step * image
    return own, inside, solved, residual, direction, image, norm, step


def step_kernel(number, in_ref, old_ref, grad_ref, rows_ref, back_ref, along_ref, lanes_ref, out_ref, new_ref, field_ref, sums_ref):
    own, inside, solved, residual, direction, image, norm, step = update(in_ref, old_ref, number)
    new_ref[0:ROWS] = solved
    new_ref[ROWS : 2 * ROWS] = residual
    new_ref[2 * ROWS : 3 * ROWS] = direction
    new_ref[3 * ROWS : 4 * ROWS] = image
    row = lax.broadcasted_iota(jnp.int32, (8, LANES), 0)
    new_ref[4 * ROWS : 4 * ROWS + 8] = jnp.where(row == 0, norm, step)
    image = apply_local(residual, grad_ref, rows_ref, back_ref, along_ref, lanes_ref, field_ref, sums_ref)
    message(residual, image * inside, own, out_ref)


def last_kernel(in_ref, old_ref, solution_ref, residual_ref):
    _, _, solved, residual, _, _, _, _ = update(in_ref, old_ref, ITERS - 1)
    write_out(solved / SCALE, residual, solution_ref, residual_ref)


def call(body, outs, *args, scratch=False):
    shapes = [
        jax.ShapeDtypeStruct(s, jnp.float32) if s else jax.ShapeDtypeStruct((1, 1), jnp.int32)
        for s in outs
    ]
    scratch_shapes = [pltpu.VMEM((96, 7 * LANES), jnp.float32)] * 2 if scratch else []
    vmem = pl.BlockSpec(memory_space=pltpu.VMEM)
    return pl.pallas_call(
        body,
        out_shape=shapes,
        in_specs=[vmem] * len(args),
        out_specs=[vmem if s else pl.BlockSpec(memory_space=pltpu.SMEM) for s in outs],
        scratch_shapes=scratch_shapes,
        compiler_params=pltpu.CompilerParams(vmem_limit_bytes=24 * 1024 * 1024),
    )(*args)


def swaps(axis):
    count = lax.axis_size(axis)
    pair = [(i, i ^ 1) for i in range(count)]
    other = [(i, (i + 1 if i % 2 else i - 1) % count) for i in range(count)]
    return pair, other


def shards(gradient, right_side):
    (gx, nx), (gy, ny), (gz, nz) = places()
    rows_x, back_x, along_y, lanes = [jnp.asarray(t) for t in tables()]
    rows_x = lax.dynamic_index_in_dim(rows_x, kind_of(gx, nx), 0, keepdims=False)
    along_y = lax.dynamic_index_in_dim(along_y, gz, 0, keepdims=False)
    lanes = lax.dynamic_index_in_dim(lanes, gz * 3 + kind_of(gy, ny), 0, keepdims=False)
    operands = (gradient, rows_x, back_x, along_y, lanes)
    group, line, box = (nx * nz, ROWS, LANES), (ny, ROWS, LANES), (ROWS, LANES)
    tile, state, shape = (8, LANES), (4 * ROWS + 8, LANES), right_side.shape

    def exchange_all(sent):
        near = lax.all_to_all(sent, ("gx", "gz"), 0, 0)
        (sent,) = call(middle_kernel, [line], near)
        return lax.all_to_all(sent, "gy", 0, 0)

    def exchange_near(sent, size=None):
        swapped = lax.ppermute(sent, "gz", swaps("gz")[0])
        (sent,) = call(z_kernel, [box], sent, swapped)
        if size is not None:
            (sent,) = call(x_first_kernel, [box], sent, size)
        pair, other = [lax.ppermute(sent, "gx", s) for s in swaps("gx")]
        (sent,) = call(x_kernel, [box], sent, pair, other)
        pair, other = swaps("gy")
        other = lax.ppermute(sent, "gy", other)
        pair = lax.ppermute(sent, "gy", pair)
        return sent, pair, other

    def exchange_last(sent):
        swapped = lax.ppermute(sent, "gz", swaps("gz")[0])
        (sent,) = call(z_last_kernel, [(nx, ROWS, LANES)], sent, swapped)
        (sent,) = call(x_last_kernel, [line], lax.all_to_all(sent, "gx", 0, 0))
        return lax.all_to_all(sent, "gy", 0, 0)

    def slow(first):
        (sent,) = call(slow_kernel, [group], first, *operands, scratch=True)
        old = first
        for number in range(ITERS - 1):
            body = functools.partial(step_kernel, number)
            sent, old = call(body, [group, state], exchange_all(sent), old, *operands, scratch=True)
        return tuple(call(last_kernel, [shape, shape], exchange_all(sent), old))

    (sent,) = call(start_kernel, [box], right_side)
    (size,) = call(size_kernel, [tile], gradient)
    vectors = []
    for number in range(6):
        near = exchange_near(sent, size if number == 0 else None)
        outs = [box, box] + [[], [], [], [box], [], [tile]][number]
        body = functools.partial(basis_kernel, number)
        sent, vector, *extra = call(body, outs, *near, *vectors, *operands, scratch=True)
        if number == 3:
            vectors[2] = extra[0]
        vectors.append(vector)
    *fast, good = call(fast_kernel, [shape, shape, None], exchange_last(sent), *vectors, extra[0])
    return lax.cond(good[0, 0] > 0, lambda first: tuple(fast), slow, vectors[0])


def solution(mesh):
    placed = P(None, "gz", "gx", "gy")
    return jax.shard_map(
        shards,
        mesh=mesh,
        in_specs=(placed, placed),
        out_specs=(placed, placed),
        check_vma=False,
    )
```

```python
import functools

import jax
import jax.numpy as jnp
import ml_dtypes
import numpy as np
from jax import lax
from jax.experimental import pallas as pl
from jax.experimental.pallas import tpu as pltpu
from jax.sharding import PartitionSpec as P

ITERS = 6
SMOOTHING = 0.5
DAMPING = 0.05
HIGHEST = lax.Precision.HIGHEST

CELLS_Z, CELLS_X, CELLS_Y = 4, 4, 16
BOX_X, BOX_Y, BOX_Z = 7, 19, 6
LANES = 128
ROWS = 24
DENOMINATOR = 3072.0
SCALE = 512.0
DAMP = DAMPING / SCALE
SHIFTS = (0.0, 0.171, 0.452, 0.776, 0.114)
WORST_PIVOT = 0.05


def numerators(t):
    return (
        (8 - t) ** 3,
        3 * t**3 - 48 * t**2 + 2048,
        -3 * t**3 + 24 * t**2 + 192 * t + 512,
        t**3,
    )


WEIGHTS = [[n / DENOMINATOR for n in numerators(t)] for t in range(8)]


def basis(cells):
    table = np.zeros((8 * cells + 1, cells + 3 + 1))
    for voxel in range(8 * cells + 1):
        for k, n in enumerate(numerators(voxel % 8)):
            table[voxel, voxel // 8 + k] = n
    return table[:, :-1]


def mass_and_edges(cells, first, last):
    table = basis(cells) / DENOMINATOR
    own = table[:-1]
    steps = table[1:] - table[:-1]
    if last:
        steps[-1] = -table[-2]
    edges = steps.T @ steps
    if first:
        edges = edges + np.outer(table[0], table[0])
    return own.T @ own, edges


def place_z(matrix, part):
    return matrix[1:7, 1:7] if part == 0 else matrix[0:6, 0:6]


@functools.lru_cache(None)
def tables():
    bx = basis(CELLS_X)[:-1]
    expand = np.zeros((96, ROWS))
    for c in range(3):
        expand[c * 32 : c * 32 + 32, c * 8 : c * 8 + BOX_X] = bx / DENOMINATOR / DENOMINATOR
    rows_x = np.zeros((3, 144, ROWS), np.float32)
    for kind in range(3):
        mass, edges = mass_and_edges(CELLS_X, kind == 0, kind == 2)
        rows_x[kind, :96] = expand
        for c in range(3):
            at = slice(c * 8, c * 8 + BOX_X)
            rows_x[kind, 96 + c * 8 : 96 + c * 8 + BOX_X, at] = SMOOTHING / SCALE * mass
            rows_x[kind, 120 + c * 8 : 120 + c * 8 + BOX_X, at] = SMOOTHING / SCALE * edges
    by = basis(CELLS_Y)[:-1]
    along_y = np.zeros((2, 2, LANES, 7 * LANES))
    for part in range(2):
        for f in range(BOX_Z):
            g = f + 1 if part == 0 else f
            low = by.T.astype(ml_dtypes.bfloat16).astype(np.float64)
            at = slice(f * BOX_Y, (f + 1) * BOX_Y)
            along_y[part, 0, at, g * LANES : (g + 1) * LANES] = low
            along_y[part, 1, at, g * LANES : (g + 1) * LANES] = by.T - low
    along_y = along_y.reshape(2, 256, 7 * LANES).astype(ml_dtypes.bfloat16)
    lanes = np.zeros((2, 3, 256, LANES), np.float32)
    for part in range(2):
        mz, kz = mass_and_edges(CELLS_Z, part == 0, part == 1)
        mz, kz = place_z(mz, part), place_z(kz, part)
        for kind in range(3):
            my, ky = mass_and_edges(CELLS_Y, kind == 0, kind == 2)
            used = BOX_Z * BOX_Y
            lanes[part, kind, :used, :used] = np.kron(kz, my) + np.kron(mz, ky)
            lanes[part, kind, 128 : 128 + used, :used] = np.kron(mz, my)
    return (
        rows_x,
        (expand.T / SCALE).astype(np.float32),
        along_y,
        lanes.reshape(6, 256, LANES),
    )


def iotas():
    row = lax.broadcasted_iota(jnp.int32, (ROWS, LANES), 0)
    lane = lax.broadcasted_iota(jnp.int32, (ROWS, LANES), 1)
    f = jnp.zeros_like(lane)
    for k in range(1, BOX_Z + 1):
        f = f + (lane >= k * BOX_Y).astype(jnp.int32)
    return row & 7, f, lane - f * BOX_Y


def masks(where):
    (gx, nx), (gy, ny), (gz, nz) = where
    kx, f, e = iotas()
    low_x, high_x = jnp.where(gx == 0, 1, 0), jnp.where(gx == nx - 1, 4, 6)
    low_y, high_y = jnp.where(gy == 0, 1, 0), jnp.where(gy == ny - 1, 16, 18)
    high_z = jnp.where(gz == 0, 5, 4)
    inside = (kx >= low_x) & (kx <= high_x) & (e >= low_y) & (e <= high_y) & (f <= high_z)
    own_z = jnp.where(gz == 0, 0, 1)
    own = (kx >= 1) & (kx <= 4) & (e >= 1) & (e <= 16) & (f >= own_z) & (f <= own_z + 3)
    return inside.astype(jnp.float32), own.astype(jnp.float32)


def places():
    return tuple((lax.axis_index(a), lax.axis_size(a)) for a in ("gx", "gy", "gz"))


def add(a, b):
    return b if a is None else a if b is None else a + b


def split3(value):
    high = value.astype(jnp.bfloat16)
    rest = value - high.astype(jnp.float32)
    middle = rest.astype(jnp.bfloat16)
    low = (rest - middle.astype(jnp.float32)).astype(jnp.bfloat16)
    return jnp.concatenate([high, middle, low], axis=0)


def dot(a, b, dims=((1,), (0,)), precision=None):
    return lax.dot_general(
        a, b, (dims, ((), ())), precision=precision, preferred_element_type=jnp.float32
    )


def kind_of(index, count):
    return jnp.where(index == 0, 0, jnp.where(index == count - 1, 2, 1))


def apply_local(vector, grad_ref, rows_ref, back_ref, along_ref, lanes_ref, field_ref, sums_ref):
    first = dot(rows_ref[...], vector, precision=HIGHEST)
    pieces = split3(first[:96])
    field = dot(jnp.concatenate([pieces, pieces], axis=1), along_ref[...])
    field_ref[...] = field[:96] + field[96:192] + field[192:]

    def column(cx, carry):
        rows = [pl.ds(pl.multiple_of(c * 32 + cx * 8, 8), 8) for c in range(3)]
        inside = pl.ds(pl.multiple_of(cx * 8, 8), 8)
        total = [[None] * 4 for _ in range(3)]
        for cz in range(CELLS_Z):
            layer = [
                [field_ref[rows[c], (cz + k) * LANES : (cz + k + 1) * LANES] for k in range(4)]
                for c in range(3)
            ]

            def weighted(t, values):
                slope = [grad_ref[c, cz * 8 + t, inside, :] for c in range(3)]
                shade = slope[0] * values[0] + slope[1] * values[1] + slope[2] * values[2]
                return [slope[c] * shade for c in range(3)]

            edge, near = WEIGHTS[0][0], WEIGHTS[0][1]
            value = weighted(0, [edge * (v[0] + v[2]) + near * v[1] for v in layer])
            first = [edge * v for v in value]
            second = [near * v for v in value]
            outer = [v[0] + v[3] for v in layer]
            inner = [v[1] + v[2] for v in layer]
            outer_odd = [v[0] - v[3] for v in layer]
            inner_odd = [v[1] - v[2] for v in layer]
            edge, near = WEIGHTS[4][0], WEIGHTS[4][1]
            value = weighted(4, [edge * a + near * b for a, b in zip(outer, inner)])
            sums = [[edge * v, near * v, None, None] for v in value]
            for t in (1, 2, 3):
                w = WEIGHTS[t]
                a, b, p, q = (w[0] + w[3]) / 2, (w[1] + w[2]) / 2, (w[0] - w[3]) / 2, (w[1] - w[2]) / 2
                even = [a * outer[c] + b * inner[c] for c in range(3)]
                odd = [p * outer_odd[c] + q * inner_odd[c] for c in range(3)]
                one = weighted(t, [even[c] + odd[c] for c in range(3)])
                two = weighted(8 - t, [even[c] - odd[c] for c in range(3)])
                for c in range(3):
                    plus, minus = one[c] + two[c], one[c] - two[c]
                    terms = (a * plus, b * plus, p * minus, q * minus)
                    sums[c] = [add(x, y) for x, y in zip(sums[c], terms)]
            for c in range(3):
                outside, middle, outside_odd, middle_odd = sums[c]
                parts = (
                    outside + outside_odd + first[c],
                    middle + middle_odd + second[c],
                    middle - middle_odd + first[c],
                    outside - outside_odd,
                )
                total[c] = [add(x, y) for x, y in zip(total[c], parts)]
                sums_ref[rows[c], cz * LANES : (cz + 1) * LANES] = total[c][0]
                total[c] = total[c][1:] + [None]
        for c in range(3):
            for k in range(3):
                g = CELLS_Z + k
                sums_ref[rows[c], g * LANES : (g + 1) * LANES] = total[c][k]
        return carry

    lax.fori_loop(0, CELLS_X, column, 0, unroll=True)
    pieces = split3(sums_ref[...])
    back = dot(pieces, along_ref[...], ((1,), (1,)))
    back = back[:, :LANES] + back[:, LANES:]
    back = back[:96] + back[96:192] + back[192:]
    data = dot(back_ref[...], back, precision=HIGHEST)
    relief = dot(
        jnp.concatenate([first[96:120], first[120:144]], axis=1),
        lanes_ref[...],
        precision=HIGHEST,
    )
    return data + relief


def roll(value, shift, axis):
    return pltpu.roll(value, shift, axis)


def put():
    first_f = jnp.where(lax.axis_index("gz") == 0, 0, 1)
    row = lax.broadcasted_iota(jnp.int32, (64, LANES), 0)
    lane = lax.broadcasted_iota(jnp.int32, (64, LANES), 1)
    target = ((row >> 4) + first_f) * BOX_Y + 1 + (row & 15)
    return (lane == target).astype(jnp.float32).astype(jnp.bfloat16)


def start_kernel(right_ref, out_ref):
    parts = []
    for c in range(3):
        own = jnp.concatenate([right_ref[c, z] for z in range(CELLS_Z)], axis=1)
        parts += [jnp.zeros((1, 64), jnp.float32), own, jnp.zeros((3, 64), jnp.float32)]
    value = dot(split3(jnp.concatenate(parts, axis=0)), put())
    out_ref[...] = value[:ROWS] + value[ROWS : 2 * ROWS] + value[2 * ROWS :]


def size_kernel(grad_ref, out_ref):
    def plane(z, totals):
        totals = list(totals)
        for x in range(4):
            slope = [grad_ref[c, z, 0, x * 8 : x * 8 + 8, :] for c in range(3)]
            k = 0
            for a in range(3):
                for b in range(a, 3):
                    totals[k] = totals[k] + slope[a] * slope[b]
                    k += 1
        return tuple(totals)

    zero = jnp.zeros((8, LANES), jnp.float32)
    totals = (zero,) * 6
    for z in range(8):
        totals = plane(z, totals)
    count = 8.0 * 32.0 * 128.0
    xx, xy, xz, yy, yz, zz = [
        jnp.sum(jnp.sum(t, axis=0, keepdims=True), axis=1, keepdims=True) / count for t in totals
    ]
    aa = xx * xx + xy * xy + xz * xz
    bb = xy * xy + yy * yy + yz * yz
    cc = xz * xz + yz * yz + zz * zz
    ab = xx * xy + xy * yy + xz * yz
    ac = xx * xz + xy * yz + xz * zz
    bc = xy * xz + yy * yz + yz * zz
    norm = aa * aa + bb * bb + cc * cc + 2.0 * (ab * ab + ac * ac + bc * bc)
    size = 0.73 * jnp.sqrt(jnp.sqrt(norm)) + 0.04
    row = lax.broadcasted_iota(jnp.int32, (8, LANES), 0)
    out_ref[...] = jnp.where(row == 7, jnp.broadcast_to(size, (8, LANES)), 0.0)


def with_size(value, *others):
    row = lax.broadcasted_iota(jnp.int32, (ROWS, LANES), 0)
    return jnp.where(row == 7, functools.reduce(jnp.maximum, others), value)


def pair_sides(index, pair, other):
    even = lax.rem(index, 2) == 0
    return jnp.where(even, other, pair), jnp.where(even, pair, other)


def z_kernel(mine_ref, swap_ref, out_ref):
    gz = lax.axis_index("gz")
    _, f, _ = iotas()
    mine, swap = mine_ref[...], swap_ref[...]
    other = roll(swap, jnp.where(gz == 0, 3 * BOX_Y, LANES - 3 * BOX_Y), 1)
    first_f = jnp.where(gz == 0, 3, 0)
    value = mine + jnp.where((f >= first_f) & (f <= first_f + 2), other, 0.0)
    out_ref[...] = with_size(value, mine, swap)


def x_kernel(mine_ref, pair_ref, other_ref, *rest):
    out_ref = rest[-1]
    gx, nx = lax.axis_index("gx"), lax.axis_size("gx")
    kx, _, _ = iotas()
    mine, pair, other = mine_ref[...], pair_ref[...], other_ref[...]
    low, high = pair_sides(gx, pair, other)
    first_x, last_x = jnp.where(gx > 0, 2, -1), jnp.where(gx < nx - 1, 4, 8)
    value = mine + jnp.where(kx <= first_x, rows_rolled(low, 4), 0.0)
    value = value + jnp.where((kx >= last_x) & (kx <= 6), rows_rolled(high, 4), 0.0)
    out_ref[...] = with_size(value, mine, pair, other)


def x_first_kernel(mine_ref, size_ref, out_ref):
    out_ref[...] = mine_ref[...]
    row = lax.broadcasted_iota(jnp.int32, (8, LANES), 0)
    out_ref[0:8] = jnp.where(row == 7, size_ref[...], mine_ref[0:8])


def y_sum(mine_ref, pair_ref, other_ref):
    gy, ny = lax.axis_index("gy"), lax.axis_size("gy")
    _, _, e = iotas()
    mine, pair, other = mine_ref[...], pair_ref[...], other_ref[...]
    low, high = pair_sides(gy, pair, other)
    first_y, last_y = jnp.where(gy > 0, 2, -1), jnp.where(gy < ny - 1, 16, LANES)
    value = mine + jnp.where(e <= first_y, roll(low, LANES - 16, 1), 0.0)
    value = value + jnp.where(e >= last_y, roll(high, 16, 1), 0.0)
    return value, jnp.maximum(jnp.maximum(mine, pair), other)[7:8]


def rows_rolled(value, shift):
    return jnp.concatenate(
        [roll(value[c * 8 : c * 8 + 8], shift, 0) for c in range(3)], axis=0
    )


def middle_kernel(in_ref, out_ref):
    (gx, nx), _, (gz, nz) = places()
    kx, f, e = iotas()
    has_low = (gx > 0).astype(jnp.int32)
    has_high = (gx < nx - 1).astype(jnp.int32)
    low = jnp.maximum(gx - 1, 0)
    high = jnp.minimum(gx + 1, nx - 1)
    take_low = (kx <= 2) & (has_low == 1)
    take_high = (kx >= 4) & (kx <= 6) & (has_high == 1)

    def along_x(part):
        value = in_ref[gx * nz + part]
        below = rows_rolled(in_ref[low * nz + part], 4)
        above = rows_rolled(in_ref[high * nz + part], 4)
        value = value + jnp.where(take_low, below, 0.0)
        return value + jnp.where(take_high, above, 0.0)

    mine = along_x(gz)
    other = along_x(1 - gz)
    other = roll(other, jnp.where(gz == 0, 3 * BOX_Y, LANES - 3 * BOX_Y), 1)
    first_f = jnp.where(gz == 0, 3, 0)
    value = mine + jnp.where((f >= first_f) & (f <= first_f + 2), other, 0.0)
    everything = in_ref[0]
    for i in range(1, in_ref.shape[0]):
        everything = everything + in_ref[i]
    value = jnp.where(kx == 7, everything, value)
    for i in range(out_ref.shape[0]):
        out_ref[i] = value


def along_y_sum(in_ref):
    _, (gy, ny), _ = places()
    kx, f, e = iotas()
    has_low = (gy > 0).astype(jnp.int32)
    has_high = (gy < ny - 1).astype(jnp.int32)
    below = roll(in_ref[jnp.maximum(gy - 1, 0)], LANES - 16, 1)
    above = roll(in_ref[jnp.minimum(gy + 1, ny - 1)], 16, 1)
    value = in_ref[gy]
    value = value + jnp.where((e <= 2) & (has_low == 1), below, 0.0)
    value = value + jnp.where((e >= 16) & (has_high == 1), above, 0.0)
    everything = in_ref[0]
    for i in range(1, in_ref.shape[0]):
        everything = everything + in_ref[i]
    return value, everything


def message(vector, image, own, out_ref):
    norm = jnp.sum(own * vector * vector, axis=0, keepdims=True)
    product = jnp.sum(vector * image, axis=0, keepdims=True)
    row = lax.broadcasted_iota(jnp.int32, (ROWS, LANES), 0)
    value = jnp.where(row == 7, norm, image)
    value = jnp.where(row == 15, product, value)
    for i in range(out_ref.shape[0]):
        out_ref[i] = value


def z_last_kernel(mine_ref, swap_ref, out_ref):
    z_kernel(mine_ref, swap_ref, out_ref.at[0])
    out_ref[0, 7:8] = mine_ref[7:8] + swap_ref[7:8]
    value = out_ref[0]
    for i in range(1, out_ref.shape[0]):
        out_ref[i] = value


def total_of(in_ref):
    total = in_ref[0]
    for i in range(1, in_ref.shape[0]):
        total = total + in_ref[i]
    return total


def x_last_kernel(in_ref, out_ref):
    gx, nx = lax.axis_index("gx"), lax.axis_size("gx")
    kx, _, _ = iotas()
    first_x, last_x = jnp.where(gx > 0, 2, -1), jnp.where(gx < nx - 1, 4, 8)
    low, high = in_ref[jnp.maximum(gx - 1, 0)], in_ref[jnp.minimum(gx + 1, nx - 1)]
    value = in_ref[gx] + jnp.where(kx <= first_x, rows_rolled(low, 4), 0.0)
    value = value + jnp.where((kx >= last_x) & (kx <= 6), rows_rolled(high, 4), 0.0)
    value = jnp.where(kx == 7, total_of(in_ref), value)
    for i in range(out_ref.shape[0]):
        out_ref[i] = value


def basis_kernel(number, mine_ref, other_ref, pair_ref, *refs):
    past = refs[:number]
    operands = refs[number : number + 5]
    out_ref, *new_refs, field_ref, sums_ref = refs[number + 5 :]
    inside, own = masks(places())
    value, size = y_sum(mine_ref, pair_ref, other_ref)
    value = value * inside
    if number:
        value = value + DAMP * past[-1][...]
    if number == 3:
        inverse = 1.0 / size
        one, two = past[1][...], past[2][...]
        second = inverse * two - SHIFTS[1] * one
        value = inverse * (inverse * value - SHIFTS[1] * two) - SHIFTS[2] * second
        new_refs[1][...] = second
    elif number > 3:
        value = value / size - SHIFTS[number - 1] * past[-1][...]
    new_refs[0][...] = value
    image = apply_local(value, *operands, field_ref, sums_ref) * inside
    if number < 5:
        out_ref[...] = with_size(image, jnp.broadcast_to(size, (ROWS, LANES)))
        return
    new_refs[1][...] = jnp.broadcast_to(size, (8, LANES))
    vectors = [ref[...] for ref in past] + [value]
    products = []
    for i in range(6):
        mine = own * vectors[i]
        for j in range(i, 6):
            products.append(mine * vectors[j])
    products.append(value * image + DAMP * own * value * value)
    sums = [jnp.sum(p, axis=0, keepdims=True) for p in products]
    sums = jnp.concatenate(sums + [jnp.zeros((2, LANES), jnp.float32)], axis=0)
    sums = jnp.sum(sums, axis=1, keepdims=True)
    row = lax.broadcasted_iota(jnp.int32, (ROWS, LANES), 0)
    lane = lax.broadcasted_iota(jnp.int32, (ROWS, LANES), 1)
    line = jnp.sum(jnp.where(row == lane, sums, 0.0), axis=0, keepdims=True)
    image = jnp.where(row == 7, line, image)
    out_ref[...] = image


def times(a, b):
    return None if a is None or b is None else a * b


def form(left, table, right):
    total = None
    for i, a in enumerate(left):
        inner = None
        for j, b in enumerate(right):
            inner = add(inner, times(table[i][j], b))
        total = add(total, times(a, inner))
    return total


def fast_kernel(in_ref, *refs):
    vectors = [ref[...] for ref in refs[:6]]
    size_ref, solution_ref, residual_ref, good_ref = refs[6:]
    inside, _ = masks(places())
    value, everything = along_y_sum(in_ref)
    size = size_ref[0:1, 0:1]
    inverse = 1.0 / size
    image = (value * inside + DAMP * vectors[5]) * inverse
    line = everything[7:8]
    lane = lax.broadcasted_iota(jnp.int32, (1, LANES), 1)
    scalars = [jnp.sum(jnp.where(lane == k, line, 0.0), axis=1, keepdims=True) for k in range(22)]
    gram = [[None] * 6 for _ in range(6)]
    k = 0
    for i in range(6):
        for j in range(i, 6):
            gram[i][j] = gram[j][i] = scalars[k]
            k += 1
    factor = [inverse] + [jnp.ones_like(inverse)] * 4
    energy = [[None] * 6 for _ in range(6)]
    for i in range(5):
        for j in range(i, 6):
            energy[i][j] = energy[j][i] = factor[i] * (gram[i + 1][j] + SHIFTS[i] * gram[i][j])
    energy[5][5] = scalars[21] * inverse
    rest = [row[:] for row in gram]
    good = jnp.ones_like(inverse)
    for k in range(6):
        good = jnp.where(rest[k][k] / gram[k][k] > WORST_PIVOT, good, 0.0)
        for i in range(k + 1, 6):
            ratio = rest[i][k] / rest[k][k]
            for j in range(i, 6):
                rest[i][j] = rest[i][j] - ratio * rest[k][j]
                rest[j][i] = rest[i][j]
    good_ref[0, 0] = jnp.sum(good).astype(jnp.int32)
    solved = [None] * 7
    residual = [jnp.ones_like(inverse)] + [None] * 6
    direction = residual[:]
    norm = gram[0][0]
    for number in range(ITERS):
        known = number + 1
        moved = [None] * 7
        for j in range(known):
            if j == 5:
                moved[6] = add(moved[6], direction[5])
            else:
                part = factor[j] * direction[j]
                moved[j + 1] = add(moved[j + 1], part)
                moved[j] = add(moved[j], SHIFTS[j] * part)
        step = norm / form(direction[:known], energy, direction[:known])
        solved = [add(a, times(step, b)) for a, b in zip(solved, direction)]
        residual = [add(a, times(-step, b)) for a, b in zip(residual, moved)]
        if number < ITERS - 1:
            known += 1
            later = form(residual[:known], gram, residual[:known])
            ratio = later / norm
            direction = [add(a, times(ratio, b)) for a, b in zip(residual, direction)]
            norm = later
    vectors = vectors + [image]
    first, second = None, None
    for j in range(7):
        if solved[j] is not None:
            first = add(first, solved[j] * vectors[j])
        second = add(second, residual[j] * vectors[j])
    write_out(first * (inverse / SCALE), second, solution_ref, residual_ref)


def write_out(solved, residual, solution_ref, residual_ref):
    both = jnp.concatenate([solved, residual], axis=0)
    value = dot(split3(both), put(), ((1,), (1,)))
    value = value[:48] + value[48:96] + value[96:]
    for z in range(CELLS_Z):
        for c in range(3):
            solution_ref[c, z] = value[c * 8 + 1 : c * 8 + 5, z * 16 : z * 16 + 16]
            residual_ref[c, z] = value[ROWS + c * 8 + 1 : ROWS + c * 8 + 5, z * 16 : z * 16 + 16]


def slow_kernel(vector_ref, grad_ref, rows_ref, back_ref, along_ref, lanes_ref, out_ref, field_ref, sums_ref):
    inside, own = masks(places())
    vector = vector_ref[...]
    image = apply_local(vector, grad_ref, rows_ref, back_ref, along_ref, lanes_ref, field_ref, sums_ref)
    message(vector, image * inside, own, out_ref)


def update(in_ref, old_ref, number):
    inside, own = masks(places())
    value, everything = along_y_sum(in_ref)
    residual = old_ref[ROWS : 2 * ROWS] if number else old_ref[...]
    image = value * inside + DAMP * residual
    norm = jnp.sum(everything[7:8], axis=1, keepdims=True)
    product = jnp.sum(everything[15:16], axis=1, keepdims=True) + DAMP * norm
    if number:
        ratio = norm / old_ref[4 * ROWS : 4 * ROWS + 1, 0:1]
        step = norm / (product - ratio * norm / old_ref[4 * ROWS + 1 : 4 * ROWS + 2, 0:1])
        direction = residual + ratio * old_ref[2 * ROWS : 3 * ROWS]
        image = image + ratio * old_ref[3 * ROWS : 4 * ROWS]
        solved = old_ref[0:ROWS] + step * direction
    else:
        step = norm / product
        direction = residual
        solved = step * direction
    residual = residual - step * image
    return own, inside, solved, residual, direction, image, norm, step


def step_kernel(number, in_ref, old_ref, grad_ref, rows_ref, back_ref, along_ref, lanes_ref, out_ref, new_ref, field_ref, sums_ref):
    own, inside, solved, residual, direction, image, norm, step = update(in_ref, old_ref, number)
    new_ref[0:ROWS] = solved
    new_ref[ROWS : 2 * ROWS] = residual
    new_ref[2 * ROWS : 3 * ROWS] = direction
    new_ref[3 * ROWS : 4 * ROWS] = image
    row = lax.broadcasted_iota(jnp.int32, (8, LANES), 0)
    new_ref[4 * ROWS : 4 * ROWS + 8] = jnp.where(row == 0, norm, step)
    image = apply_local(residual, grad_ref, rows_ref, back_ref, along_ref, lanes_ref, field_ref, sums_ref)
    message(residual, image * inside, own, out_ref)


def last_kernel(in_ref, old_ref, solution_ref, residual_ref):
    _, _, solved, residual, _, _, _, _ = update(in_ref, old_ref, ITERS - 1)
    write_out(solved / SCALE, residual, solution_ref, residual_ref)


def call(body, outs, *args, scratch=False):
    shapes = [
        jax.ShapeDtypeStruct(s, jnp.float32) if s else jax.ShapeDtypeStruct((1, 1), jnp.int32)
        for s in outs
    ]
    scratch_shapes = [pltpu.VMEM((96, 7 * LANES), jnp.float32)] * 2 if scratch else []
    vmem = pl.BlockSpec(memory_space=pltpu.VMEM)
    return pl.pallas_call(
        body,
        out_shape=shapes,
        in_specs=[vmem] * len(args),
        out_specs=[vmem if s else pl.BlockSpec(memory_space=pltpu.SMEM) for s in outs],
        scratch_shapes=scratch_shapes,
        compiler_params=pltpu.CompilerParams(vmem_limit_bytes=24 * 1024 * 1024),
    )(*args)


def swaps(axis):
    count = lax.axis_size(axis)
    pair = [(i, i ^ 1) for i in range(count)]
    other = [(i, (i + 1 if i % 2 else i - 1) % count) for i in range(count)]
    return pair, other


def shards(gradient, right_side):
    (gx, nx), (gy, ny), (gz, nz) = places()
    rows_x, back_x, along_y, lanes = [jnp.asarray(t) for t in tables()]
    rows_x = lax.dynamic_index_in_dim(rows_x, kind_of(gx, nx), 0, keepdims=False)
    along_y = lax.dynamic_index_in_dim(along_y, gz, 0, keepdims=False)
    lanes = lax.dynamic_index_in_dim(lanes, gz * 3 + kind_of(gy, ny), 0, keepdims=False)
    operands = (gradient, rows_x, back_x, along_y, lanes)
    group, line, box = (nx * nz, ROWS, LANES), (ny, ROWS, LANES), (ROWS, LANES)
    tile, state, shape = (8, LANES), (4 * ROWS + 8, LANES), right_side.shape

    def exchange_all(sent):
        near = lax.all_to_all(sent, ("gx", "gz"), 0, 0)
        (sent,) = call(middle_kernel, [line], near)
        return lax.all_to_all(sent, "gy", 0, 0)

    def exchange_near(sent, size=None):
        swapped = lax.ppermute(sent, "gz", swaps("gz")[0])
        (sent,) = call(z_kernel, [box], sent, swapped)
        if size is not None:
            (sent,) = call(x_first_kernel, [box], sent, size)
        pair, other = [lax.ppermute(sent, "gx", s) for s in swaps("gx")]
        (sent,) = call(x_kernel, [box], sent, pair, other)
        pair, other = swaps("gy")
        return sent, lax.ppermute(sent, "gy", other), lax.ppermute(sent, "gy", pair)

    def exchange_last(sent):
        swapped = lax.ppermute(sent, "gz", swaps("gz")[0])
        (sent,) = call(z_last_kernel, [(nx, ROWS, LANES)], sent, swapped)
        (sent,) = call(x_last_kernel, [line], lax.all_to_all(sent, "gx", 0, 0))
        return lax.all_to_all(sent, "gy", 0, 0)

    def slow(first):
        (sent,) = call(slow_kernel, [group], first, *operands, scratch=True)
        old = first
        for number in range(ITERS - 1):
            body = functools.partial(step_kernel, number)
            sent, old = call(body, [group, state], exchange_all(sent), old, *operands, scratch=True)
        return tuple(call(last_kernel, [shape, shape], exchange_all(sent), old))

    (sent,) = call(start_kernel, [box], right_side)
    size = pl.pallas_call(
        size_kernel,
        grid=(1,),
        out_shape=jax.ShapeDtypeStruct(tile, jnp.float32),
        in_specs=[pl.BlockSpec((3, 8, 1, 32, LANES), lambda i: (0, 0, 0, 0, 0))],
        out_specs=pl.BlockSpec(tile, lambda i: (0, 0)),
    )(gradient.reshape(3, 8, 4, 32, LANES))
    vectors = []
    for number in range(6):
        near = exchange_near(sent, size if number == 0 else None)
        outs = [box, box] + [[], [], [], [box], [], [tile]][number]
        body = functools.partial(basis_kernel, number)
        sent, vector, *extra = call(body, outs, *near, *vectors, *operands, scratch=True)
        if number == 3:
            vectors[2] = extra[0]
        vectors.append(vector)
    *fast, good = call(fast_kernel, [shape, shape, None], exchange_last(sent), *vectors, extra[0])
    return lax.cond(good[0, 0] > 0, lambda first: tuple(fast), slow, vectors[0])


def solution(mesh):
    placed = P(None, "gz", "gx", "gy")
    return jax.shard_map(
        shards,
        mesh=mesh,
        in_specs=(placed, placed),
        out_specs=(placed, placed),
        check_vma=False,
    )
```

```python
import functools

import jax
import jax.numpy as jnp
import ml_dtypes
import numpy as np
from jax import lax
from jax.experimental import pallas as pl
from jax.experimental.pallas import tpu as pltpu
from jax.sharding import PartitionSpec as P

ITERS = 6
SMOOTHING = 0.5
DAMPING = 0.05
HIGHEST = lax.Precision.HIGHEST

CELLS_Z, CELLS_X, CELLS_Y = 4, 4, 16
BOX_X, BOX_Y, BOX_Z = 7, 19, 6
LANES = 128
ROWS = 24
DENOMINATOR = 3072.0
SCALE = 512.0
DAMP = DAMPING / SCALE
SHIFTS = (0.0, 0.171, 0.452, 0.776, 0.114)
WORST_PIVOT = 0.05


def numerators(t):
    return (
        (8 - t) ** 3,
        3 * t**3 - 48 * t**2 + 2048,
        -3 * t**3 + 24 * t**2 + 192 * t + 512,
        t**3,
    )


WEIGHTS = [[n / DENOMINATOR for n in numerators(t)] for t in range(8)]


def basis(cells):
    table = np.zeros((8 * cells + 1, cells + 3 + 1))
    for voxel in range(8 * cells + 1):
        for k, n in enumerate(numerators(voxel % 8)):
            table[voxel, voxel // 8 + k] = n
    return table[:, :-1]


def mass_and_edges(cells, first, last):
    table = basis(cells) / DENOMINATOR
    own = table[:-1]
    steps = table[1:] - table[:-1]
    if last:
        steps[-1] = -table[-2]
    edges = steps.T @ steps
    if first:
        edges = edges + np.outer(table[0], table[0])
    return own.T @ own, edges


def place_z(matrix, part):
    return matrix[1:7, 1:7] if part == 0 else matrix[0:6, 0:6]


@functools.lru_cache(None)
def tables():
    bx = basis(CELLS_X)[:-1]
    expand = np.zeros((96, ROWS))
    for c in range(3):
        expand[c * 32 : c * 32 + 32, c * 8 : c * 8 + BOX_X] = bx / DENOMINATOR / DENOMINATOR
    rows_x = np.zeros((3, 144, ROWS), np.float32)
    for kind in range(3):
        mass, edges = mass_and_edges(CELLS_X, kind == 0, kind == 2)
        rows_x[kind, :96] = expand
        for c in range(3):
            at = slice(c * 8, c * 8 + BOX_X)
            rows_x[kind, 96 + c * 8 : 96 + c * 8 + BOX_X, at] = SMOOTHING / SCALE * mass
            rows_x[kind, 120 + c * 8 : 120 + c * 8 + BOX_X, at] = SMOOTHING / SCALE * edges
    by = basis(CELLS_Y)[:-1]
    along_y = np.zeros((2, 2, LANES, 7 * LANES))
    for part in range(2):
        for f in range(BOX_Z):
            g = f + 1 if part == 0 else f
            low = by.T.astype(ml_dtypes.bfloat16).astype(np.float64)
            at = slice(f * BOX_Y, (f + 1) * BOX_Y)
            along_y[part, 0, at, g * LANES : (g + 1) * LANES] = low
            along_y[part, 1, at, g * LANES : (g + 1) * LANES] = by.T - low
    along_y = along_y.reshape(2, 256, 7 * LANES).astype(ml_dtypes.bfloat16)
    lanes = np.zeros((2, 3, 256, LANES), np.float32)
    for part in range(2):
        mz, kz = mass_and_edges(CELLS_Z, part == 0, part == 1)
        mz, kz = place_z(mz, part), place_z(kz, part)
        for kind in range(3):
            my, ky = mass_and_edges(CELLS_Y, kind == 0, kind == 2)
            used = BOX_Z * BOX_Y
            lanes[part, kind, :used, :used] = np.kron(kz, my) + np.kron(mz, ky)
            lanes[part, kind, 128 : 128 + used, :used] = np.kron(mz, my)
    return (
        rows_x,
        (expand.T / SCALE).astype(np.float32),
        along_y,
        lanes.reshape(6, 256, LANES),
    )


def iotas():
    row = lax.broadcasted_iota(jnp.int32, (ROWS, LANES), 0)
    lane = lax.broadcasted_iota(jnp.int32, (ROWS, LANES), 1)
    f = jnp.zeros_like(lane)
    for k in range(1, BOX_Z + 1):
        f = f + (lane >= k * BOX_Y).astype(jnp.int32)
    return row & 7, f, lane - f * BOX_Y


def masks(where):
    (gx, nx), (gy, ny), (gz, nz) = where
    kx, f, e = iotas()
    low_x, high_x = jnp.where(gx == 0, 1, 0), jnp.where(gx == nx - 1, 4, 6)
    low_y, high_y = jnp.where(gy == 0, 1, 0), jnp.where(gy == ny - 1, 16, 18)
    high_z = jnp.where(gz == 0, 5, 4)
    inside = (kx >= low_x) & (kx <= high_x) & (e >= low_y) & (e <= high_y) & (f <= high_z)
    own_z = jnp.where(gz == 0, 0, 1)
    own = (kx >= 1) & (kx <= 4) & (e >= 1) & (e <= 16) & (f >= own_z) & (f <= own_z + 3)
    return inside.astype(jnp.float32), own.astype(jnp.float32)


def places():
    return tuple((lax.axis_index(a), lax.axis_size(a)) for a in ("gx", "gy", "gz"))


def add(a, b):
    return b if a is None else a if b is None else a + b


def split3(value):
    high = value.astype(jnp.bfloat16)
    rest = value - high.astype(jnp.float32)
    middle = rest.astype(jnp.bfloat16)
    low = (rest - middle.astype(jnp.float32)).astype(jnp.bfloat16)
    return jnp.concatenate([high, middle, low], axis=0)


def dot(a, b, dims=((1,), (0,)), precision=None):
    return lax.dot_general(
        a, b, (dims, ((), ())), precision=precision, preferred_element_type=jnp.float32
    )


def kind_of(index, count):
    return jnp.where(index == 0, 0, jnp.where(index == count - 1, 2, 1))


def apply_local(vector, grad_ref, rows_ref, back_ref, along_ref, lanes_ref, field_ref, sums_ref):
    first = dot(rows_ref[...], vector, precision=HIGHEST)
    pieces = split3(first[:96])
    field = dot(jnp.concatenate([pieces, pieces], axis=1), along_ref[...])
    field_ref[...] = field[:96] + field[96:192] + field[192:]

    def column(cx, carry):
        rows = [pl.ds(pl.multiple_of(c * 32 + cx * 8, 8), 8) for c in range(3)]
        inside = pl.ds(pl.multiple_of(cx * 8, 8), 8)
        total = [[None] * 4 for _ in range(3)]
        for cz in range(CELLS_Z):
            layer = [
                [field_ref[rows[c], (cz + k) * LANES : (cz + k + 1) * LANES] for k in range(4)]
                for c in range(3)
            ]

            def weighted(t, values):
                slope = [grad_ref[c, cz * 8 + t, inside, :] for c in range(3)]
                shade = slope[0] * values[0] + slope[1] * values[1] + slope[2] * values[2]
                return [slope[c] * shade for c in range(3)]

            edge, near = WEIGHTS[0][0], WEIGHTS[0][1]
            value = weighted(0, [edge * (v[0] + v[2]) + near * v[1] for v in layer])
            first = [edge * v for v in value]
            second = [near * v for v in value]
            outer = [v[0] + v[3] for v in layer]
            inner = [v[1] + v[2] for v in layer]
            outer_odd = [v[0] - v[3] for v in layer]
            inner_odd = [v[1] - v[2] for v in layer]
            edge, near = WEIGHTS[4][0], WEIGHTS[4][1]
            value = weighted(4, [edge * a + near * b for a, b in zip(outer, inner)])
            sums = [[edge * v, near * v, None, None] for v in value]
            for t in (1, 2, 3):
                w = WEIGHTS[t]
                a, b, p, q = (w[0] + w[3]) / 2, (w[1] + w[2]) / 2, (w[0] - w[3]) / 2, (w[1] - w[2]) / 2
                even = [a * outer[c] + b * inner[c] for c in range(3)]
                odd = [p * outer_odd[c] + q * inner_odd[c] for c in range(3)]
                one = weighted(t, [even[c] + odd[c] for c in range(3)])
                two = weighted(8 - t, [even[c] - odd[c] for c in range(3)])
                for c in range(3):
                    plus, minus = one[c] + two[c], one[c] - two[c]
                    terms = (a * plus, b * plus, p * minus, q * minus)
                    sums[c] = [add(x, y) for x, y in zip(sums[c], terms)]
            for c in range(3):
                outside, middle, outside_odd, middle_odd = sums[c]
                parts = (
                    outside + outside_odd + first[c],
                    middle + middle_odd + second[c],
                    middle - middle_odd + first[c],
                    outside - outside_odd,
                )
                total[c] = [add(x, y) for x, y in zip(total[c], parts)]
                sums_ref[rows[c], cz * LANES : (cz + 1) * LANES] = total[c][0]
                total[c] = total[c][1:] + [None]
        for c in range(3):
            for k in range(3):
                g = CELLS_Z + k
                sums_ref[rows[c], g * LANES : (g + 1) * LANES] = total[c][k]
        return carry

    lax.fori_loop(0, CELLS_X, column, 0, unroll=True)
    pieces = split3(sums_ref[...])
    back = dot(pieces, along_ref[...], ((1,), (1,)))
    back = back[:, :LANES] + back[:, LANES:]
    back = back[:96] + back[96:192] + back[192:]
    data = dot(back_ref[...], back, precision=HIGHEST)
    relief = dot(
        jnp.concatenate([first[96:120], first[120:144]], axis=1),
        lanes_ref[...],
        precision=HIGHEST,
    )
    return data + relief


def roll(value, shift, axis):
    return pltpu.roll(value, shift, axis)


def put():
    first_f = jnp.where(lax.axis_index("gz") == 0, 0, 1)
    row = lax.broadcasted_iota(jnp.int32, (64, LANES), 0)
    lane = lax.broadcasted_iota(jnp.int32, (64, LANES), 1)
    target = ((row >> 4) + first_f) * BOX_Y + 1 + (row & 15)
    return (lane == target).astype(jnp.float32).astype(jnp.bfloat16)


def start_kernel(right_ref, out_ref):
    parts = []
    for c in range(3):
        own = jnp.concatenate([right_ref[c, z] for z in range(CELLS_Z)], axis=1)
        parts += [jnp.zeros((1, 64), jnp.float32), own, jnp.zeros((3, 64), jnp.float32)]
    value = dot(split3(jnp.concatenate(parts, axis=0)), put())
    out_ref[...] = value[:ROWS] + value[ROWS : 2 * ROWS] + value[2 * ROWS :]


def size_kernel(grad_ref, out_ref):
    def plane(z, totals):
        totals = list(totals)
        for x in range(4):
            slope = [grad_ref[c, z, x * 8 : x * 8 + 8, :] for c in range(3)]
            k = 0
            for a in range(3):
                for b in range(a, 3):
                    totals[k] = totals[k] + slope[a] * slope[b]
                    k += 1
        return tuple(totals)

    zero = jnp.zeros((8, LANES), jnp.float32)
    totals = lax.fori_loop(0, 32, plane, (zero,) * 6)
    count = 32.0 * 32.0 * 128.0
    xx, xy, xz, yy, yz, zz = [
        jnp.sum(jnp.sum(t, axis=0, keepdims=True), axis=1, keepdims=True) / count for t in totals
    ]
    aa = xx * xx + xy * xy + xz * xz
    bb = xy * xy + yy * yy + yz * yz
    cc = xz * xz + yz * yz + zz * zz
    ab = xx * xy + xy * yy + xz * yz
    ac = xx * xz + xy * yz + xz * zz
    bc = xy * xz + yy * yz + yz * zz
    norm = aa * aa + bb * bb + cc * cc + 2.0 * (ab * ab + ac * ac + bc * bc)
    size = 0.73 * jnp.sqrt(jnp.sqrt(norm)) + 0.04
    row = lax.broadcasted_iota(jnp.int32, (8, LANES), 0)
    out_ref[...] = jnp.where(row == 7, jnp.broadcast_to(size, (8, LANES)), 0.0)


def with_size(value, *others):
    row = lax.broadcasted_iota(jnp.int32, (ROWS, LANES), 0)
    return jnp.where(row == 7, functools.reduce(jnp.maximum, others), value)


def pair_sides(index, pair, other):
    even = lax.rem(index, 2) == 0
    return jnp.where(even, other, pair), jnp.where(even, pair, other)


def z_kernel(mine_ref, swap_ref, out_ref):
    gz = lax.axis_index("gz")
    _, f, _ = iotas()
    mine, swap = mine_ref[...], swap_ref[...]
    other = roll(swap, jnp.where(gz == 0, 3 * BOX_Y, LANES - 3 * BOX_Y), 1)
    first_f = jnp.where(gz == 0, 3, 0)
    value = mine + jnp.where((f >= first_f) & (f <= first_f + 2), other, 0.0)
    out_ref[...] = with_size(value, mine, swap)


def x_kernel(mine_ref, pair_ref, other_ref, *rest):
    out_ref = rest[-1]
    gx, nx = lax.axis_index("gx"), lax.axis_size("gx")
    kx, _, _ = iotas()
    mine, pair, other = mine_ref[...], pair_ref[...], other_ref[...]
    low, high = pair_sides(gx, pair, other)
    first_x, last_x = jnp.where(gx > 0, 2, -1), jnp.where(gx < nx - 1, 4, 8)
    value = mine + jnp.where(kx <= first_x, rows_rolled(low, 4), 0.0)
    value = value + jnp.where((kx >= last_x) & (kx <= 6), rows_rolled(high, 4), 0.0)
    out_ref[...] = with_size(value, mine, pair, other)


def x_first_kernel(mine_ref, size_ref, out_ref):
    out_ref[...] = mine_ref[...]
    row = lax.broadcasted_iota(jnp.int32, (8, LANES), 0)
    out_ref[0:8] = jnp.where(row == 7, size_ref[...], mine_ref[0:8])


def y_sum(mine_ref, pair_ref, other_ref):
    gy, ny = lax.axis_index("gy"), lax.axis_size("gy")
    _, _, e = iotas()
    mine, pair, other = mine_ref[...], pair_ref[...], other_ref[...]
    low, high = pair_sides(gy, pair, other)
    first_y, last_y = jnp.where(gy > 0, 2, -1), jnp.where(gy < ny - 1, 16, LANES)
    value = mine + jnp.where(e <= first_y, roll(low, LANES - 16, 1), 0.0)
    value = value + jnp.where(e >= last_y, roll(high, 16, 1), 0.0)
    return value, jnp.maximum(jnp.maximum(mine, pair), other)[7:8]


def rows_rolled(value, shift):
    return jnp.concatenate(
        [roll(value[c * 8 : c * 8 + 8], shift, 0) for c in range(3)], axis=0
    )


def middle_kernel(in_ref, out_ref):
    (gx, nx), _, (gz, nz) = places()
    kx, f, e = iotas()
    has_low = (gx > 0).astype(jnp.int32)
    has_high = (gx < nx - 1).astype(jnp.int32)
    low = jnp.maximum(gx - 1, 0)
    high = jnp.minimum(gx + 1, nx - 1)
    take_low = (kx <= 2) & (has_low == 1)
    take_high = (kx >= 4) & (kx <= 6) & (has_high == 1)

    def along_x(part):
        value = in_ref[gx * nz + part]
        below = rows_rolled(in_ref[low * nz + part], 4)
        above = rows_rolled(in_ref[high * nz + part], 4)
        value = value + jnp.where(take_low, below, 0.0)
        return value + jnp.where(take_high, above, 0.0)

    mine = along_x(gz)
    other = along_x(1 - gz)
    other = roll(other, jnp.where(gz == 0, 3 * BOX_Y, LANES - 3 * BOX_Y), 1)
    first_f = jnp.where(gz == 0, 3, 0)
    value = mine + jnp.where((f >= first_f) & (f <= first_f + 2), other, 0.0)
    everything = in_ref[0]
    for i in range(1, in_ref.shape[0]):
        everything = everything + in_ref[i]
    value = jnp.where(kx == 7, everything, value)
    for i in range(out_ref.shape[0]):
        out_ref[i] = value


def along_y_sum(in_ref):
    _, (gy, ny), _ = places()
    kx, f, e = iotas()
    has_low = (gy > 0).astype(jnp.int32)
    has_high = (gy < ny - 1).astype(jnp.int32)
    below = roll(in_ref[jnp.maximum(gy - 1, 0)], LANES - 16, 1)
    above = roll(in_ref[jnp.minimum(gy + 1, ny - 1)], 16, 1)
    value = in_ref[gy]
    value = value + jnp.where((e <= 2) & (has_low == 1), below, 0.0)
    value = value + jnp.where((e >= 16) & (has_high == 1), above, 0.0)
    everything = in_ref[0]
    for i in range(1, in_ref.shape[0]):
        everything = everything + in_ref[i]
    return value, everything


def message(vector, image, own, out_ref):
    norm = jnp.sum(own * vector * vector, axis=0, keepdims=True)
    product = jnp.sum(vector * image, axis=0, keepdims=True)
    row = lax.broadcasted_iota(jnp.int32, (ROWS, LANES), 0)
    value = jnp.where(row == 7, norm, image)
    value = jnp.where(row == 15, product, value)
    for i in range(out_ref.shape[0]):
        out_ref[i] = value


def total_of(in_ref):
    total = in_ref[0]
    for i in range(1, in_ref.shape[0]):
        total = total + in_ref[i]
    return total


def own_parts(image, line, out_ref):
    (gx, nx), (gy, ny), (gz, nz) = places()
    kx, f, e = (v[0:8] for v in iotas())
    lane = lax.broadcasted_iota(jnp.int32, (8, LANES), 1)
    parts = [image[c * 8 : c * 8 + 8] for c in range(3)]
    after = jnp.zeros((8, LANES), jnp.float32)
    before, other_z, beside_y = after, after, after
    layers = 2 * BOX_Y
    start = jnp.where(gz == 0, 4 * BOX_Y, 0)
    for c, part in enumerate(parts):
        here = (kx == 2 * c) | (kx == 2 * c + 1)
        after = jnp.where(here, roll(part, (2 * c + 3) % 8, 0), after)
        before = jnp.where(kx == 2 * c, roll(part, 2 * c, 0), before)
        packed = roll(part, lax.rem(layers * c - start + LANES, LANES), 1)
        other_z = jnp.where((lane >= layers * c) & (lane < layers * c + layers), packed, other_z)
        beside_y = jnp.where(e == c, roll(part, c, 1), beside_y)
        here = (e == 17 - 2 * c) | (e == 18 - 2 * c)
        beside_y = jnp.where(here, roll(part, (LANES - 2 * c) % LANES, 1), beside_y)
    after, before, other_z, beside_y = [
        jnp.where(kx == 7, line, v) for v in (after, before, other_z, beside_y)
    ]
    for x in range(nx):
        for z in range(nz):
            value = jnp.where((gx == x) & (gz != z), other_z, beside_y)
            value = jnp.where(gx + 1 == x, after, jnp.where(gx - 1 == x, before, value))
            for y in range(ny):
                out_ref[(x * ny + y) * nz + z] = value


def own_sum(image, in_ref):
    (gx, nx), (gy, ny), (gz, nz) = places()
    kx, f, e = (v[0:8] for v in iotas())
    lower_y, upper_y = gy > 0, gy < ny - 1
    below_y, above_y = jnp.maximum(gy - 1, 0), jnp.minimum(gy + 1, ny - 1)
    below_mask = ((e == 1) | (e == 2)) & lower_y
    above_mask = (e == 16) & upper_y
    first_f, last_f = jnp.where(gz == 0, 3, 1), jnp.where(gz == 0, 3, 2)
    z_mask = (f >= first_f) & (f <= last_f)

    def tile(x, y, z):
        return in_ref[(x * ny + y) * nz + z]

    def over_y(x, z):
        value = tile(x, gy, z)
        value = value + jnp.where(below_mask, roll(tile(x, below_y, z), LANES - 16, 1), 0.0)
        return value + jnp.where(above_mask, roll(tile(x, above_y, z), 16, 1), 0.0)

    def over_z(x):
        moved = roll(over_y(x, 1 - gz), jnp.where(gz == 0, 3 * BOX_Y, LANES - 3 * BOX_Y), 1)
        return over_y(x, gz) + jnp.where(z_mask, moved, 0.0)

    from_before = over_z(jnp.maximum(gx - 1, 0))
    from_after = over_z(jnp.minimum(gx + 1, nx - 1))
    from_z = over_y(gx, 1 - gz)
    from_below, from_above = tile(gx, below_y, gz), tile(gx, above_y, gz)
    layers = 2 * BOX_Y
    start = jnp.where(gz == 0, 3 * BOX_Y, BOX_Y)
    own_rows = (kx >= 1) & (kx <= 4)
    sums = []
    for c in range(3):
        value = image[c * 8 : c * 8 + 8]
        here = ((kx == 1) | (kx == 2)) & (gx > 0)
        value = value + jnp.where(here, roll(from_before, (1 - 2 * c) % 8, 0), 0.0)
        here = (kx == 4) & (gx < nx - 1)
        value = value + jnp.where(here, roll(from_after, (4 - 2 * c) % 8, 0), 0.0)
        moved = roll(from_z, lax.rem(start - layers * c + LANES, LANES), 1)
        value = value + jnp.where(own_rows & z_mask, moved, 0.0)
        moved = roll(from_below, LANES - 16 + 2 * c, 1)
        value = value + jnp.where(own_rows & below_mask, moved, 0.0)
        moved = roll(from_above, 16 - c, 1)
        value = value + jnp.where(own_rows & above_mask, moved, 0.0)
        sums.append(value)
    return jnp.concatenate(sums, axis=0)


def basis_kernel(number, mine_ref, pair_ref, other_ref, *refs):
    past = refs[:number]
    operands = refs[number : number + 5]
    out_ref, *new_refs, field_ref, sums_ref = refs[number + 5 :]
    inside, own = masks(places())
    value, size = y_sum(mine_ref, pair_ref, other_ref)
    value = value * inside
    if number:
        value = value + DAMP * past[-1][...]
    if number == 3:
        inverse = 1.0 / size
        one, two = past[1][...], past[2][...]
        second = inverse * two - SHIFTS[1] * one
        value = inverse * (inverse * value - SHIFTS[1] * two) - SHIFTS[2] * second
        new_refs[1][...] = second
    elif number > 3:
        value = value / size - SHIFTS[number - 1] * past[-1][...]
    new_refs[0][...] = value
    image = apply_local(value, *operands, field_ref, sums_ref) * inside
    if number < 5:
        out_ref[...] = with_size(image, jnp.broadcast_to(size, (ROWS, LANES)))
        return
    new_refs[1][...] = jnp.broadcast_to(size, (8, LANES))
    vectors = [ref[...] for ref in past] + [value]
    products = []
    for i in range(6):
        mine = own * vectors[i]
        for j in range(i, 6):
            products.append(mine * vectors[j])
    products.append(value * image + DAMP * own * value * value)
    sums = [jnp.sum(p, axis=0, keepdims=True) for p in products]
    sums = jnp.concatenate(sums + [jnp.zeros((2, LANES), jnp.float32)], axis=0)
    sums = jnp.sum(sums, axis=1, keepdims=True)
    row = lax.broadcasted_iota(jnp.int32, (ROWS, LANES), 0)
    lane = lax.broadcasted_iota(jnp.int32, (ROWS, LANES), 1)
    line = jnp.sum(jnp.where(row == lane, sums, 0.0), axis=0, keepdims=True)
    own_parts(image, line, out_ref)
    new_refs[2][...] = image


def times(a, b):
    return None if a is None or b is None else a * b


def form(left, table, right):
    total = None
    for i, a in enumerate(left):
        inner = None
        for j, b in enumerate(right):
            inner = add(inner, times(table[i][j], b))
        total = add(total, times(a, inner))
    return total


def fast_kernel(in_ref, *refs):
    vectors = [ref[...] for ref in refs[:6]]
    size_ref, last_ref, solution_ref, residual_ref, good_ref = refs[6:]
    inside, _ = masks(places())
    value = own_sum(last_ref[...], in_ref)
    size = size_ref[0:1, 0:1]
    inverse = 1.0 / size
    image = (value * inside + DAMP * vectors[5]) * inverse
    line = total_of(in_ref)[7:8]
    lane = lax.broadcasted_iota(jnp.int32, (1, LANES), 1)
    scalars = [jnp.sum(jnp.where(lane == k, line, 0.0), axis=1, keepdims=True) for k in range(22)]
    gram = [[None] * 6 for _ in range(6)]
    k = 0
    for i in range(6):
        for j in range(i, 6):
            gram[i][j] = gram[j][i] = scalars[k]
            k += 1
    factor = [inverse] + [jnp.ones_like(inverse)] * 4
    energy = [[None] * 6 for _ in range(6)]
    for i in range(5):
        for j in range(i, 6):
            energy[i][j] = energy[j][i] = factor[i] * (gram[i + 1][j] + SHIFTS[i] * gram[i][j])
    energy[5][5] = scalars[21] * inverse
    rest = [row[:] for row in gram]
    good = jnp.ones_like(inverse)
    for k in range(6):
        good = jnp.where(rest[k][k] / gram[k][k] > WORST_PIVOT, good, 0.0)
        for i in range(k + 1, 6):
            ratio = rest[i][k] / rest[k][k]
            for j in range(i, 6):
                rest[i][j] = rest[i][j] - ratio * rest[k][j]
                rest[j][i] = rest[i][j]
    good_ref[0, 0] = jnp.sum(good).astype(jnp.int32)
    solved = [None] * 7
    residual = [jnp.ones_like(inverse)] + [None] * 6
    direction = residual[:]
    norm = gram[0][0]
    for number in range(ITERS):
        known = number + 1
        moved = [None] * 7
        for j in range(known):
            if j == 5:
                moved[6] = add(moved[6], direction[5])
            else:
                part = factor[j] * direction[j]
                moved[j + 1] = add(moved[j + 1], part)
                moved[j] = add(moved[j], SHIFTS[j] * part)
        step = norm / form(direction[:known], energy, direction[:known])
        solved = [add(a, times(step, b)) for a, b in zip(solved, direction)]
        residual = [add(a, times(-step, b)) for a, b in zip(residual, moved)]
        if number < ITERS - 1:
            known += 1
            later = form(residual[:known], gram, residual[:known])
            ratio = later / norm
            direction = [add(a, times(ratio, b)) for a, b in zip(residual, direction)]
            norm = later
    vectors = vectors + [image]
    first, second = None, None
    for j in range(7):
        if solved[j] is not None:
            first = add(first, solved[j] * vectors[j])
        second = add(second, residual[j] * vectors[j])
    write_out(first * (inverse / SCALE), second, solution_ref, residual_ref)


def write_out(solved, residual, solution_ref, residual_ref):
    both = jnp.concatenate([solved, residual], axis=0)
    value = dot(split3(both), put(), ((1,), (1,)))
    value = value[:48] + value[48:96] + value[96:]
    for z in range(CELLS_Z):
        for c in range(3):
            solution_ref[c, z] = value[c * 8 + 1 : c * 8 + 5, z * 16 : z * 16 + 16]
            residual_ref[c, z] = value[ROWS + c * 8 + 1 : ROWS + c * 8 + 5, z * 16 : z * 16 + 16]


def slow_kernel(vector_ref, grad_ref, rows_ref, back_ref, along_ref, lanes_ref, out_ref, field_ref, sums_ref):
    inside, own = masks(places())
    vector = vector_ref[...]
    image = apply_local(vector, grad_ref, rows_ref, back_ref, along_ref, lanes_ref, field_ref, sums_ref)
    message(vector, image * inside, own, out_ref)


def update(in_ref, old_ref, number):
    inside, own = masks(places())
    value, everything = along_y_sum(in_ref)
    residual = old_ref[ROWS : 2 * ROWS] if number else old_ref[...]
    image = value * inside + DAMP * residual
    norm = jnp.sum(everything[7:8], axis=1, keepdims=True)
    product = jnp.sum(everything[15:16], axis=1, keepdims=True) + DAMP * norm
    if number:
        ratio = norm / old_ref[4 * ROWS : 4 * ROWS + 1, 0:1]
        step = norm / (product - ratio * norm / old_ref[4 * ROWS + 1 : 4 * ROWS + 2, 0:1])
        direction = residual + ratio * old_ref[2 * ROWS : 3 * ROWS]
        image = image + ratio * old_ref[3 * ROWS : 4 * ROWS]
        solved = old_ref[0:ROWS] + step * direction
    else:
        step = norm / product
        direction = residual
        solved = step * direction
    residual = residual - step * image
    return own, inside, solved, residual, direction, image, norm, step


def step_kernel(number, in_ref, old_ref, grad_ref, rows_ref, back_ref, along_ref, lanes_ref, out_ref, new_ref, field_ref, sums_ref):
    own, inside, solved, residual, direction, image, norm, step = update(in_ref, old_ref, number)
    new_ref[0:ROWS] = solved
    new_ref[ROWS : 2 * ROWS] = residual
    new_ref[2 * ROWS : 3 * ROWS] = direction
    new_ref[3 * ROWS : 4 * ROWS] = image
    row = lax.broadcasted_iota(jnp.int32, (8, LANES), 0)
    new_ref[4 * ROWS : 4 * ROWS + 8] = jnp.where(row == 0, norm, step)
    image = apply_local(residual, grad_ref, rows_ref, back_ref, along_ref, lanes_ref, field_ref, sums_ref)
    message(residual, image * inside, own, out_ref)


def last_kernel(in_ref, old_ref, solution_ref, residual_ref):
    _, _, solved, residual, _, _, _, _ = update(in_ref, old_ref, ITERS - 1)
    write_out(solved / SCALE, residual, solution_ref, residual_ref)


def call(body, outs, *args, scratch=False):
    shapes = [
        jax.ShapeDtypeStruct(s, jnp.float32) if s else jax.ShapeDtypeStruct((1, 1), jnp.int32)
        for s in outs
    ]
    scratch_shapes = [pltpu.VMEM((96, 7 * LANES), jnp.float32)] * 2 if scratch else []
    vmem = pl.BlockSpec(memory_space=pltpu.VMEM)
    return pl.pallas_call(
        body,
        out_shape=shapes,
        in_specs=[vmem] * len(args),
        out_specs=[vmem if s else pl.BlockSpec(memory_space=pltpu.SMEM) for s in outs],
        scratch_shapes=scratch_shapes,
        compiler_params=pltpu.CompilerParams(vmem_limit_bytes=24 * 1024 * 1024),
    )(*args)


def swaps(axis):
    count = lax.axis_size(axis)
    pair = [(i, i ^ 1) for i in range(count)]
    other = [(i, (i + 1 if i % 2 else i - 1) % count) for i in range(count)]
    return pair, other


def shards(gradient, right_side):
    (gx, nx), (gy, ny), (gz, nz) = places()
    rows_x, back_x, along_y, lanes = [jnp.asarray(t) for t in tables()]
    rows_x = lax.dynamic_index_in_dim(rows_x, kind_of(gx, nx), 0, keepdims=False)
    along_y = lax.dynamic_index_in_dim(along_y, gz, 0, keepdims=False)
    lanes = lax.dynamic_index_in_dim(lanes, gz * 3 + kind_of(gy, ny), 0, keepdims=False)
    operands = (gradient, rows_x, back_x, along_y, lanes)
    group, line, box = (nx * nz, ROWS, LANES), (ny, ROWS, LANES), (ROWS, LANES)
    everyone = (nx * ny * nz, 8, LANES)
    tile, state, shape = (8, LANES), (4 * ROWS + 8, LANES), right_side.shape

    def exchange_all(sent):
        near = lax.all_to_all(sent, ("gx", "gz"), 0, 0)
        (sent,) = call(middle_kernel, [line], near)
        return lax.all_to_all(sent, "gy", 0, 0)

    def exchange_near(sent, size=None):
        swapped = lax.ppermute(sent, "gz", swaps("gz")[0])
        (sent,) = call(z_kernel, [box], sent, swapped)
        if size is not None:
            (sent,) = call(x_first_kernel, [box], sent, size)
        pair, other = [lax.ppermute(sent, "gx", s) for s in swaps("gx")]
        (sent,) = call(x_kernel, [box], sent, pair, other)
        pair, other = swaps("gy")
        other = lax.ppermute(sent, "gy", other)
        pair = lax.ppermute(sent, "gy", pair)
        return sent, pair, other

    def slow(first):
        (sent,) = call(slow_kernel, [group], first, *operands, scratch=True)
        old = first
        for number in range(ITERS - 1):
            body = functools.partial(step_kernel, number)
            sent, old = call(body, [group, state], exchange_all(sent), old, *operands, scratch=True)
        return tuple(call(last_kernel, [shape, shape], exchange_all(sent), old))

    (sent,) = call(start_kernel, [box], right_side)
    (size,) = call(size_kernel, [tile], gradient)
    vectors = []
    for number in range(6):
        near = exchange_near(sent, size if number == 0 else None)
        outs = [everyone if number == 5 else box, box] + [[], [], [], [box], [], [tile, box]][number]
        body = functools.partial(basis_kernel, number)
        sent, vector, *extra = call(body, outs, *near, *vectors, *operands, scratch=True)
        if number == 3:
            vectors[2] = extra[0]
        vectors.append(vector)
    arrived = lax.all_to_all(sent, ("gx", "gy", "gz"), 0, 0)
    *fast, good = call(fast_kernel, [shape, shape, None], arrived, *vectors, *extra)
    return lax.cond(good[0, 0] > 0, lambda first: tuple(fast), slow, vectors[0])


def solution(mesh):
    placed = P(None, "gz", "gx", "gy")
    return jax.shard_map(
        shards,
        mesh=mesh,
        in_specs=(placed, placed),
        out_specs=(placed, placed),
        check_vma=False,
    )
```

```python
import functools

import jax
import jax.numpy as jnp
import ml_dtypes
import numpy as np
from jax import lax
from jax.experimental import pallas as pl
from jax.experimental.pallas import tpu as pltpu
from jax.sharding import PartitionSpec as P

ITERS = 6
SMOOTHING = 0.5
DAMPING = 0.05
HIGHEST = lax.Precision.HIGHEST

CELLS_Z, CELLS_X, CELLS_Y = 4, 4, 16
BOX_X, BOX_Y, BOX_Z = 7, 19, 6
LANES = 128
ROWS = 24
DENOMINATOR = 3072.0
SCALE = 512.0
DAMP = DAMPING / SCALE
SHIFTS = (0.0, 0.171, 0.452, 0.776, 0.114)
WORST_PIVOT = 0.05
SPARE = ((4, 0, 76), (4, 1, 38), (5, 2, 76), (5, 3, 38))


def numerators(t):
    return (
        (8 - t) ** 3,
        3 * t**3 - 48 * t**2 + 2048,
        -3 * t**3 + 24 * t**2 + 192 * t + 512,
        t**3,
    )


WEIGHTS = [[n / DENOMINATOR for n in numerators(t)] for t in range(8)]


def basis(cells):
    table = np.zeros((8 * cells + 1, cells + 3 + 1))
    for voxel in range(8 * cells + 1):
        for k, n in enumerate(numerators(voxel % 8)):
            table[voxel, voxel // 8 + k] = n
    return table[:, :-1]


def mass_and_edges(cells, first, last):
    table = basis(cells) / DENOMINATOR
    own = table[:-1]
    steps = table[1:] - table[:-1]
    if last:
        steps[-1] = -table[-2]
    edges = steps.T @ steps
    if first:
        edges = edges + np.outer(table[0], table[0])
    return own.T @ own, edges


def place_z(matrix, part):
    return matrix[1:7, 1:7] if part == 0 else matrix[0:6, 0:6]


@functools.lru_cache(None)
def tables():
    bx = basis(CELLS_X)[:-1]
    expand = np.zeros((96, ROWS))
    for c in range(3):
        expand[c * 32 : c * 32 + 32, c * 8 : c * 8 + BOX_X] = bx / DENOMINATOR / DENOMINATOR
    rows_x = np.zeros((3, 144, ROWS), np.float32)
    for kind in range(3):
        mass, edges = mass_and_edges(CELLS_X, kind == 0, kind == 2)
        rows_x[kind, :96] = expand
        for c in range(3):
            at = slice(c * 8, c * 8 + BOX_X)
            rows_x[kind, 96 + c * 8 : 96 + c * 8 + BOX_X, at] = SMOOTHING / SCALE * mass
            rows_x[kind, 120 + c * 8 : 120 + c * 8 + BOX_X, at] = SMOOTHING / SCALE * edges
    by = basis(CELLS_Y)[:-1]
    along_y = np.zeros((2, 2, LANES, 7 * LANES))
    for part in range(2):
        for f in range(BOX_Z):
            g = f + 1 if part == 0 else f
            low = by.T.astype(ml_dtypes.bfloat16).astype(np.float64)
            at = slice(f * BOX_Y, (f + 1) * BOX_Y)
            along_y[part, 0, at, g * LANES : (g + 1) * LANES] = low
            along_y[part, 1, at, g * LANES : (g + 1) * LANES] = by.T - low
    along_y = along_y.reshape(2, 256, 7 * LANES).astype(ml_dtypes.bfloat16)
    lanes = np.zeros((2, 3, 256, LANES), np.float32)
    for part in range(2):
        mz, kz = mass_and_edges(CELLS_Z, part == 0, part == 1)
        mz, kz = place_z(mz, part), place_z(kz, part)
        for kind in range(3):
            my, ky = mass_and_edges(CELLS_Y, kind == 0, kind == 2)
            used = BOX_Z * BOX_Y
            lanes[part, kind, :used, :used] = np.kron(kz, my) + np.kron(mz, ky)
            lanes[part, kind, 128 : 128 + used, :used] = np.kron(mz, my)
    return (
        rows_x,
        (expand.T / SCALE).astype(np.float32),
        along_y,
        lanes.reshape(6, 256, LANES),
    )


def iotas():
    row = lax.broadcasted_iota(jnp.int32, (ROWS, LANES), 0)
    lane = lax.broadcasted_iota(jnp.int32, (ROWS, LANES), 1)
    f = jnp.zeros_like(lane)
    for k in range(1, BOX_Z + 1):
        f = f + (lane >= k * BOX_Y).astype(jnp.int32)
    return row & 7, f, lane - f * BOX_Y


def masks(where):
    (gx, nx), (gy, ny), (gz, nz) = where
    kx, f, e = iotas()
    low_x, high_x = jnp.where(gx == 0, 1, 0), jnp.where(gx == nx - 1, 4, 6)
    low_y, high_y = jnp.where(gy == 0, 1, 0), jnp.where(gy == ny - 1, 16, 18)
    high_z = jnp.where(gz == 0, 5, 4)
    inside = (kx >= low_x) & (kx <= high_x) & (e >= low_y) & (e <= high_y) & (f <= high_z)
    own_z = jnp.where(gz == 0, 0, 1)
    own = (kx >= 1) & (kx <= 4) & (e >= 1) & (e <= 16) & (f >= own_z) & (f <= own_z + 3)
    return inside.astype(jnp.float32), own.astype(jnp.float32)


def places():
    return tuple((lax.axis_index(a), lax.axis_size(a)) for a in ("gx", "gy", "gz"))


def add(a, b):
    return b if a is None else a if b is None else a + b


def split3(value):
    high = value.astype(jnp.bfloat16)
    rest = value - high.astype(jnp.float32)
    middle = rest.astype(jnp.bfloat16)
    low = (rest - middle.astype(jnp.float32)).astype(jnp.bfloat16)
    return jnp.concatenate([high, middle, low], axis=0)


def dot(a, b, dims=((1,), (0,)), precision=None):
    return lax.dot_general(
        a, b, (dims, ((), ())), precision=precision, preferred_element_type=jnp.float32
    )


def kind_of(index, count):
    return jnp.where(index == 0, 0, jnp.where(index == count - 1, 2, 1))


def apply_local(vector, grad_ref, rows_ref, back_ref, along_ref, lanes_ref, field_ref, sums_ref):
    first = dot(rows_ref[...], vector, precision=HIGHEST)
    pieces = split3(first[:96])
    field = dot(jnp.concatenate([pieces, pieces], axis=1), along_ref[...])
    field_ref[...] = field[:96] + field[96:192] + field[192:]

    def column(cx, carry):
        rows = [pl.ds(pl.multiple_of(c * 32 + cx * 8, 8), 8) for c in range(3)]
        inside = pl.ds(pl.multiple_of(cx * 8, 8), 8)
        total = [[None] * 4 for _ in range(3)]
        for cz in range(CELLS_Z):
            layer = [
                [field_ref[rows[c], (cz + k) * LANES : (cz + k + 1) * LANES] for k in range(4)]
                for c in range(3)
            ]

            def weighted(t, values):
                slope = [grad_ref[c, cz * 8 + t, inside, :] for c in range(3)]
                shade = slope[0] * values[0] + slope[1] * values[1] + slope[2] * values[2]
                return [slope[c] * shade for c in range(3)]

            edge, near = WEIGHTS[0][0], WEIGHTS[0][1]
            value = weighted(0, [edge * (v[0] + v[2]) + near * v[1] for v in layer])
            first = [edge * v for v in value]
            second = [near * v for v in value]
            outer = [v[0] + v[3] for v in layer]
            inner = [v[1] + v[2] for v in layer]
            outer_odd = [v[0] - v[3] for v in layer]
            inner_odd = [v[1] - v[2] for v in layer]
            edge, near = WEIGHTS[4][0], WEIGHTS[4][1]
            value = weighted(4, [edge * a + near * b for a, b in zip(outer, inner)])
            sums = [[edge * v, near * v, None, None] for v in value]
            for t in (1, 2, 3):
                w = WEIGHTS[t]
                a, b, p, q = (w[0] + w[3]) / 2, (w[1] + w[2]) / 2, (w[0] - w[3]) / 2, (w[1] - w[2]) / 2
                even = [a * outer[c] + b * inner[c] for c in range(3)]
                odd = [p * outer_odd[c] + q * inner_odd[c] for c in range(3)]
                one = weighted(t, [even[c] + odd[c] for c in range(3)])
                two = weighted(8 - t, [even[c] - odd[c] for c in range(3)])
                for c in range(3):
                    plus, minus = one[c] + two[c], one[c] - two[c]
                    terms = (a * plus, b * plus, p * minus, q * minus)
                    sums[c] = [add(x, y) for x, y in zip(sums[c], terms)]
            for c in range(3):
                outside, middle, outside_odd, middle_odd = sums[c]
                parts = (
                    outside + outside_odd + first[c],
                    middle + middle_odd + second[c],
                    middle - middle_odd + first[c],
                    outside - outside_odd,
                )
                total[c] = [add(x, y) for x, y in zip(total[c], parts)]
                sums_ref[rows[c], cz * LANES : (cz + 1) * LANES] = total[c][0]
                total[c] = total[c][1:] + [None]
        for c in range(3):
            for k in range(3):
                g = CELLS_Z + k
                sums_ref[rows[c], g * LANES : (g + 1) * LANES] = total[c][k]
        return carry

    lax.fori_loop(0, CELLS_X, column, 0, unroll=True)
    pieces = split3(sums_ref[...])
    back = dot(pieces, along_ref[...], ((1,), (1,)))
    back = back[:, :LANES] + back[:, LANES:]
    back = back[:96] + back[96:192] + back[192:]
    data = dot(back_ref[...], back, precision=HIGHEST)
    relief = dot(
        jnp.concatenate([first[96:120], first[120:144]], axis=1),
        lanes_ref[...],
        precision=HIGHEST,
    )
    return data + relief


def roll(value, shift, axis):
    return pltpu.roll(value, shift, axis)


def put():
    first_f = jnp.where(lax.axis_index("gz") == 0, 0, 1)
    row = lax.broadcasted_iota(jnp.int32, (64, LANES), 0)
    lane = lax.broadcasted_iota(jnp.int32, (64, LANES), 1)
    target = ((row >> 4) + first_f) * BOX_Y + 1 + (row & 15)
    return (lane == target).astype(jnp.float32).astype(jnp.bfloat16)


def start_kernel(right_ref, out_ref):
    parts = []
    for c in range(3):
        own = jnp.concatenate([right_ref[c, z] for z in range(CELLS_Z)], axis=1)
        parts += [jnp.zeros((1, 64), jnp.float32), own, jnp.zeros((3, 64), jnp.float32)]
    value = dot(split3(jnp.concatenate(parts, axis=0)), put())
    out_ref[...] = value[:ROWS] + value[ROWS : 2 * ROWS] + value[2 * ROWS :]


def size_kernel(grad_ref, out_ref):
    def plane(z, totals):
        totals = list(totals)
        for x in range(4):
            slope = [grad_ref[c, z, x * 8 : x * 8 + 8, :] for c in range(3)]
            k = 0
            for a in range(3):
                for b in range(a, 3):
                    totals[k] = totals[k] + slope[a] * slope[b]
                    k += 1
        return tuple(totals)

    zero = jnp.zeros((8, LANES), jnp.float32)
    totals = lax.fori_loop(0, 32, plane, (zero,) * 6)
    count = 32.0 * 32.0 * 128.0
    xx, xy, xz, yy, yz, zz = [
        jnp.sum(jnp.sum(t, axis=0, keepdims=True), axis=1, keepdims=True) / count for t in totals
    ]
    aa = xx * xx + xy * xy + xz * xz
    bb = xy * xy + yy * yy + yz * yz
    cc = xz * xz + yz * yz + zz * zz
    ab = xx * xy + xy * yy + xz * yz
    ac = xx * xz + xy * yz + xz * zz
    bc = xy * xz + yy * yz + yz * zz
    norm = aa * aa + bb * bb + cc * cc + 2.0 * (ab * ab + ac * ac + bc * bc)
    size = 0.73 * jnp.sqrt(jnp.sqrt(norm)) + 0.04
    row = lax.broadcasted_iota(jnp.int32, (8, LANES), 0)
    out_ref[...] = jnp.where(row == 7, jnp.broadcast_to(size, (8, LANES)), 0.0)


def with_size(value, *others):
    row = lax.broadcasted_iota(jnp.int32, (ROWS, LANES), 0)
    return jnp.where(row == 7, functools.reduce(jnp.maximum, others), value)


def pair_sides(index, pair, other):
    even = lax.rem(index, 2) == 0
    return jnp.where(even, other, pair), jnp.where(even, pair, other)


def z_kernel(mine_ref, swap_ref, out_ref):
    gz = lax.axis_index("gz")
    _, f, _ = iotas()
    mine, swap = mine_ref[...], swap_ref[...]
    other = roll(swap, jnp.where(gz == 0, 3 * BOX_Y, LANES - 3 * BOX_Y), 1)
    first_f = jnp.where(gz == 0, 3, 0)
    value = mine + jnp.where((f >= first_f) & (f <= first_f + 2), other, 0.0)
    out_ref[...] = with_size(value, mine, swap)


def x_kernel(mine_ref, pair_ref, other_ref, *rest):
    out_ref = rest[-1]
    gx, nx = lax.axis_index("gx"), lax.axis_size("gx")
    kx, _, _ = iotas()
    mine, pair, other = mine_ref[...], pair_ref[...], other_ref[...]
    low, high = pair_sides(gx, pair, other)
    first_x, last_x = jnp.where(gx > 0, 2, -1), jnp.where(gx < nx - 1, 4, 8)
    value = mine + jnp.where(kx <= first_x, rows_rolled(low, 4), 0.0)
    value = value + jnp.where((kx >= last_x) & (kx <= 6), rows_rolled(high, 4), 0.0)
    out_ref[...] = with_size(value, mine, pair, other)


def x_first_kernel(mine_ref, size_ref, out_ref):
    out_ref[...] = mine_ref[...]
    row = lax.broadcasted_iota(jnp.int32, (8, LANES), 0)
    out_ref[0:8] = jnp.where(row == 7, size_ref[...], mine_ref[0:8])


def y_sum(mine_ref, pair_ref, other_ref):
    gy, ny = lax.axis_index("gy"), lax.axis_size("gy")
    _, _, e = iotas()
    mine, pair, other = mine_ref[...], pair_ref[...], other_ref[...]
    low, high = pair_sides(gy, pair, other)
    first_y, last_y = jnp.where(gy > 0, 2, -1), jnp.where(gy < ny - 1, 16, LANES)
    value = mine + jnp.where(e <= first_y, roll(low, LANES - 16, 1), 0.0)
    value = value + jnp.where(e >= last_y, roll(high, 16, 1), 0.0)
    return value, jnp.maximum(jnp.maximum(mine, pair), other)[7:8]


def rows_rolled(value, shift):
    return jnp.concatenate(
        [roll(value[c * 8 : c * 8 + 8], shift, 0) for c in range(3)], axis=0
    )


def middle_kernel(in_ref, out_ref):
    (gx, nx), _, (gz, nz) = places()
    kx, f, e = iotas()
    has_low = (gx > 0).astype(jnp.int32)
    has_high = (gx < nx - 1).astype(jnp.int32)
    low = jnp.maximum(gx - 1, 0)
    high = jnp.minimum(gx + 1, nx - 1)
    take_low = (kx <= 2) & (has_low == 1)
    take_high = (kx >= 4) & (kx <= 6) & (has_high == 1)

    def along_x(part):
        value = in_ref[gx * nz + part]
        below = rows_rolled(in_ref[low * nz + part], 4)
        above = rows_rolled(in_ref[high * nz + part], 4)
        value = value + jnp.where(take_low, below, 0.0)
        return value + jnp.where(take_high, above, 0.0)

    mine = along_x(gz)
    other = along_x(1 - gz)
    other = roll(other, jnp.where(gz == 0, 3 * BOX_Y, LANES - 3 * BOX_Y), 1)
    first_f = jnp.where(gz == 0, 3, 0)
    value = mine + jnp.where((f >= first_f) & (f <= first_f + 2), other, 0.0)
    everything = in_ref[0]
    for i in range(1, in_ref.shape[0]):
        everything = everything + in_ref[i]
    value = jnp.where(kx == 7, everything, value)
    for i in range(out_ref.shape[0]):
        out_ref[i] = value


def along_y_sum(in_ref):
    _, (gy, ny), _ = places()
    kx, f, e = iotas()
    has_low = (gy > 0).astype(jnp.int32)
    has_high = (gy < ny - 1).astype(jnp.int32)
    below = roll(in_ref[jnp.maximum(gy - 1, 0)], LANES - 16, 1)
    above = roll(in_ref[jnp.minimum(gy + 1, ny - 1)], 16, 1)
    value = in_ref[gy]
    value = value + jnp.where((e <= 2) & (has_low == 1), below, 0.0)
    value = value + jnp.where((e >= 16) & (has_high == 1), above, 0.0)
    everything = in_ref[0]
    for i in range(1, in_ref.shape[0]):
        everything = everything + in_ref[i]
    return value, everything


def message(vector, image, own, out_ref):
    norm = jnp.sum(own * vector * vector, axis=0, keepdims=True)
    product = jnp.sum(vector * image, axis=0, keepdims=True)
    row = lax.broadcasted_iota(jnp.int32, (ROWS, LANES), 0)
    value = jnp.where(row == 7, norm, image)
    value = jnp.where(row == 15, product, value)
    for i in range(out_ref.shape[0]):
        out_ref[i] = value


def total_of(in_ref):
    values = [in_ref[i] for i in range(in_ref.shape[0])]
    while len(values) > 1:
        values = [a + b for a, b in zip(values[::2], values[1::2])]
    return values[0]


def tile_parts():
    kx, f, e = (v[0:8] for v in iotas())
    return kx, f, e, lax.broadcasted_iota(jnp.int32, (8, LANES), 1)


def own_parts(image, line, out_ref):
    (gx, nx), (gy, ny), (gz, nz) = places()
    row, f, e, lane = tile_parts()
    parts = [image[c * 8 : c * 8 + 8] for c in range(3)]
    six = jnp.zeros((8, LANES), jnp.float32)
    before, other_z, beside_y = six, six, six
    layers = 2 * BOX_Y
    start = jnp.where(gz == 0, 4 * BOX_Y, 0)
    for c, part in enumerate(parts):
        here = (row == 2 * c) | (row == 2 * c + 1)
        six = jnp.where(here, roll(part, (2 * c + 3) % 8, 0), six)
        before = jnp.where(row == c, roll(part, c, 0), before)
        part = roll(part, 7, 0)
        packed = roll(part, lax.rem(layers * c - start + LANES, LANES), 1)
        other_z = jnp.where((lane >= layers * c) & (lane < layers * c + layers), packed, other_z)
        beside_y = jnp.where(e == c, roll(part, c, 1), beside_y)
        here = (e == 17 - 2 * c) | (e == 18 - 2 * c)
        beside_y = jnp.where(here, roll(part, (LANES - 2 * c) % LANES, 1), beside_y)
    own = roll(six, jnp.where(gz == 0, 0, LANES - BOX_Y), 1)
    after = own
    for source, target, shift in SPARE:
        moved = roll(roll(own, (target - source) % 8, 0), shift, 1)
        after = jnp.where((row == target) & (lane >= 2 * layers), moved, after)
    own = roll(six, jnp.where(gz == 0, LANES - 4 * BOX_Y, 0), 1)
    after_z = jnp.where(lane < layers, own, roll(roll(own, 4, 0), layers, 1))
    values = (after, after_z, before, other_z, beside_y)
    scalars = jnp.where(row == 0, roll(line, 114, 1), roll(line, 100, 1))
    after, after_z, before, other_z, beside_y = [
        jnp.where(lane >= BOX_Z * BOX_Y, scalars, v)[0:4] for v in values
    ]
    for x in range(nx):
        for z in range(nz):
            same = gz == z
            value = jnp.where(gx == x, jnp.where(same, beside_y, other_z), before)
            value = jnp.where(gx + 1 == x, jnp.where(same, after, after_z), value)
            for y in range(ny):
                out_ref[(x * ny + y) * nz + z] = value


def own_sum(image, in_ref):
    (gx, nx), (gy, ny), (gz, nz) = places()
    row, f, e, lane = tile_parts()
    lower_y, upper_y = gy > 0, gy < ny - 1
    below_y, above_y = jnp.maximum(gy - 1, 0), jnp.minimum(gy + 1, ny - 1)
    below_mask = ((e == 1) | (e == 2)) & lower_y
    above_mask = (e == 16) & upper_y
    first_f, last_f = jnp.where(gz == 0, 3, 1), jnp.where(gz == 0, 3, 2)
    z_mask = (f >= first_f) & (f <= last_f)
    nothing = jnp.zeros((4, LANES), jnp.float32)

    def tile(x, y, z):
        return jnp.concatenate([in_ref[(x * ny + y) * nz + z], nothing], axis=0)

    def over_y(x, z):
        value = tile(x, gy, z)
        value = value + jnp.where(below_mask, roll(tile(x, below_y, z), LANES - 16, 1), 0.0)
        return value + jnp.where(above_mask, roll(tile(x, above_y, z), 16, 1), 0.0)

    layers = 2 * BOX_Y
    z_start = jnp.where(gz == 0, 3 * BOX_Y, BOX_Y)
    packed = over_y(jnp.maximum(gx - 1, 0), gz)
    six = packed
    for source, target, shift in SPARE:
        moved = roll(roll(packed, (source - target) % 8, 0), LANES - shift, 1)
        first = 2 * layers - shift
        six = jnp.where((row == source) & (lane >= first) & (lane < first + layers), moved, six)
    six = roll(six, jnp.where(gz == 0, 0, BOX_Y), 1)
    packed = over_y(jnp.maximum(gx - 1, 0), 1 - gz)
    moved = jnp.where(row < 4, packed, roll(roll(packed, 4, 0), LANES - layers, 1))
    from_before = six + jnp.where(z_mask, roll(moved, z_start, 1), 0.0)
    above_x = jnp.minimum(gx + 1, nx - 1)
    moved = roll(over_y(above_x, 1 - gz), jnp.where(gz == 0, 3 * BOX_Y, LANES - 3 * BOX_Y), 1)
    from_after = over_y(above_x, gz) + jnp.where(z_mask, moved, 0.0)
    from_z = roll(over_y(gx, 1 - gz), 1, 0)
    from_below, from_above = roll(tile(gx, below_y, gz), 1, 0), roll(tile(gx, above_y, gz), 1, 0)
    own_rows = (row >= 1) & (row <= 4)
    sums = []
    for c in range(3):
        value = image[c * 8 : c * 8 + 8]
        here = ((row == 1) | (row == 2)) & (gx > 0)
        value = value + jnp.where(here, roll(from_before, (1 - 2 * c) % 8, 0), 0.0)
        here = (row == 4) & (gx < nx - 1)
        value = value + jnp.where(here, roll(from_after, 4 - c, 0), 0.0)
        moved = roll(from_z, lax.rem(z_start - layers * c + LANES, LANES), 1)
        value = value + jnp.where(own_rows & z_mask, moved, 0.0)
        moved = roll(from_below, LANES - 16 + 2 * c, 1)
        value = value + jnp.where(own_rows & below_mask, moved, 0.0)
        moved = roll(from_above, 16 - c, 1)
        value = value + jnp.where(own_rows & above_mask, moved, 0.0)
        sums.append(value)
    return jnp.concatenate(sums, axis=0)


def basis_kernel(number, mine_ref, pair_ref, other_ref, *refs):
    past = refs[:number]
    operands = refs[number : number + 5]
    out_ref, *new_refs, field_ref, sums_ref = refs[number + 5 :]
    inside, own = masks(places())
    value, size = y_sum(mine_ref, pair_ref, other_ref)
    value = value * inside
    if number:
        value = value + DAMP * past[-1][...]
    if number == 3:
        inverse = 1.0 / size
        one, two = past[1][...], past[2][...]
        second = inverse * two - SHIFTS[1] * one
        value = inverse * (inverse * value - SHIFTS[1] * two) - SHIFTS[2] * second
        new_refs[1][...] = second
    elif number > 3:
        value = value / size - SHIFTS[number - 1] * past[-1][...]
    new_refs[0][...] = value
    image = apply_local(value, *operands, field_ref, sums_ref) * inside
    if number < 5:
        out_ref[...] = with_size(image, jnp.broadcast_to(size, (ROWS, LANES)))
        return
    new_refs[1][...] = jnp.broadcast_to(size, (8, LANES))
    vectors = [ref[...] for ref in past] + [value]
    products = []
    for i in range(6):
        mine = own * vectors[i]
        for j in range(i, 6):
            products.append(mine * vectors[j])
    products.append(value * image + DAMP * own * value * value)
    sums = [jnp.sum(p, axis=0, keepdims=True) for p in products]
    sums = jnp.concatenate(sums + [jnp.zeros((2, LANES), jnp.float32)], axis=0)
    sums = jnp.sum(sums, axis=1, keepdims=True)
    row = lax.broadcasted_iota(jnp.int32, (ROWS, LANES), 0)
    lane = lax.broadcasted_iota(jnp.int32, (ROWS, LANES), 1)
    line = jnp.sum(jnp.where(row == lane, sums, 0.0), axis=0, keepdims=True)
    own_parts(image, line, out_ref)
    new_refs[2][...] = image


def times(a, b):
    return None if a is None or b is None else a * b


def form(left, table, right):
    total = None
    for i, a in enumerate(left):
        inner = None
        for j, b in enumerate(right):
            inner = add(inner, times(table[i][j], b))
        total = add(total, times(a, inner))
    return total


def fast_kernel(in_ref, *refs):
    vectors = [ref[...] for ref in refs[:6]]
    size_ref, last_ref, solution_ref, residual_ref, good_ref = refs[6:]
    inside, _ = masks(places())
    value = own_sum(last_ref[...], in_ref)
    size = size_ref[0:1, 0:1]
    inverse = 1.0 / size
    image = (value * inside + DAMP * vectors[5]) * inverse
    total = total_of(in_ref)
    lane = lax.broadcasted_iota(jnp.int32, (1, LANES), 1)
    scalars = []
    for k in range(22):
        row, at = (0, 114 + k) if k < 14 else (1, 100 + k)
        scalars.append(jnp.sum(jnp.where(lane == at, total[row : row + 1], 0.0), axis=1, keepdims=True))
    gram = [[None] * 6 for _ in range(6)]
    k = 0
    for i in range(6):
        for j in range(i, 6):
            gram[i][j] = gram[j][i] = scalars[k]
            k += 1
    factor = [inverse] + [jnp.ones_like(inverse)] * 4
    energy = [[None] * 6 for _ in range(6)]
    for i in range(5):
        for j in range(i, 6):
            energy[i][j] = energy[j][i] = factor[i] * (gram[i + 1][j] + SHIFTS[i] * gram[i][j])
    energy[5][5] = scalars[21] * inverse
    rest = [row[:] for row in gram]
    good = jnp.ones_like(inverse)
    for k in range(6):
        good = jnp.where(rest[k][k] / gram[k][k] > WORST_PIVOT, good, 0.0)
        for i in range(k + 1, 6):
            ratio = rest[i][k] / rest[k][k]
            for j in range(i, 6):
                rest[i][j] = rest[i][j] - ratio * rest[k][j]
                rest[j][i] = rest[i][j]
    good_ref[0, 0] = jnp.sum(good).astype(jnp.int32)
    solved = [None] * 7
    residual = [jnp.ones_like(inverse)] + [None] * 6
    direction = residual[:]
    norm = gram[0][0]
    for number in range(ITERS):
        known = number + 1
        moved = [None] * 7
        for j in range(known):
            if j == 5:
                moved[6] = add(moved[6], direction[5])
            else:
                part = factor[j] * direction[j]
                moved[j + 1] = add(moved[j + 1], part)
                moved[j] = add(moved[j], SHIFTS[j] * part)
        step = norm / form(direction[:known], energy, direction[:known])
        solved = [add(a, times(step, b)) for a, b in zip(solved, direction)]
        residual = [add(a, times(-step, b)) for a, b in zip(residual, moved)]
        if number < ITERS - 1:
            known += 1
            later = form(residual[:known], gram, residual[:known])
            ratio = later / norm
            direction = [add(a, times(ratio, b)) for a, b in zip(residual, direction)]
            norm = later
    vectors = vectors + [image]
    first, second = None, None
    for j in range(7):
        if solved[j] is not None:
            first = add(first, solved[j] * vectors[j])
        second = add(second, residual[j] * vectors[j])
    write_out(first * (inverse / SCALE), second, solution_ref, residual_ref)


def write_out(solved, residual, solution_ref, residual_ref):
    both = jnp.concatenate([solved, residual], axis=0)
    value = dot(split3(both), put(), ((1,), (1,)))
    value = value[:48] + value[48:96] + value[96:]
    for z in range(CELLS_Z):
        for c in range(3):
            solution_ref[c, z] = value[c * 8 + 1 : c * 8 + 5, z * 16 : z * 16 + 16]
            residual_ref[c, z] = value[ROWS + c * 8 + 1 : ROWS + c * 8 + 5, z * 16 : z * 16 + 16]


def slow_kernel(vector_ref, grad_ref, rows_ref, back_ref, along_ref, lanes_ref, out_ref, field_ref, sums_ref):
    inside, own = masks(places())
    vector = vector_ref[...]
    image = apply_local(vector, grad_ref, rows_ref, back_ref, along_ref, lanes_ref, field_ref, sums_ref)
    message(vector, image * inside, own, out_ref)


def update(in_ref, old_ref, number):
    inside, own = masks(places())
    value, everything = along_y_sum(in_ref)
    residual = old_ref[ROWS : 2 * ROWS] if number else old_ref[...]
    image = value * inside + DAMP * residual
    norm = jnp.sum(everything[7:8], axis=1, keepdims=True)
    product = jnp.sum(everything[15:16], axis=1, keepdims=True) + DAMP * norm
    if number:
        ratio = norm / old_ref[4 * ROWS : 4 * ROWS + 1, 0:1]
        step = norm / (product - ratio * norm / old_ref[4 * ROWS + 1 : 4 * ROWS + 2, 0:1])
        direction = residual + ratio * old_ref[2 * ROWS : 3 * ROWS]
        image = image + ratio * old_ref[3 * ROWS : 4 * ROWS]
        solved = old_ref[0:ROWS] + step * direction
    else:
        step = norm / product
        direction = residual
        solved = step * direction
    residual = residual - step * image
    return own, inside, solved, residual, direction, image, norm, step


def step_kernel(number, in_ref, old_ref, grad_ref, rows_ref, back_ref, along_ref, lanes_ref, out_ref, new_ref, field_ref, sums_ref):
    own, inside, solved, residual, direction, image, norm, step = update(in_ref, old_ref, number)
    new_ref[0:ROWS] = solved
    new_ref[ROWS : 2 * ROWS] = residual
    new_ref[2 * ROWS : 3 * ROWS] = direction
    new_ref[3 * ROWS : 4 * ROWS] = image
    row = lax.broadcasted_iota(jnp.int32, (8, LANES), 0)
    new_ref[4 * ROWS : 4 * ROWS + 8] = jnp.where(row == 0, norm, step)
    image = apply_local(residual, grad_ref, rows_ref, back_ref, along_ref, lanes_ref, field_ref, sums_ref)
    message(residual, image * inside, own, out_ref)


def last_kernel(in_ref, old_ref, solution_ref, residual_ref):
    _, _, solved, residual, _, _, _, _ = update(in_ref, old_ref, ITERS - 1)
    write_out(solved / SCALE, residual, solution_ref, residual_ref)


def call(body, outs, *args, scratch=False):
    shapes = [
        jax.ShapeDtypeStruct(s, jnp.float32) if s else jax.ShapeDtypeStruct((1, 1), jnp.int32)
        for s in outs
    ]
    scratch_shapes = [pltpu.VMEM((96, 7 * LANES), jnp.float32)] * 2 if scratch else []
    vmem = pl.BlockSpec(memory_space=pltpu.VMEM)
    return pl.pallas_call(
        body,
        out_shape=shapes,
        in_specs=[vmem] * len(args),
        out_specs=[vmem if s else pl.BlockSpec(memory_space=pltpu.SMEM) for s in outs],
        scratch_shapes=scratch_shapes,
        compiler_params=pltpu.CompilerParams(vmem_limit_bytes=24 * 1024 * 1024),
    )(*args)


def swaps(axis):
    count = lax.axis_size(axis)
    pair = [(i, i ^ 1) for i in range(count)]
    other = [(i, (i + 1 if i % 2 else i - 1) % count) for i in range(count)]
    return pair, other


def shards(gradient, right_side):
    (gx, nx), (gy, ny), (gz, nz) = places()
    rows_x, back_x, along_y, lanes = [jnp.asarray(t) for t in tables()]
    rows_x = lax.dynamic_index_in_dim(rows_x, kind_of(gx, nx), 0, keepdims=False)
    along_y = lax.dynamic_index_in_dim(along_y, gz, 0, keepdims=False)
    lanes = lax.dynamic_index_in_dim(lanes, gz * 3 + kind_of(gy, ny), 0, keepdims=False)
    operands = (gradient, rows_x, back_x, along_y, lanes)
    group, line, box = (nx * nz, ROWS, LANES), (ny, ROWS, LANES), (ROWS, LANES)
    everyone = (nx * ny * nz, 4, LANES)
    tile, state, shape = (8, LANES), (4 * ROWS + 8, LANES), right_side.shape

    def exchange_all(sent):
        near = lax.all_to_all(sent, ("gx", "gz"), 0, 0)
        (sent,) = call(middle_kernel, [line], near)
        return lax.all_to_all(sent, "gy", 0, 0)

    def exchange_near(sent, size=None):
        swapped = lax.ppermute(sent, "gz", swaps("gz")[0])
        (sent,) = call(z_kernel, [box], sent, swapped)
        if size is not None:
            (sent,) = call(x_first_kernel, [box], sent, size)
        pair, other = [lax.ppermute(sent, "gx", s) for s in swaps("gx")]
        (sent,) = call(x_kernel, [box], sent, pair, other)
        pair, other = swaps("gy")
        other = lax.ppermute(sent, "gy", other)
        pair = lax.ppermute(sent, "gy", pair)
        return sent, pair, other

    def slow(first):
        (sent,) = call(slow_kernel, [group], first, *operands, scratch=True)
        old = first
        for number in range(ITERS - 1):
            body = functools.partial(step_kernel, number)
            sent, old = call(body, [group, state], exchange_all(sent), old, *operands, scratch=True)
        return tuple(call(last_kernel, [shape, shape], exchange_all(sent), old))

    (sent,) = call(start_kernel, [box], right_side)
    (size,) = call(size_kernel, [tile], gradient)
    vectors = []
    for number in range(6):
        near = exchange_near(sent, size if number == 0 else None)
        outs = [everyone if number == 5 else box, box] + [[], [], [], [box], [], [tile, box]][number]
        body = functools.partial(basis_kernel, number)
        sent, vector, *extra = call(body, outs, *near, *vectors, *operands, scratch=True)
        if number == 3:
            vectors[2] = extra[0]
        vectors.append(vector)
    arrived = lax.all_to_all(sent, ("gx", "gy", "gz"), 0, 0)
    *fast, good = call(fast_kernel, [shape, shape, None], arrived, *vectors, *extra)
    return lax.cond(good[0, 0] > 0, lambda first: tuple(fast), slow, vectors[0])


def solution(mesh):
    placed = P(None, "gz", "gx", "gy")
    return jax.shard_map(
        shards,
        mesh=mesh,
        in_specs=(placed, placed),
        out_specs=(placed, placed),
        check_vma=False,
    )
```

```python
import functools

import jax
import jax.numpy as jnp
import ml_dtypes
import numpy as np
from jax import lax
from jax.experimental import pallas as pl
from jax.experimental.pallas import tpu as pltpu
from jax.sharding import PartitionSpec as P

ITERS = 6
SMOOTHING = 0.5
DAMPING = 0.05
HIGHEST = lax.Precision.HIGHEST

CELLS_Z, CELLS_X, CELLS_Y = 4, 4, 16
BOX_X, BOX_Y, BOX_Z = 7, 19, 6
LANES = 128
ROWS = 24
DENOMINATOR = 3072.0
SCALE = 512.0
DAMP = DAMPING / SCALE
SHIFTS = (0.0, 0.171, 0.452, 0.776, 0.114)
WORST_PIVOT = 0.05
SPARE = ((4, 0, 76), (4, 1, 38), (5, 2, 76), (5, 3, 38))


def numerators(t):
    return (
        (8 - t) ** 3,
        3 * t**3 - 48 * t**2 + 2048,
        -3 * t**3 + 24 * t**2 + 192 * t + 512,
        t**3,
    )


WEIGHTS = [[n / DENOMINATOR for n in numerators(t)] for t in range(8)]


def basis(cells):
    table = np.zeros((8 * cells + 1, cells + 3 + 1))
    for voxel in range(8 * cells + 1):
        for k, n in enumerate(numerators(voxel % 8)):
            table[voxel, voxel // 8 + k] = n
    return table[:, :-1]


def mass_and_edges(cells, first, last):
    table = basis(cells) / DENOMINATOR
    own = table[:-1]
    steps = table[1:] - table[:-1]
    if last:
        steps[-1] = -table[-2]
    edges = steps.T @ steps
    if first:
        edges = edges + np.outer(table[0], table[0])
    return own.T @ own, edges


def place_z(matrix, part):
    return matrix[1:7, 1:7] if part == 0 else matrix[0:6, 0:6]


@functools.lru_cache(None)
def tables():
    bx = basis(CELLS_X)[:-1]
    expand = np.zeros((96, ROWS))
    for c in range(3):
        expand[c * 32 : c * 32 + 32, c * 8 : c * 8 + BOX_X] = bx / DENOMINATOR / DENOMINATOR
    rows_x = np.zeros((3, 144, ROWS), np.float32)
    for kind in range(3):
        mass, edges = mass_and_edges(CELLS_X, kind == 0, kind == 2)
        rows_x[kind, :96] = expand
        for c in range(3):
            at = slice(c * 8, c * 8 + BOX_X)
            rows_x[kind, 96 + c * 8 : 96 + c * 8 + BOX_X, at] = SMOOTHING / SCALE * mass
            rows_x[kind, 120 + c * 8 : 120 + c * 8 + BOX_X, at] = SMOOTHING / SCALE * edges
    by = basis(CELLS_Y)[:-1]
    along_y = np.zeros((2, 2, LANES, 7 * LANES))
    for part in range(2):
        for f in range(BOX_Z):
            g = f + 1 if part == 0 else f
            low = by.T.astype(ml_dtypes.bfloat16).astype(np.float64)
            at = slice(f * BOX_Y, (f + 1) * BOX_Y)
            along_y[part, 0, at, g * LANES : (g + 1) * LANES] = low
            along_y[part, 1, at, g * LANES : (g + 1) * LANES] = by.T - low
    along_y = along_y.reshape(2, 256, 7 * LANES).astype(ml_dtypes.bfloat16)
    lanes = np.zeros((2, 3, 256, LANES), np.float32)
    for part in range(2):
        mz, kz = mass_and_edges(CELLS_Z, part == 0, part == 1)
        mz, kz = place_z(mz, part), place_z(kz, part)
        for kind in range(3):
            my, ky = mass_and_edges(CELLS_Y, kind == 0, kind == 2)
            used = BOX_Z * BOX_Y
            lanes[part, kind, :used, :used] = np.kron(kz, my) + np.kron(mz, ky)
            lanes[part, kind, 128 : 128 + used, :used] = np.kron(mz, my)
    return (
        rows_x,
        (expand.T / SCALE).astype(np.float32),
        along_y,
        lanes.reshape(6, 256, LANES),
    )


def iotas():
    row = lax.broadcasted_iota(jnp.int32, (ROWS, LANES), 0)
    lane = lax.broadcasted_iota(jnp.int32, (ROWS, LANES), 1)
    f = jnp.zeros_like(lane)
    for k in range(1, BOX_Z + 1):
        f = f + (lane >= k * BOX_Y).astype(jnp.int32)
    return row & 7, f, lane - f * BOX_Y


def masks(where):
    (gx, nx), (gy, ny), (gz, nz) = where
    kx, f, e = iotas()
    low_x, high_x = jnp.where(gx == 0, 1, 0), jnp.where(gx == nx - 1, 4, 6)
    low_y, high_y = jnp.where(gy == 0, 1, 0), jnp.where(gy == ny - 1, 16, 18)
    high_z = jnp.where(gz == 0, 5, 4)
    inside = (kx >= low_x) & (kx <= high_x) & (e >= low_y) & (e <= high_y) & (f <= high_z)
    own_z = jnp.where(gz == 0, 0, 1)
    own = (kx >= 1) & (kx <= 4) & (e >= 1) & (e <= 16) & (f >= own_z) & (f <= own_z + 3)
    return inside.astype(jnp.float32), own.astype(jnp.float32)


def places():
    return tuple((lax.axis_index(a), lax.axis_size(a)) for a in ("gx", "gy", "gz"))


def add(a, b):
    return b if a is None else a if b is None else a + b


def split3(value):
    high = value.astype(jnp.bfloat16)
    rest = value - high.astype(jnp.float32)
    middle = rest.astype(jnp.bfloat16)
    low = (rest - middle.astype(jnp.float32)).astype(jnp.bfloat16)
    return jnp.concatenate([high, middle, low], axis=0)


def dot(a, b, dims=((1,), (0,)), precision=None):
    return lax.dot_general(
        a, b, (dims, ((), ())), precision=precision, preferred_element_type=jnp.float32
    )


def kind_of(index, count):
    return jnp.where(index == 0, 0, jnp.where(index == count - 1, 2, 1))


def apply_local(vector, grad_ref, rows_ref, back_ref, along_ref, lanes_ref, field_ref, sums_ref):
    first = dot(rows_ref[...], vector, precision=HIGHEST)
    pieces = split3(first[:96])
    field = dot(jnp.concatenate([pieces, pieces], axis=1), along_ref[...])
    field_ref[...] = field[:96] + field[96:192] + field[192:]

    def column(cx, carry):
        rows = [pl.ds(pl.multiple_of(c * 32 + cx * 8, 8), 8) for c in range(3)]
        inside = pl.ds(pl.multiple_of(cx * 8, 8), 8)
        total = [[None] * 4 for _ in range(3)]
        for cz in range(CELLS_Z):
            layer = [
                [field_ref[rows[c], (cz + k) * LANES : (cz + k + 1) * LANES] for k in range(4)]
                for c in range(3)
            ]

            def weighted(t, values):
                slope = [grad_ref[c, cz * 8 + t, inside, :] for c in range(3)]
                shade = slope[0] * values[0] + slope[1] * values[1] + slope[2] * values[2]
                return [slope[c] * shade for c in range(3)]

            edge, near = WEIGHTS[0][0], WEIGHTS[0][1]
            value = weighted(0, [edge * (v[0] + v[2]) + near * v[1] for v in layer])
            first = [edge * v for v in value]
            second = [near * v for v in value]
            outer = [v[0] + v[3] for v in layer]
            inner = [v[1] + v[2] for v in layer]
            outer_odd = [v[0] - v[3] for v in layer]
            inner_odd = [v[1] - v[2] for v in layer]
            edge, near = WEIGHTS[4][0], WEIGHTS[4][1]
            value = weighted(4, [edge * a + near * b for a, b in zip(outer, inner)])
            sums = [[edge * v, near * v, None, None] for v in value]
            for t in (1, 2, 3):
                w = WEIGHTS[t]
                a, b, p, q = (w[0] + w[3]) / 2, (w[1] + w[2]) / 2, (w[0] - w[3]) / 2, (w[1] - w[2]) / 2
                even = [a * outer[c] + b * inner[c] for c in range(3)]
                odd = [p * outer_odd[c] + q * inner_odd[c] for c in range(3)]
                one = weighted(t, [even[c] + odd[c] for c in range(3)])
                two = weighted(8 - t, [even[c] - odd[c] for c in range(3)])
                for c in range(3):
                    plus, minus = one[c] + two[c], one[c] - two[c]
                    terms = (a * plus, b * plus, p * minus, q * minus)
                    sums[c] = [add(x, y) for x, y in zip(sums[c], terms)]
            for c in range(3):
                outside, middle, outside_odd, middle_odd = sums[c]
                parts = (
                    outside + outside_odd + first[c],
                    middle + middle_odd + second[c],
                    middle - middle_odd + first[c],
                    outside - outside_odd,
                )
                total[c] = [add(x, y) for x, y in zip(total[c], parts)]
                sums_ref[rows[c], cz * LANES : (cz + 1) * LANES] = total[c][0]
                total[c] = total[c][1:] + [None]
        for c in range(3):
            for k in range(3):
                g = CELLS_Z + k
                sums_ref[rows[c], g * LANES : (g + 1) * LANES] = total[c][k]
        return carry

    lax.fori_loop(0, CELLS_X, column, 0, unroll=True)
    pieces = split3(sums_ref[...])
    back = dot(pieces, along_ref[...], ((1,), (1,)))
    back = back[:, :LANES] + back[:, LANES:]
    back = back[:96] + back[96:192] + back[192:]
    data = dot(back_ref[...], back, precision=HIGHEST)
    relief = dot(
        jnp.concatenate([first[96:120], first[120:144]], axis=1),
        lanes_ref[...],
        precision=HIGHEST,
    )
    return data + relief


def roll(value, shift, axis):
    return pltpu.roll(value, shift, axis)


def put():
    first_f = jnp.where(lax.axis_index("gz") == 0, 0, 1)
    row = lax.broadcasted_iota(jnp.int32, (64, LANES), 0)
    lane = lax.broadcasted_iota(jnp.int32, (64, LANES), 1)
    target = ((row >> 4) + first_f) * BOX_Y + 1 + (row & 15)
    return (lane == target).astype(jnp.float32).astype(jnp.bfloat16)


def start_kernel(right_ref, out_ref):
    parts = []
    for c in range(3):
        own = jnp.concatenate([right_ref[c, z] for z in range(CELLS_Z)], axis=1)
        parts += [jnp.zeros((1, 64), jnp.float32), own, jnp.zeros((3, 64), jnp.float32)]
    value = dot(split3(jnp.concatenate(parts, axis=0)), put())
    out_ref[...] = value[:ROWS] + value[ROWS : 2 * ROWS] + value[2 * ROWS :]


def size_kernel(grad_ref, out_ref):
    def plane(z, totals):
        totals = list(totals)
        for x in range(4):
            slope = [grad_ref[c, z, x * 8 : x * 8 + 8, :] for c in range(3)]
            k = 0
            for a in range(3):
                for b in range(a, 3):
                    totals[k] = totals[k] + slope[a] * slope[b]
                    k += 1
        return tuple(totals)

    zero = jnp.zeros((8, LANES), jnp.float32)
    totals = lax.fori_loop(0, 32, plane, (zero,) * 6)
    count = 32.0 * 32.0 * 128.0
    xx, xy, xz, yy, yz, zz = [
        jnp.sum(jnp.sum(t, axis=0, keepdims=True), axis=1, keepdims=True) / count for t in totals
    ]
    aa = xx * xx + xy * xy + xz * xz
    bb = xy * xy + yy * yy + yz * yz
    cc = xz * xz + yz * yz + zz * zz
    ab = xx * xy + xy * yy + xz * yz
    ac = xx * xz + xy * yz + xz * zz
    bc = xy * xz + yy * yz + yz * zz
    norm = aa * aa + bb * bb + cc * cc + 2.0 * (ab * ab + ac * ac + bc * bc)
    size = 0.73 * jnp.sqrt(jnp.sqrt(norm)) + 0.04
    row = lax.broadcasted_iota(jnp.int32, (8, LANES), 0)
    out_ref[...] = jnp.where(row == 7, jnp.broadcast_to(size, (8, LANES)), 0.0)


def with_size(value, *others):
    row = lax.broadcasted_iota(jnp.int32, (ROWS, LANES), 0)
    return jnp.where(row == 7, functools.reduce(jnp.maximum, others), value)


def pair_sides(index, pair, other):
    even = lax.rem(index, 2) == 0
    return jnp.where(even, other, pair), jnp.where(even, pair, other)


def z_kernel(mine_ref, swap_ref, out_ref):
    gz = lax.axis_index("gz")
    _, f, _ = iotas()
    mine, swap = mine_ref[...], swap_ref[...]
    other = roll(swap, jnp.where(gz == 0, 3 * BOX_Y, LANES - 3 * BOX_Y), 1)
    first_f = jnp.where(gz == 0, 3, 0)
    value = mine + jnp.where((f >= first_f) & (f <= first_f + 2), other, 0.0)
    out_ref[...] = with_size(value, mine, swap)


def x_kernel(mine_ref, pair_ref, other_ref, *rest):
    out_ref = rest[-1]
    gx, nx = lax.axis_index("gx"), lax.axis_size("gx")
    kx, _, _ = iotas()
    mine, pair, other = mine_ref[...], pair_ref[...], other_ref[...]
    low, high = pair_sides(gx, pair, other)
    first_x, last_x = jnp.where(gx > 0, 2, -1), jnp.where(gx < nx - 1, 4, 8)
    value = mine + jnp.where(kx <= first_x, rows_rolled(low, 4), 0.0)
    value = value + jnp.where((kx >= last_x) & (kx <= 6), rows_rolled(high, 4), 0.0)
    out_ref[...] = with_size(value, mine, pair, other)


def x_first_kernel(mine_ref, size_ref, out_ref):
    out_ref[...] = mine_ref[...]
    row = lax.broadcasted_iota(jnp.int32, (8, LANES), 0)
    out_ref[0:8] = jnp.where(row == 7, size_ref[...], mine_ref[0:8])


def y_sum(mine_ref, pair_ref, other_ref):
    gy, ny = lax.axis_index("gy"), lax.axis_size("gy")
    _, _, e = iotas()
    mine, pair, other = mine_ref[...], pair_ref[...], other_ref[...]
    low, high = pair_sides(gy, pair, other)
    first_y, last_y = jnp.where(gy > 0, 2, -1), jnp.where(gy < ny - 1, 16, LANES)
    value = mine + jnp.where(e <= first_y, roll(low, LANES - 16, 1), 0.0)
    value = value + jnp.where(e >= last_y, roll(high, 16, 1), 0.0)
    return value, jnp.maximum(jnp.maximum(mine, pair), other)[7:8]


def rows_rolled(value, shift):
    return jnp.concatenate(
        [roll(value[c * 8 : c * 8 + 8], shift, 0) for c in range(3)], axis=0
    )


def middle_kernel(in_ref, out_ref):
    (gx, nx), _, (gz, nz) = places()
    kx, f, e = iotas()
    has_low = (gx > 0).astype(jnp.int32)
    has_high = (gx < nx - 1).astype(jnp.int32)
    low = jnp.maximum(gx - 1, 0)
    high = jnp.minimum(gx + 1, nx - 1)
    take_low = (kx <= 2) & (has_low == 1)
    take_high = (kx >= 4) & (kx <= 6) & (has_high == 1)

    def along_x(part):
        value = in_ref[gx * nz + part]
        below = rows_rolled(in_ref[low * nz + part], 4)
        above = rows_rolled(in_ref[high * nz + part], 4)
        value = value + jnp.where(take_low, below, 0.0)
        return value + jnp.where(take_high, above, 0.0)

    mine = along_x(gz)
    other = along_x(1 - gz)
    other = roll(other, jnp.where(gz == 0, 3 * BOX_Y, LANES - 3 * BOX_Y), 1)
    first_f = jnp.where(gz == 0, 3, 0)
    value = mine + jnp.where((f >= first_f) & (f <= first_f + 2), other, 0.0)
    everything = in_ref[0]
    for i in range(1, in_ref.shape[0]):
        everything = everything + in_ref[i]
    value = jnp.where(kx == 7, everything, value)
    for i in range(out_ref.shape[0]):
        out_ref[i] = value


def along_y_sum(in_ref):
    _, (gy, ny), _ = places()
    kx, f, e = iotas()
    has_low = (gy > 0).astype(jnp.int32)
    has_high = (gy < ny - 1).astype(jnp.int32)
    below = roll(in_ref[jnp.maximum(gy - 1, 0)], LANES - 16, 1)
    above = roll(in_ref[jnp.minimum(gy + 1, ny - 1)], 16, 1)
    value = in_ref[gy]
    value = value + jnp.where((e <= 2) & (has_low == 1), below, 0.0)
    value = value + jnp.where((e >= 16) & (has_high == 1), above, 0.0)
    everything = in_ref[0]
    for i in range(1, in_ref.shape[0]):
        everything = everything + in_ref[i]
    return value, everything


def message(vector, image, own, out_ref):
    norm = jnp.sum(own * vector * vector, axis=0, keepdims=True)
    product = jnp.sum(vector * image, axis=0, keepdims=True)
    row = lax.broadcasted_iota(jnp.int32, (ROWS, LANES), 0)
    value = jnp.where(row == 7, norm, image)
    value = jnp.where(row == 15, product, value)
    for i in range(out_ref.shape[0]):
        out_ref[i] = value


def total_of(in_ref):
    values = [in_ref[i] for i in range(in_ref.shape[0])]
    while len(values) > 1:
        values = [a + b for a, b in zip(values[::2], values[1::2])]
    return values[0]


def tile_parts():
    kx, f, e = (v[0:8] for v in iotas())
    return kx, f, e, lax.broadcasted_iota(jnp.int32, (8, LANES), 1)


def own_parts(image, line, out_ref):
    (gx, nx), (gy, ny), (gz, nz) = places()
    row, f, e, lane = tile_parts()
    parts = [image[c * 8 : c * 8 + 8] for c in range(3)]
    six = jnp.zeros((8, LANES), jnp.float32)
    before, other_z, beside_y = six, six, six
    layers = 2 * BOX_Y
    start = jnp.where(gz == 0, 4 * BOX_Y, 0)
    for c, part in enumerate(parts):
        here = (row == 2 * c) | (row == 2 * c + 1)
        six = jnp.where(here, roll(part, (2 * c + 3) % 8, 0), six)
        before = jnp.where(row == c, roll(part, c, 0), before)
        part = roll(part, 7, 0)
        packed = roll(part, lax.rem(layers * c - start + LANES, LANES), 1)
        other_z = jnp.where((lane >= layers * c) & (lane < layers * c + layers), packed, other_z)
        beside_y = jnp.where(e == c, roll(part, c, 1), beside_y)
        here = (e == 17 - 2 * c) | (e == 18 - 2 * c)
        beside_y = jnp.where(here, roll(part, (LANES - 2 * c) % LANES, 1), beside_y)
    own = roll(six, jnp.where(gz == 0, 0, LANES - BOX_Y), 1)
    after = own
    for source, target, shift in SPARE:
        moved = roll(roll(own, (target - source) % 8, 0), shift, 1)
        after = jnp.where((row == target) & (lane >= 2 * layers), moved, after)
    own = roll(six, jnp.where(gz == 0, LANES - 4 * BOX_Y, 0), 1)
    after_z = jnp.where(lane < layers, own, roll(roll(own, 4, 0), layers, 1))
    values = (after, after_z, before, other_z, beside_y)
    scalars = jnp.where(row == 0, roll(line, 114, 1), roll(line, 100, 1))
    after, after_z, before, other_z, beside_y = [
        jnp.where(lane >= BOX_Z * BOX_Y, scalars, v)[0:4] for v in values
    ]
    for x in range(nx):
        for z in range(nz):
            same = gz == z
            value = jnp.where(gx == x, jnp.where(same, beside_y, other_z), before)
            value = jnp.where(gx + 1 == x, jnp.where(same, after, after_z), value)
            for y in range(ny):
                out_ref[(x * ny + y) * nz + z] = value


def own_sum(image, in_ref):
    (gx, nx), (gy, ny), (gz, nz) = places()
    row, f, e, lane = tile_parts()
    lower_y, upper_y = gy > 0, gy < ny - 1
    below_y, above_y = jnp.maximum(gy - 1, 0), jnp.minimum(gy + 1, ny - 1)
    below_mask = ((e == 1) | (e == 2)) & lower_y
    above_mask = (e == 16) & upper_y
    first_f, last_f = jnp.where(gz == 0, 3, 1), jnp.where(gz == 0, 3, 2)
    z_mask = (f >= first_f) & (f <= last_f)
    nothing = jnp.zeros((4, LANES), jnp.float32)

    def tile(x, y, z):
        return jnp.concatenate([in_ref[(x * ny + y) * nz + z], nothing], axis=0)

    def over_y(x, z):
        value = tile(x, gy, z)
        value = value + jnp.where(below_mask, roll(tile(x, below_y, z), LANES - 16, 1), 0.0)
        return value + jnp.where(above_mask, roll(tile(x, above_y, z), 16, 1), 0.0)

    layers = 2 * BOX_Y
    z_start = jnp.where(gz == 0, 3 * BOX_Y, BOX_Y)
    packed = over_y(jnp.maximum(gx - 1, 0), gz)
    six = packed
    for source, target, shift in SPARE:
        moved = roll(roll(packed, (source - target) % 8, 0), LANES - shift, 1)
        first = 2 * layers - shift
        six = jnp.where((row == source) & (lane >= first) & (lane < first + layers), moved, six)
    six = roll(six, jnp.where(gz == 0, 0, BOX_Y), 1)
    packed = over_y(jnp.maximum(gx - 1, 0), 1 - gz)
    moved = jnp.where(row < 4, packed, roll(roll(packed, 4, 0), LANES - layers, 1))
    from_before = six + jnp.where(z_mask, roll(moved, z_start, 1), 0.0)
    above_x = jnp.minimum(gx + 1, nx - 1)
    moved = roll(over_y(above_x, 1 - gz), jnp.where(gz == 0, 3 * BOX_Y, LANES - 3 * BOX_Y), 1)
    from_after = over_y(above_x, gz) + jnp.where(z_mask, moved, 0.0)
    from_z = roll(over_y(gx, 1 - gz), 1, 0)
    from_below, from_above = roll(tile(gx, below_y, gz), 1, 0), roll(tile(gx, above_y, gz), 1, 0)
    own_rows = (row >= 1) & (row <= 4)
    sums = []
    for c in range(3):
        value = image[c * 8 : c * 8 + 8]
        here = ((row == 1) | (row == 2)) & (gx > 0)
        value = value + jnp.where(here, roll(from_before, (1 - 2 * c) % 8, 0), 0.0)
        here = (row == 4) & (gx < nx - 1)
        value = value + jnp.where(here, roll(from_after, 4 - c, 0), 0.0)
        moved = roll(from_z, lax.rem(z_start - layers * c + LANES, LANES), 1)
        value = value + jnp.where(own_rows & z_mask, moved, 0.0)
        moved = roll(from_below, LANES - 16 + 2 * c, 1)
        value = value + jnp.where(own_rows & below_mask, moved, 0.0)
        moved = roll(from_above, 16 - c, 1)
        value = value + jnp.where(own_rows & above_mask, moved, 0.0)
        sums.append(value)
    return jnp.concatenate(sums, axis=0)


def row_sums(products, rows):
    sums = [jnp.sum(p, axis=0, keepdims=True) for p in products]
    return jnp.concatenate(sums + [jnp.zeros((rows - len(sums), LANES), jnp.float32)], axis=0)


def early_kernel(*refs):
    _, own = masks(places())
    vectors = [ref[...] for ref in refs[:5]]
    products = []
    for i in range(5):
        mine = own * vectors[i]
        products += [mine * vectors[j] for j in range(i, 5)]
    refs[5][...] = row_sums(products, 16)


def basis_kernel(number, mine_ref, pair_ref, other_ref, *refs):
    past = refs[:number]
    early_ref, refs = (refs[number], refs[1:]) if number == 5 else (None, refs)
    operands = refs[number : number + 5]
    out_ref, *new_refs, field_ref, sums_ref = refs[number + 5 :]
    inside, own = masks(places())
    value, size = y_sum(mine_ref, pair_ref, other_ref)
    value = value * inside
    if number:
        value = value + DAMP * past[-1][...]
    if number == 3:
        inverse = 1.0 / size
        one, two = past[1][...], past[2][...]
        second = inverse * two - SHIFTS[1] * one
        value = inverse * (inverse * value - SHIFTS[1] * two) - SHIFTS[2] * second
        new_refs[1][...] = second
    elif number > 3:
        value = value / size - SHIFTS[number - 1] * past[-1][...]
    new_refs[0][...] = value
    image = apply_local(value, *operands, field_ref, sums_ref) * inside
    if number < 5:
        out_ref[...] = with_size(image, jnp.broadcast_to(size, (ROWS, LANES)))
        return
    new_refs[1][...] = jnp.broadcast_to(size, (8, LANES))
    mine = own * value
    late = [mine * ref[...] for ref in past] + [mine * value]
    late.append(value * image + DAMP * late[5])
    sums = jnp.concatenate([early_ref[...], row_sums(late, 8)], axis=0)
    sums = jnp.sum(sums, axis=1, keepdims=True)
    row = lax.broadcasted_iota(jnp.int32, (ROWS, LANES), 0)
    lane = lax.broadcasted_iota(jnp.int32, (ROWS, LANES), 1)
    line = jnp.sum(jnp.where(row == lane, sums, 0.0), axis=0, keepdims=True)
    own_parts(image, line, out_ref)
    new_refs[2][...] = image


def times(a, b):
    return None if a is None or b is None else a * b


def form(left, table, right):
    total = None
    for i, a in enumerate(left):
        inner = None
        for j, b in enumerate(right):
            inner = add(inner, times(table[i][j], b))
        total = add(total, times(a, inner))
    return total


def fast_kernel(in_ref, *refs):
    vectors = [ref[...] for ref in refs[:6]]
    size_ref, last_ref, solution_ref, residual_ref, good_ref = refs[6:]
    inside, _ = masks(places())
    value = own_sum(last_ref[...], in_ref)
    size = size_ref[0:1, 0:1]
    inverse = 1.0 / size
    image = (value * inside + DAMP * vectors[5]) * inverse
    total = total_of(in_ref)
    lane = lax.broadcasted_iota(jnp.int32, (1, LANES), 1)
    scalars = []
    for k in range(23):
        row, at = (0, 114 + k) if k < 14 else (1, 100 + k)
        scalars.append(jnp.sum(jnp.where(lane == at, total[row : row + 1], 0.0), axis=1, keepdims=True))
    gram = [[None] * 6 for _ in range(6)]
    k = 0
    for i in range(5):
        for j in range(i, 5):
            gram[i][j] = gram[j][i] = scalars[k]
            k += 1
    for i in range(6):
        gram[i][5] = gram[5][i] = scalars[16 + i]
    factor = [inverse] + [jnp.ones_like(inverse)] * 4
    energy = [[None] * 6 for _ in range(6)]
    for i in range(5):
        for j in range(i, 6):
            energy[i][j] = energy[j][i] = factor[i] * (gram[i + 1][j] + SHIFTS[i] * gram[i][j])
    energy[5][5] = scalars[22] * inverse
    rest = [row[:] for row in gram]
    good = jnp.ones_like(inverse)
    for k in range(6):
        good = jnp.where(rest[k][k] / gram[k][k] > WORST_PIVOT, good, 0.0)
        for i in range(k + 1, 6):
            ratio = rest[i][k] / rest[k][k]
            for j in range(i, 6):
                rest[i][j] = rest[i][j] - ratio * rest[k][j]
                rest[j][i] = rest[i][j]
    good_ref[0, 0] = jnp.sum(good).astype(jnp.int32)
    solved = [None] * 7
    residual = [jnp.ones_like(inverse)] + [None] * 6
    direction = residual[:]
    norm = gram[0][0]
    for number in range(ITERS):
        known = number + 1
        moved = [None] * 7
        for j in range(known):
            if j == 5:
                moved[6] = add(moved[6], direction[5])
            else:
                part = factor[j] * direction[j]
                moved[j + 1] = add(moved[j + 1], part)
                moved[j] = add(moved[j], SHIFTS[j] * part)
        step = norm / form(direction[:known], energy, direction[:known])
        solved = [add(a, times(step, b)) for a, b in zip(solved, direction)]
        residual = [add(a, times(-step, b)) for a, b in zip(residual, moved)]
        if number < ITERS - 1:
            known += 1
            later = form(residual[:known], gram, residual[:known])
            ratio = later / norm
            direction = [add(a, times(ratio, b)) for a, b in zip(residual, direction)]
            norm = later
    vectors = vectors + [image]
    first, second = None, None
    for j in range(7):
        if solved[j] is not None:
            first = add(first, solved[j] * vectors[j])
        second = add(second, residual[j] * vectors[j])
    write_out(first * (inverse / SCALE), second, solution_ref, residual_ref)


def write_out(solved, residual, solution_ref, residual_ref):
    both = jnp.concatenate([solved, residual], axis=0)
    value = dot(split3(both), put(), ((1,), (1,)))
    value = value[:48] + value[48:96] + value[96:]
    for z in range(CELLS_Z):
        for c in range(3):
            solution_ref[c, z] = value[c * 8 + 1 : c * 8 + 5, z * 16 : z * 16 + 16]
            residual_ref[c, z] = value[ROWS + c * 8 + 1 : ROWS + c * 8 + 5, z * 16 : z * 16 + 16]


def slow_kernel(vector_ref, grad_ref, rows_ref, back_ref, along_ref, lanes_ref, out_ref, field_ref, sums_ref):
    inside, own = masks(places())
    vector = vector_ref[...]
    image = apply_local(vector, grad_ref, rows_ref, back_ref, along_ref, lanes_ref, field_ref, sums_ref)
    message(vector, image * inside, own, out_ref)


def update(in_ref, old_ref, number):
    inside, own = masks(places())
    value, everything = along_y_sum(in_ref)
    residual = old_ref[ROWS : 2 * ROWS] if number else old_ref[...]
    image = value * inside + DAMP * residual
    norm = jnp.sum(everything[7:8], axis=1, keepdims=True)
    product = jnp.sum(everything[15:16], axis=1, keepdims=True) + DAMP * norm
    if number:
        ratio = norm / old_ref[4 * ROWS : 4 * ROWS + 1, 0:1]
        step = norm / (product - ratio * norm / old_ref[4 * ROWS + 1 : 4 * ROWS + 2, 0:1])
        direction = residual + ratio * old_ref[2 * ROWS : 3 * ROWS]
        image = image + ratio * old_ref[3 * ROWS : 4 * ROWS]
        solved = old_ref[0:ROWS] + step * direction
    else:
        step = norm / product
        direction = residual
        solved = step * direction
    residual = residual - step * image
    return own, inside, solved, residual, direction, image, norm, step


def step_kernel(number, in_ref, old_ref, grad_ref, rows_ref, back_ref, along_ref, lanes_ref, out_ref, new_ref, field_ref, sums_ref):
    own, inside, solved, residual, direction, image, norm, step = update(in_ref, old_ref, number)
    new_ref[0:ROWS] = solved
    new_ref[ROWS : 2 * ROWS] = residual
    new_ref[2 * ROWS : 3 * ROWS] = direction
    new_ref[3 * ROWS : 4 * ROWS] = image
    row = lax.broadcasted_iota(jnp.int32, (8, LANES), 0)
    new_ref[4 * ROWS : 4 * ROWS + 8] = jnp.where(row == 0, norm, step)
    image = apply_local(residual, grad_ref, rows_ref, back_ref, along_ref, lanes_ref, field_ref, sums_ref)
    message(residual, image * inside, own, out_ref)


def last_kernel(in_ref, old_ref, solution_ref, residual_ref):
    _, _, solved, residual, _, _, _, _ = update(in_ref, old_ref, ITERS - 1)
    write_out(solved / SCALE, residual, solution_ref, residual_ref)


def call(body, outs, *args, scratch=False):
    shapes = [
        jax.ShapeDtypeStruct(s, jnp.float32) if s else jax.ShapeDtypeStruct((1, 1), jnp.int32)
        for s in outs
    ]
    scratch_shapes = [pltpu.VMEM((96, 7 * LANES), jnp.float32)] * 2 if scratch else []
    vmem = pl.BlockSpec(memory_space=pltpu.VMEM)
    return pl.pallas_call(
        body,
        out_shape=shapes,
        in_specs=[vmem] * len(args),
        out_specs=[vmem if s else pl.BlockSpec(memory_space=pltpu.SMEM) for s in outs],
        scratch_shapes=scratch_shapes,
        compiler_params=pltpu.CompilerParams(vmem_limit_bytes=24 * 1024 * 1024),
    )(*args)


def swaps(axis):
    count = lax.axis_size(axis)
    pair = [(i, i ^ 1) for i in range(count)]
    other = [(i, (i + 1 if i % 2 else i - 1) % count) for i in range(count)]
    return pair, other


def shards(gradient, right_side):
    (gx, nx), (gy, ny), (gz, nz) = places()
    rows_x, back_x, along_y, lanes = [jnp.asarray(t) for t in tables()]
    rows_x = lax.dynamic_index_in_dim(rows_x, kind_of(gx, nx), 0, keepdims=False)
    along_y = lax.dynamic_index_in_dim(along_y, gz, 0, keepdims=False)
    lanes = lax.dynamic_index_in_dim(lanes, gz * 3 + kind_of(gy, ny), 0, keepdims=False)
    operands = (gradient, rows_x, back_x, along_y, lanes)
    group, line, box = (nx * nz, ROWS, LANES), (ny, ROWS, LANES), (ROWS, LANES)
    everyone = (nx * ny * nz, 4, LANES)
    tile, state, shape = (8, LANES), (4 * ROWS + 8, LANES), right_side.shape

    def exchange_all(sent):
        near = lax.all_to_all(sent, ("gx", "gz"), 0, 0)
        (sent,) = call(middle_kernel, [line], near)
        return lax.all_to_all(sent, "gy", 0, 0)

    def exchange_near(sent, size=None):
        swapped = lax.ppermute(sent, "gz", swaps("gz")[0])
        (sent,) = call(z_kernel, [box], sent, swapped)
        if size is not None:
            (sent,) = call(x_first_kernel, [box], sent, size)
        pair, other = [lax.ppermute(sent, "gx", s) for s in swaps("gx")]
        (sent,) = call(x_kernel, [box], sent, pair, other)
        pair, other = swaps("gy")
        other = lax.ppermute(sent, "gy", other)
        pair = lax.ppermute(sent, "gy", pair)
        return sent, pair, other

    def slow(first):
        (sent,) = call(slow_kernel, [group], first, *operands, scratch=True)
        old = first
        for number in range(ITERS - 1):
            body = functools.partial(step_kernel, number)
            sent, old = call(body, [group, state], exchange_all(sent), old, *operands, scratch=True)
        return tuple(call(last_kernel, [shape, shape], exchange_all(sent), old))

    (sent,) = call(start_kernel, [box], right_side)
    (size,) = call(size_kernel, [tile], gradient)
    vectors = []
    for number in range(6):
        near = exchange_near(sent, size if number == 0 else None)
        outs = [everyone if number == 5 else box, box] + [[], [], [], [box], [], [tile, box]][number]
        body = functools.partial(basis_kernel, number)
        early = call(early_kernel, [(16, LANES)], *vectors) if number == 5 else []
        sent, vector, *extra = call(
            body, outs, *near, *vectors, *early, *operands, scratch=True
        )
        if number == 3:
            vectors[2] = extra[0]
        vectors.append(vector)
    arrived = lax.all_to_all(sent, ("gx", "gy", "gz"), 0, 0)
    *fast, good = call(fast_kernel, [shape, shape, None], arrived, *vectors, *extra)
    return lax.cond(good[0, 0] > 0, lambda first: tuple(fast), slow, vectors[0])


def solution(mesh):
    placed = P(None, "gz", "gx", "gy")
    return jax.shard_map(
        shards,
        mesh=mesh,
        in_specs=(placed, placed),
        out_specs=(placed, placed),
        check_vma=False,
    )
```

```python
import functools

import jax
import jax.numpy as jnp
import ml_dtypes
import numpy as np
from jax import lax
from jax.experimental import pallas as pl
from jax.experimental.pallas import tpu as pltpu
from jax.sharding import PartitionSpec as P

ITERS = 6
SMOOTHING = 0.5
DAMPING = 0.05
HIGHEST = lax.Precision.HIGHEST

CELLS_Z, CELLS_X, CELLS_Y = 4, 4, 16
BOX_X, BOX_Y, BOX_Z = 7, 19, 6
LANES = 128
ROWS = 24
DENOMINATOR = 3072.0
SCALE = 512.0
DAMP = DAMPING / SCALE
SHIFTS = (0.0, 0.171, 0.452, 0.776, 0.114)
WORST_PIVOT = 0.05
SPARE = ((4, 0, 76), (4, 1, 38), (5, 2, 76), (5, 3, 38))


def numerators(t):
    return (
        (8 - t) ** 3,
        3 * t**3 - 48 * t**2 + 2048,
        -3 * t**3 + 24 * t**2 + 192 * t + 512,
        t**3,
    )


WEIGHTS = [[n / DENOMINATOR for n in numerators(t)] for t in range(8)]


def basis(cells):
    table = np.zeros((8 * cells + 1, cells + 3 + 1))
    for voxel in range(8 * cells + 1):
        for k, n in enumerate(numerators(voxel % 8)):
            table[voxel, voxel // 8 + k] = n
    return table[:, :-1]


def mass_and_edges(cells, first, last):
    table = basis(cells) / DENOMINATOR
    own = table[:-1]
    steps = table[1:] - table[:-1]
    if last:
        steps[-1] = -table[-2]
    edges = steps.T @ steps
    if first:
        edges = edges + np.outer(table[0], table[0])
    return own.T @ own, edges


def place_z(matrix, part):
    return matrix[1:7, 1:7] if part == 0 else matrix[0:6, 0:6]


def stacked(table):
    high = table.astype(ml_dtypes.bfloat16)
    rest = table - high.astype(table.dtype)
    middle = rest.astype(ml_dtypes.bfloat16)
    low = (rest - middle.astype(table.dtype)).astype(ml_dtypes.bfloat16)
    return np.concatenate([high, high, high, middle, middle, low], axis=-1)


@functools.lru_cache(None)
def tables():
    bx = basis(CELLS_X)[:-1]
    expand = np.zeros((96, ROWS))
    for c in range(3):
        expand[c * 32 : c * 32 + 32, c * 8 : c * 8 + BOX_X] = bx / DENOMINATOR / DENOMINATOR
    rows_x = np.zeros((3, 144, ROWS), np.float32)
    for kind in range(3):
        mass, edges = mass_and_edges(CELLS_X, kind == 0, kind == 2)
        rows_x[kind, :96] = expand
        for c in range(3):
            at = slice(c * 8, c * 8 + BOX_X)
            rows_x[kind, 96 + c * 8 : 96 + c * 8 + BOX_X, at] = SMOOTHING / SCALE * mass
            rows_x[kind, 120 + c * 8 : 120 + c * 8 + BOX_X, at] = SMOOTHING / SCALE * edges
    by = basis(CELLS_Y)[:-1]
    along_y = np.zeros((2, 2, LANES, 7 * LANES))
    for part in range(2):
        for f in range(BOX_Z):
            g = f + 1 if part == 0 else f
            low = by.T.astype(ml_dtypes.bfloat16).astype(np.float64)
            at = slice(f * BOX_Y, (f + 1) * BOX_Y)
            along_y[part, 0, at, g * LANES : (g + 1) * LANES] = low
            along_y[part, 1, at, g * LANES : (g + 1) * LANES] = by.T - low
    along_y = along_y.reshape(2, 256, 7 * LANES).astype(ml_dtypes.bfloat16)
    lanes = np.zeros((2, 3, 256, LANES), np.float32)
    for part in range(2):
        mz, kz = mass_and_edges(CELLS_Z, part == 0, part == 1)
        mz, kz = place_z(mz, part), place_z(kz, part)
        for kind in range(3):
            my, ky = mass_and_edges(CELLS_Y, kind == 0, kind == 2)
            used = BOX_Z * BOX_Y
            lanes[part, kind, :used, :used] = np.kron(kz, my) + np.kron(mz, ky)
            lanes[part, kind, 128 : 128 + used, :used] = np.kron(mz, my)
    return (
        stacked(rows_x.astype(np.float64)),
        stacked(expand.T / SCALE),
        along_y,
        lanes.reshape(6, 256, LANES),
    )


def iotas():
    row = lax.broadcasted_iota(jnp.int32, (ROWS, LANES), 0)
    lane = lax.broadcasted_iota(jnp.int32, (ROWS, LANES), 1)
    f = jnp.zeros_like(lane)
    for k in range(1, BOX_Z + 1):
        f = f + (lane >= k * BOX_Y).astype(jnp.int32)
    return row & 7, f, lane - f * BOX_Y


def masks(where):
    (gx, nx), (gy, ny), (gz, nz) = where
    kx, f, e = iotas()
    low_x, high_x = jnp.where(gx == 0, 1, 0), jnp.where(gx == nx - 1, 4, 6)
    low_y, high_y = jnp.where(gy == 0, 1, 0), jnp.where(gy == ny - 1, 16, 18)
    high_z = jnp.where(gz == 0, 5, 4)
    inside = (kx >= low_x) & (kx <= high_x) & (e >= low_y) & (e <= high_y) & (f <= high_z)
    own_z = jnp.where(gz == 0, 0, 1)
    own = (kx >= 1) & (kx <= 4) & (e >= 1) & (e <= 16) & (f >= own_z) & (f <= own_z + 3)
    return inside.astype(jnp.float32), own.astype(jnp.float32)


def places():
    return tuple((lax.axis_index(a), lax.axis_size(a)) for a in ("gx", "gy", "gz"))


def add(a, b):
    return b if a is None else a if b is None else a + b


def split3(value):
    high = value.astype(jnp.bfloat16)
    rest = value - high.astype(jnp.float32)
    middle = rest.astype(jnp.bfloat16)
    low = (rest - middle.astype(jnp.float32)).astype(jnp.bfloat16)
    return jnp.concatenate([high, middle, low], axis=0)


def pieces6(value):
    pieces = split3(value)
    count = value.shape[0]
    return jnp.concatenate([pieces, pieces[: 2 * count], pieces[:count]], axis=0)


def dot(a, b, dims=((1,), (0,)), precision=None):
    return lax.dot_general(
        a, b, (dims, ((), ())), precision=precision, preferred_element_type=jnp.float32
    )


def kind_of(index, count):
    return jnp.where(index == 0, 0, jnp.where(index == count - 1, 2, 1))


def apply_local(vector, grad_ref, rows_ref, back_ref, along_ref, lanes_ref, field_ref, sums_ref):
    first = dot(rows_ref[...], pieces6(vector))
    pieces = split3(first[:96])
    field = dot(jnp.concatenate([pieces, pieces], axis=1), along_ref[...])
    field_ref[...] = field[:96] + field[96:192] + field[192:]

    def column(cx, carry):
        rows = [pl.ds(pl.multiple_of(c * 32 + cx * 8, 8), 8) for c in range(3)]
        inside = pl.ds(pl.multiple_of(cx * 8, 8), 8)
        total = [[None] * 4 for _ in range(3)]
        for cz in range(CELLS_Z):
            layer = [
                [field_ref[rows[c], (cz + k) * LANES : (cz + k + 1) * LANES] for k in range(4)]
                for c in range(3)
            ]

            def weighted(t, values):
                slope = [grad_ref[c, cz * 8 + t, inside, :] for c in range(3)]
                shade = slope[0] * values[0] + slope[1] * values[1] + slope[2] * values[2]
                return [slope[c] * shade for c in range(3)]

            edge, near = WEIGHTS[0][0], WEIGHTS[0][1]
            value = weighted(0, [edge * (v[0] + v[2]) + near * v[1] for v in layer])
            first = [edge * v for v in value]
            second = [near * v for v in value]
            outer = [v[0] + v[3] for v in layer]
            inner = [v[1] + v[2] for v in layer]
            outer_odd = [v[0] - v[3] for v in layer]
            inner_odd = [v[1] - v[2] for v in layer]
            edge, near = WEIGHTS[4][0], WEIGHTS[4][1]
            value = weighted(4, [edge * a + near * b for a, b in zip(outer, inner)])
            sums = [[edge * v, near * v, None, None] for v in value]
            for t in (1, 2, 3):
                w = WEIGHTS[t]
                a, b, p, q = (w[0] + w[3]) / 2, (w[1] + w[2]) / 2, (w[0] - w[3]) / 2, (w[1] - w[2]) / 2
                even = [a * outer[c] + b * inner[c] for c in range(3)]
                odd = [p * outer_odd[c] + q * inner_odd[c] for c in range(3)]
                one = weighted(t, [even[c] + odd[c] for c in range(3)])
                two = weighted(8 - t, [even[c] - odd[c] for c in range(3)])
                for c in range(3):
                    plus, minus = one[c] + two[c], one[c] - two[c]
                    terms = (a * plus, b * plus, p * minus, q * minus)
                    sums[c] = [add(x, y) for x, y in zip(sums[c], terms)]
            for c in range(3):
                outside, middle, outside_odd, middle_odd = sums[c]
                parts = (
                    outside + outside_odd + first[c],
                    middle + middle_odd + second[c],
                    middle - middle_odd + first[c],
                    outside - outside_odd,
                )
                total[c] = [add(x, y) for x, y in zip(total[c], parts)]
                sums_ref[rows[c], cz * LANES : (cz + 1) * LANES] = total[c][0]
                total[c] = total[c][1:] + [None]
        for c in range(3):
            for k in range(3):
                g = CELLS_Z + k
                sums_ref[rows[c], g * LANES : (g + 1) * LANES] = total[c][k]
        return carry

    lax.fori_loop(0, CELLS_X, column, 0, unroll=True)
    pieces = split3(sums_ref[...])[:192]
    back = dot(pieces, along_ref[...], ((1,), (1,)))
    back = back[:, :LANES] + back[:, LANES:]
    back = back[:96] + back[96:192]
    data = dot(back_ref[...], pieces6(back))
    relief = dot(
        jnp.concatenate([first[96:120], first[120:144]], axis=1),
        lanes_ref[...],
        precision=HIGHEST,
    )
    return data + relief


def roll(value, shift, axis):
    return pltpu.roll(value, shift, axis)


def put():
    first_f = jnp.where(lax.axis_index("gz") == 0, 0, 1)
    row = lax.broadcasted_iota(jnp.int32, (64, LANES), 0)
    lane = lax.broadcasted_iota(jnp.int32, (64, LANES), 1)
    target = ((row >> 4) + first_f) * BOX_Y + 1 + (row & 15)
    return (lane == target).astype(jnp.float32).astype(jnp.bfloat16)


def start_kernel(right_ref, out_ref):
    parts = []
    for c in range(3):
        own = jnp.concatenate([right_ref[c, z] for z in range(CELLS_Z)], axis=1)
        parts += [jnp.zeros((1, 64), jnp.float32), own, jnp.zeros((3, 64), jnp.float32)]
    value = dot(split3(jnp.concatenate(parts, axis=0)), put())
    out_ref[...] = value[:ROWS] + value[ROWS : 2 * ROWS] + value[2 * ROWS :]


def size_kernel(grad_ref, out_ref):
    def plane(z, totals):
        totals = list(totals)
        for x in range(4):
            slope = [grad_ref[c, z, x * 8 : x * 8 + 8, :] for c in range(3)]
            k = 0
            for a in range(3):
                for b in range(a, 3):
                    totals[k] = totals[k] + slope[a] * slope[b]
                    k += 1
        return tuple(totals)

    zero = jnp.zeros((8, LANES), jnp.float32)
    totals = lax.fori_loop(0, 32, plane, (zero,) * 6)
    count = 32.0 * 32.0 * 128.0
    xx, xy, xz, yy, yz, zz = [
        jnp.sum(jnp.sum(t, axis=0, keepdims=True), axis=1, keepdims=True) / count for t in totals
    ]
    aa = xx * xx + xy * xy + xz * xz
    bb = xy * xy + yy * yy + yz * yz
    cc = xz * xz + yz * yz + zz * zz
    ab = xx * xy + xy * yy + xz * yz
    ac = xx * xz + xy * yz + xz * zz
    bc = xy * xz + yy * yz + yz * zz
    norm = aa * aa + bb * bb + cc * cc + 2.0 * (ab * ab + ac * ac + bc * bc)
    size = 0.73 * jnp.sqrt(jnp.sqrt(norm)) + 0.04
    row = lax.broadcasted_iota(jnp.int32, (8, LANES), 0)
    out_ref[...] = jnp.where(row == 7, jnp.broadcast_to(size, (8, LANES)), 0.0)


def with_size(value, *others):
    row = lax.broadcasted_iota(jnp.int32, (ROWS, LANES), 0)
    return jnp.where(row == 7, functools.reduce(jnp.maximum, others), value)


def pair_sides(index, pair, other):
    even = lax.rem(index, 2) == 0
    return jnp.where(even, other, pair), jnp.where(even, pair, other)


def z_kernel(mine_ref, swap_ref, out_ref):
    gz = lax.axis_index("gz")
    _, f, _ = iotas()
    mine, swap = mine_ref[...], swap_ref[...]
    other = roll(swap, jnp.where(gz == 0, 3 * BOX_Y, LANES - 3 * BOX_Y), 1)
    first_f = jnp.where(gz == 0, 3, 0)
    value = mine + jnp.where((f >= first_f) & (f <= first_f + 2), other, 0.0)
    out_ref[...] = with_size(value, mine, swap)


def x_kernel(mine_ref, pair_ref, other_ref, *rest):
    out_ref = rest[-1]
    gx, nx = lax.axis_index("gx"), lax.axis_size("gx")
    kx, _, _ = iotas()
    mine, pair, other = mine_ref[...], pair_ref[...], other_ref[...]
    low, high = pair_sides(gx, pair, other)
    first_x, last_x = jnp.where(gx > 0, 2, -1), jnp.where(gx < nx - 1, 4, 8)
    value = mine + jnp.where(kx <= first_x, rows_rolled(low, 4), 0.0)
    value = value + jnp.where((kx >= last_x) & (kx <= 6), rows_rolled(high, 4), 0.0)
    out_ref[...] = with_size(value, mine, pair, other)


def x_first_kernel(mine_ref, size_ref, out_ref):
    out_ref[...] = mine_ref[...]
    row = lax.broadcasted_iota(jnp.int32, (8, LANES), 0)
    out_ref[0:8] = jnp.where(row == 7, size_ref[...], mine_ref[0:8])


def y_sum(mine_ref, pair_ref, other_ref):
    gy, ny = lax.axis_index("gy"), lax.axis_size("gy")
    _, _, e = iotas()
    mine, pair, other = mine_ref[...], pair_ref[...], other_ref[...]
    low, high = pair_sides(gy, pair, other)
    first_y, last_y = jnp.where(gy > 0, 2, -1), jnp.where(gy < ny - 1, 16, LANES)
    value = mine + jnp.where(e <= first_y, roll(low, LANES - 16, 1), 0.0)
    value = value + jnp.where(e >= last_y, roll(high, 16, 1), 0.0)
    return value, jnp.maximum(jnp.maximum(mine, pair), other)[7:8]


def rows_rolled(value, shift):
    return jnp.concatenate(
        [roll(value[c * 8 : c * 8 + 8], shift, 0) for c in range(3)], axis=0
    )


def middle_kernel(in_ref, out_ref):
    (gx, nx), _, (gz, nz) = places()
    kx, f, e = iotas()
    has_low = (gx > 0).astype(jnp.int32)
    has_high = (gx < nx - 1).astype(jnp.int32)
    low = jnp.maximum(gx - 1, 0)
    high = jnp.minimum(gx + 1, nx - 1)
    take_low = (kx <= 2) & (has_low == 1)
    take_high = (kx >= 4) & (kx <= 6) & (has_high == 1)

    def along_x(part):
        value = in_ref[gx * nz + part]
        below = rows_rolled(in_ref[low * nz + part], 4)
        above = rows_rolled(in_ref[high * nz + part], 4)
        value = value + jnp.where(take_low, below, 0.0)
        return value + jnp.where(take_high, above, 0.0)

    mine = along_x(gz)
    other = along_x(1 - gz)
    other = roll(other, jnp.where(gz == 0, 3 * BOX_Y, LANES - 3 * BOX_Y), 1)
    first_f = jnp.where(gz == 0, 3, 0)
    value = mine + jnp.where((f >= first_f) & (f <= first_f + 2), other, 0.0)
    everything = in_ref[0]
    for i in range(1, in_ref.shape[0]):
        everything = everything + in_ref[i]
    value = jnp.where(kx == 7, everything, value)
    for i in range(out_ref.shape[0]):
        out_ref[i] = value


def along_y_sum(in_ref):
    _, (gy, ny), _ = places()
    kx, f, e = iotas()
    has_low = (gy > 0).astype(jnp.int32)
    has_high = (gy < ny - 1).astype(jnp.int32)
    below = roll(in_ref[jnp.maximum(gy - 1, 0)], LANES - 16, 1)
    above = roll(in_ref[jnp.minimum(gy + 1, ny - 1)], 16, 1)
    value = in_ref[gy]
    value = value + jnp.where((e <= 2) & (has_low == 1), below, 0.0)
    value = value + jnp.where((e >= 16) & (has_high == 1), above, 0.0)
    everything = in_ref[0]
    for i in range(1, in_ref.shape[0]):
        everything = everything + in_ref[i]
    return value, everything


def message(vector, image, own, out_ref):
    norm = jnp.sum(own * vector * vector, axis=0, keepdims=True)
    product = jnp.sum(vector * image, axis=0, keepdims=True)
    row = lax.broadcasted_iota(jnp.int32, (ROWS, LANES), 0)
    value = jnp.where(row == 7, norm, image)
    value = jnp.where(row == 15, product, value)
    for i in range(out_ref.shape[0]):
        out_ref[i] = value


def total_of(in_ref):
    values = [in_ref[i] for i in range(in_ref.shape[0])]
    while len(values) > 1:
        values = [a + b for a, b in zip(values[::2], values[1::2])]
    return values[0]


def tile_parts():
    kx, f, e = (v[0:8] for v in iotas())
    return kx, f, e, lax.broadcasted_iota(jnp.int32, (8, LANES), 1)


def own_parts(image, line, out_ref):
    (gx, nx), (gy, ny), (gz, nz) = places()
    row, f, e, lane = tile_parts()
    parts = [image[c * 8 : c * 8 + 8] for c in range(3)]
    six = jnp.zeros((8, LANES), jnp.float32)
    before, other_z, beside_y = six, six, six
    layers = 2 * BOX_Y
    start = jnp.where(gz == 0, 4 * BOX_Y, 0)
    for c, part in enumerate(parts):
        here = (row == 2 * c) | (row == 2 * c + 1)
        six = jnp.where(here, roll(part, (2 * c + 3) % 8, 0), six)
        before = jnp.where(row == c, roll(part, c, 0), before)
        part = roll(part, 7, 0)
        packed = roll(part, lax.rem(layers * c - start + LANES, LANES), 1)
        other_z = jnp.where((lane >= layers * c) & (lane < layers * c + layers), packed, other_z)
        beside_y = jnp.where(e == c, roll(part, c, 1), beside_y)
        here = (e == 17 - 2 * c) | (e == 18 - 2 * c)
        beside_y = jnp.where(here, roll(part, (LANES - 2 * c) % LANES, 1), beside_y)
    own = roll(six, jnp.where(gz == 0, 0, LANES - BOX_Y), 1)
    after = own
    for source, target, shift in SPARE:
        moved = roll(roll(own, (target - source) % 8, 0), shift, 1)
        after = jnp.where((row == target) & (lane >= 2 * layers), moved, after)
    own = roll(six, jnp.where(gz == 0, LANES - 4 * BOX_Y, 0), 1)
    after_z = jnp.where(lane < layers, own, roll(roll(own, 4, 0), layers, 1))
    values = (after, after_z, before, other_z, beside_y)
    scalars = jnp.where(row == 0, roll(line, 114, 1), roll(line, 100, 1))
    after, after_z, before, other_z, beside_y = [
        jnp.where(lane >= BOX_Z * BOX_Y, scalars, v)[0:4] for v in values
    ]
    for x in range(nx):
        for z in range(nz):
            same = gz == z
            value = jnp.where(gx == x, jnp.where(same, beside_y, other_z), before)
            value = jnp.where(gx + 1 == x, jnp.where(same, after, after_z), value)
            for y in range(ny):
                out_ref[(x * ny + y) * nz + z] = value


def own_sum(image, in_ref):
    (gx, nx), (gy, ny), (gz, nz) = places()
    row, f, e, lane = tile_parts()
    lower_y, upper_y = gy > 0, gy < ny - 1
    below_y, above_y = jnp.maximum(gy - 1, 0), jnp.minimum(gy + 1, ny - 1)
    below_mask = ((e == 1) | (e == 2)) & lower_y
    above_mask = (e == 16) & upper_y
    first_f, last_f = jnp.where(gz == 0, 3, 1), jnp.where(gz == 0, 3, 2)
    z_mask = (f >= first_f) & (f <= last_f)
    nothing = jnp.zeros((4, LANES), jnp.float32)

    def tile(x, y, z):
        return jnp.concatenate([in_ref[(x * ny + y) * nz + z], nothing], axis=0)

    def over_y(x, z):
        value = tile(x, gy, z)
        value = value + jnp.where(below_mask, roll(tile(x, below_y, z), LANES - 16, 1), 0.0)
        return value + jnp.where(above_mask, roll(tile(x, above_y, z), 16, 1), 0.0)

    layers = 2 * BOX_Y
    z_start = jnp.where(gz == 0, 3 * BOX_Y, BOX_Y)
    packed = over_y(jnp.maximum(gx - 1, 0), gz)
    six = packed
    for source, target, shift in SPARE:
        moved = roll(roll(packed, (source - target) % 8, 0), LANES - shift, 1)
        first = 2 * layers - shift
        six = jnp.where((row == source) & (lane >= first) & (lane < first + layers), moved, six)
    six = roll(six, jnp.where(gz == 0, 0, BOX_Y), 1)
    packed = over_y(jnp.maximum(gx - 1, 0), 1 - gz)
    moved = jnp.where(row < 4, packed, roll(roll(packed, 4, 0), LANES - layers, 1))
    from_before = six + jnp.where(z_mask, roll(moved, z_start, 1), 0.0)
    above_x = jnp.minimum(gx + 1, nx - 1)
    moved = roll(over_y(above_x, 1 - gz), jnp.where(gz == 0, 3 * BOX_Y, LANES - 3 * BOX_Y), 1)
    from_after = over_y(above_x, gz) + jnp.where(z_mask, moved, 0.0)
    from_z = roll(over_y(gx, 1 - gz), 1, 0)
    from_below, from_above = roll(tile(gx, below_y, gz), 1, 0), roll(tile(gx, above_y, gz), 1, 0)
    own_rows = (row >= 1) & (row <= 4)
    sums = []
    for c in range(3):
        value = image[c * 8 : c * 8 + 8]
        here = ((row == 1) | (row == 2)) & (gx > 0)
        value = value + jnp.where(here, roll(from_before, (1 - 2 * c) % 8, 0), 0.0)
        here = (row == 4) & (gx < nx - 1)
        value = value + jnp.where(here, roll(from_after, 4 - c, 0), 0.0)
        moved = roll(from_z, lax.rem(z_start - layers * c + LANES, LANES), 1)
        value = value + jnp.where(own_rows & z_mask, moved, 0.0)
        moved = roll(from_below, LANES - 16 + 2 * c, 1)
        value = value + jnp.where(own_rows & below_mask, moved, 0.0)
        moved = roll(from_above, 16 - c, 1)
        value = value + jnp.where(own_rows & above_mask, moved, 0.0)
        sums.append(value)
    return jnp.concatenate(sums, axis=0)


def row_sums(products, rows):
    sums = [jnp.sum(p, axis=0, keepdims=True) for p in products]
    return jnp.concatenate(sums + [jnp.zeros((rows - len(sums), LANES), jnp.float32)], axis=0)


def early_kernel(*refs):
    _, own = masks(places())
    vectors = [ref[...] for ref in refs[:5]]
    products = []
    for i in range(5):
        mine = own * vectors[i]
        products += [mine * vectors[j] for j in range(i, 5)]
    refs[5][...] = row_sums(products, 16)


def basis_kernel(number, mine_ref, pair_ref, other_ref, *refs):
    past = refs[:number]
    early_ref, refs = (refs[number], refs[1:]) if number == 5 else (None, refs)
    operands = refs[number : number + 5]
    out_ref, *new_refs, field_ref, sums_ref = refs[number + 5 :]
    inside, own = masks(places())
    value, size = y_sum(mine_ref, pair_ref, other_ref)
    value = value * inside
    if number:
        value = value + DAMP * past[-1][...]
    if number == 3:
        inverse = 1.0 / size
        one, two = past[1][...], past[2][...]
        second = inverse * two - SHIFTS[1] * one
        value = inverse * (inverse * value - SHIFTS[1] * two) - SHIFTS[2] * second
        new_refs[1][...] = second
    elif number > 3:
        value = value / size - SHIFTS[number - 1] * past[-1][...]
    new_refs[0][...] = value
    image = apply_local(value, *operands, field_ref, sums_ref) * inside
    if number < 5:
        out_ref[...] = with_size(image, jnp.broadcast_to(size, (ROWS, LANES)))
        return
    new_refs[1][...] = jnp.broadcast_to(size, (8, LANES))
    mine = own * value
    late = [mine * ref[...] for ref in past] + [mine * value]
    late.append(value * image + DAMP * late[5])
    sums = jnp.concatenate([early_ref[...], row_sums(late, 8)], axis=0)
    sums = jnp.sum(sums, axis=1, keepdims=True)
    row = lax.broadcasted_iota(jnp.int32, (ROWS, LANES), 0)
    lane = lax.broadcasted_iota(jnp.int32, (ROWS, LANES), 1)
    line = jnp.sum(jnp.where(row == lane, sums, 0.0), axis=0, keepdims=True)
    own_parts(image, line, out_ref)
    new_refs[2][...] = image


def times(a, b):
    return None if a is None or b is None else a * b


def form(left, table, right):
    total = None
    for i, a in enumerate(left):
        inner = None
        for j, b in enumerate(right):
            inner = add(inner, times(table[i][j], b))
        total = add(total, times(a, inner))
    return total


def fast_kernel(in_ref, *refs):
    vectors = [ref[...] for ref in refs[:6]]
    size_ref, last_ref, solution_ref, residual_ref, good_ref = refs[6:]
    inside, _ = masks(places())
    value = own_sum(last_ref[...], in_ref)
    size = size_ref[0:1, 0:1]
    inverse = 1.0 / size
    image = (value * inside + DAMP * vectors[5]) * inverse
    total = total_of(in_ref)
    lane = lax.broadcasted_iota(jnp.int32, (1, LANES), 1)
    scalars = []
    for k in range(23):
        row, at = (0, 114 + k) if k < 14 else (1, 100 + k)
        scalars.append(jnp.sum(jnp.where(lane == at, total[row : row + 1], 0.0), axis=1, keepdims=True))
    gram = [[None] * 6 for _ in range(6)]
    k = 0
    for i in range(5):
        for j in range(i, 5):
            gram[i][j] = gram[j][i] = scalars[k]
            k += 1
    for i in range(6):
        gram[i][5] = gram[5][i] = scalars[16 + i]
    factor = [inverse] + [jnp.ones_like(inverse)] * 4
    energy = [[None] * 6 for _ in range(6)]
    for i in range(5):
        for j in range(i, 6):
            energy[i][j] = energy[j][i] = factor[i] * (gram[i + 1][j] + SHIFTS[i] * gram[i][j])
    energy[5][5] = scalars[22] * inverse
    rest = [row[:] for row in gram]
    good = jnp.ones_like(inverse)
    for k in range(6):
        good = jnp.where(rest[k][k] / gram[k][k] > WORST_PIVOT, good, 0.0)
        for i in range(k + 1, 6):
            ratio = rest[i][k] / rest[k][k]
            for j in range(i, 6):
                rest[i][j] = rest[i][j] - ratio * rest[k][j]
                rest[j][i] = rest[i][j]
    good_ref[0, 0] = jnp.sum(good).astype(jnp.int32)
    solved = [None] * 7
    residual = [jnp.ones_like(inverse)] + [None] * 6
    direction = residual[:]
    norm = gram[0][0]
    for number in range(ITERS):
        known = number + 1
        moved = [None] * 7
        for j in range(known):
            if j == 5:
                moved[6] = add(moved[6], direction[5])
            else:
                part = factor[j] * direction[j]
                moved[j + 1] = add(moved[j + 1], part)
                moved[j] = add(moved[j], SHIFTS[j] * part)
        step = norm / form(direction[:known], energy, direction[:known])
        solved = [add(a, times(step, b)) for a, b in zip(solved, direction)]
        residual = [add(a, times(-step, b)) for a, b in zip(residual, moved)]
        if number < ITERS - 1:
            known += 1
            later = form(residual[:known], gram, residual[:known])
            ratio = later / norm
            direction = [add(a, times(ratio, b)) for a, b in zip(residual, direction)]
            norm = later
    vectors = vectors + [image]
    first, second = None, None
    for j in range(7):
        if solved[j] is not None:
            first = add(first, solved[j] * vectors[j])
        second = add(second, residual[j] * vectors[j])
    write_out(first * (inverse / SCALE), second, solution_ref, residual_ref)


def write_out(solved, residual, solution_ref, residual_ref):
    both = jnp.concatenate([solved, residual], axis=0)
    value = dot(split3(both), put(), ((1,), (1,)))
    value = value[:48] + value[48:96] + value[96:]
    for z in range(CELLS_Z):
        for c in range(3):
            solution_ref[c, z] = value[c * 8 + 1 : c * 8 + 5, z * 16 : z * 16 + 16]
            residual_ref[c, z] = value[ROWS + c * 8 + 1 : ROWS + c * 8 + 5, z * 16 : z * 16 + 16]


def slow_kernel(vector_ref, grad_ref, rows_ref, back_ref, along_ref, lanes_ref, out_ref, field_ref, sums_ref):
    inside, own = masks(places())
    vector = vector_ref[...]
    image = apply_local(vector, grad_ref, rows_ref, back_ref, along_ref, lanes_ref, field_ref, sums_ref)
    message(vector, image * inside, own, out_ref)


def update(in_ref, old_ref, number):
    inside, own = masks(places())
    value, everything = along_y_sum(in_ref)
    residual = old_ref[ROWS : 2 * ROWS] if number else old_ref[...]
    image = value * inside + DAMP * residual
    norm = jnp.sum(everything[7:8], axis=1, keepdims=True)
    product = jnp.sum(everything[15:16], axis=1, keepdims=True) + DAMP * norm
    if number:
        ratio = norm / old_ref[4 * ROWS : 4 * ROWS + 1, 0:1]
        step = norm / (product - ratio * norm / old_ref[4 * ROWS + 1 : 4 * ROWS + 2, 0:1])
        direction = residual + ratio * old_ref[2 * ROWS : 3 * ROWS]
        image = image + ratio * old_ref[3 * ROWS : 4 * ROWS]
        solved = old_ref[0:ROWS] + step * direction
    else:
        step = norm / product
        direction = residual
        solved = step * direction
    residual = residual - step * image
    return own, inside, solved, residual, direction, image, norm, step


def step_kernel(number, in_ref, old_ref, grad_ref, rows_ref, back_ref, along_ref, lanes_ref, out_ref, new_ref, field_ref, sums_ref):
    own, inside, solved, residual, direction, image, norm, step = update(in_ref, old_ref, number)
    new_ref[0:ROWS] = solved
    new_ref[ROWS : 2 * ROWS] = residual
    new_ref[2 * ROWS : 3 * ROWS] = direction
    new_ref[3 * ROWS : 4 * ROWS] = image
    row = lax.broadcasted_iota(jnp.int32, (8, LANES), 0)
    new_ref[4 * ROWS : 4 * ROWS + 8] = jnp.where(row == 0, norm, step)
    image = apply_local(residual, grad_ref, rows_ref, back_ref, along_ref, lanes_ref, field_ref, sums_ref)
    message(residual, image * inside, own, out_ref)


def last_kernel(in_ref, old_ref, solution_ref, residual_ref):
    _, _, solved, residual, _, _, _, _ = update(in_ref, old_ref, ITERS - 1)
    write_out(solved / SCALE, residual, solution_ref, residual_ref)


def call(body, outs, *args, scratch=False):
    shapes = [
        jax.ShapeDtypeStruct(s, jnp.float32) if s else jax.ShapeDtypeStruct((1, 1), jnp.int32)
        for s in outs
    ]
    scratch_shapes = [pltpu.VMEM((96, 7 * LANES), jnp.float32)] * 2 if scratch else []
    vmem = pl.BlockSpec(memory_space=pltpu.VMEM)
    return pl.pallas_call(
        body,
        out_shape=shapes,
        in_specs=[vmem] * len(args),
        out_specs=[vmem if s else pl.BlockSpec(memory_space=pltpu.SMEM) for s in outs],
        scratch_shapes=scratch_shapes,
        compiler_params=pltpu.CompilerParams(vmem_limit_bytes=24 * 1024 * 1024),
    )(*args)


def swaps(axis):
    count = lax.axis_size(axis)
    pair = [(i, i ^ 1) for i in range(count)]
    other = [(i, (i + 1 if i % 2 else i - 1) % count) for i in range(count)]
    return pair, other


def shards(gradient, right_side):
    (gx, nx), (gy, ny), (gz, nz) = places()
    rows_x, back_x, along_y, lanes = [jnp.asarray(t) for t in tables()]
    rows_x = lax.dynamic_index_in_dim(rows_x, kind_of(gx, nx), 0, keepdims=False)
    along_y = lax.dynamic_index_in_dim(along_y, gz, 0, keepdims=False)
    lanes = lax.dynamic_index_in_dim(lanes, gz * 3 + kind_of(gy, ny), 0, keepdims=False)
    operands = (gradient, rows_x, back_x, along_y, lanes)
    group, line, box = (nx * nz, ROWS, LANES), (ny, ROWS, LANES), (ROWS, LANES)
    everyone = (nx * ny * nz, 4, LANES)
    tile, state, shape = (8, LANES), (4 * ROWS + 8, LANES), right_side.shape

    def exchange_all(sent):
        near = lax.all_to_all(sent, ("gx", "gz"), 0, 0)
        (sent,) = call(middle_kernel, [line], near)
        return lax.all_to_all(sent, "gy", 0, 0)

    def exchange_near(sent, size=None):
        swapped = lax.ppermute(sent, "gz", swaps("gz")[0])
        (sent,) = call(z_kernel, [box], sent, swapped)
        if size is not None:
            (sent,) = call(x_first_kernel, [box], sent, size)
        pair, other = [lax.ppermute(sent, "gx", s) for s in swaps("gx")]
        (sent,) = call(x_kernel, [box], sent, pair, other)
        pair, other = swaps("gy")
        other = lax.ppermute(sent, "gy", other)
        pair = lax.ppermute(sent, "gy", pair)
        return sent, pair, other

    def slow(first):
        (sent,) = call(slow_kernel, [group], first, *operands, scratch=True)
        old = first
        for number in range(ITERS - 1):
            body = functools.partial(step_kernel, number)
            sent, old = call(body, [group, state], exchange_all(sent), old, *operands, scratch=True)
        return tuple(call(last_kernel, [shape, shape], exchange_all(sent), old))

    (sent,) = call(start_kernel, [box], right_side)
    (size,) = call(size_kernel, [tile], gradient)
    vectors = []
    for number in range(6):
        near = exchange_near(sent, size if number == 0 else None)
        outs = [everyone if number == 5 else box, box] + [[], [], [], [box], [], [tile, box]][number]
        body = functools.partial(basis_kernel, number)
        early = call(early_kernel, [(16, LANES)], *vectors) if number == 5 else []
        sent, vector, *extra = call(
            body, outs, *near, *vectors, *early, *operands, scratch=True
        )
        if number == 3:
            vectors[2] = extra[0]
        vectors.append(vector)
    arrived = lax.all_to_all(sent, ("gx", "gy", "gz"), 0, 0)
    *fast, good = call(fast_kernel, [shape, shape, None], arrived, *vectors, *extra)
    return lax.cond(good[0, 0] > 0, lambda first: tuple(fast), slow, vectors[0])


def solution(mesh):
    placed = P(None, "gz", "gx", "gy")
    return jax.shard_map(
        shards,
        mesh=mesh,
        in_specs=(placed, placed),
        out_specs=(placed, placed),
        check_vma=False,
    )
```

```python
import functools

import jax
import jax.numpy as jnp
import ml_dtypes
import numpy as np
from jax import lax
from jax.experimental import pallas as pl
from jax.experimental.pallas import tpu as pltpu
from jax.sharding import PartitionSpec as P

ITERS = 6
SMOOTHING = 0.5
DAMPING = 0.05
HIGHEST = lax.Precision.HIGHEST

CELLS_Z, CELLS_X, CELLS_Y = 4, 4, 16
BOX_X, BOX_Y, BOX_Z = 7, 19, 6
LANES = 128
ROWS = 24
DENOMINATOR = 3072.0
SCALE = 512.0
DAMP = DAMPING / SCALE
SHIFTS = (0.0, 0.171, 0.452, 0.776, 0.114)
WORST_PIVOT = 0.05
SPARE = ((4, 0, 76), (4, 1, 38), (5, 2, 76), (5, 3, 38))


def numerators(t):
    return (
        (8 - t) ** 3,
        3 * t**3 - 48 * t**2 + 2048,
        -3 * t**3 + 24 * t**2 + 192 * t + 512,
        t**3,
    )


WEIGHTS = [[n / DENOMINATOR for n in numerators(t)] for t in range(8)]


def basis(cells):
    table = np.zeros((8 * cells + 1, cells + 3 + 1))
    for voxel in range(8 * cells + 1):
        for k, n in enumerate(numerators(voxel % 8)):
            table[voxel, voxel // 8 + k] = n
    return table[:, :-1]


def mass_and_edges(cells, first, last):
    table = basis(cells) / DENOMINATOR
    own = table[:-1]
    steps = table[1:] - table[:-1]
    if last:
        steps[-1] = -table[-2]
    edges = steps.T @ steps
    if first:
        edges = edges + np.outer(table[0], table[0])
    return own.T @ own, edges


def place_z(matrix, part):
    return matrix[1:7, 1:7] if part == 0 else matrix[0:6, 0:6]


def stacked(table):
    high = table.astype(ml_dtypes.bfloat16)
    rest = table - high.astype(table.dtype)
    middle = rest.astype(ml_dtypes.bfloat16)
    low = (rest - middle.astype(table.dtype)).astype(ml_dtypes.bfloat16)
    return np.concatenate([high, high, high, middle, middle, low], axis=-1)


@functools.lru_cache(None)
def tables():
    bx = basis(CELLS_X)[:-1]
    expand = np.zeros((96, ROWS))
    for c in range(3):
        expand[c * 32 : c * 32 + 32, c * 8 : c * 8 + BOX_X] = bx / DENOMINATOR / DENOMINATOR
    rows_x = np.zeros((3, 144, ROWS), np.float32)
    for kind in range(3):
        mass, edges = mass_and_edges(CELLS_X, kind == 0, kind == 2)
        rows_x[kind, :96] = expand
        for c in range(3):
            at = slice(c * 8, c * 8 + BOX_X)
            rows_x[kind, 96 + c * 8 : 96 + c * 8 + BOX_X, at] = SMOOTHING / SCALE * mass
            rows_x[kind, 120 + c * 8 : 120 + c * 8 + BOX_X, at] = SMOOTHING / SCALE * edges
    by = basis(CELLS_Y)[:-1]
    along_y = np.zeros((2, 2, LANES, 7 * LANES))
    for part in range(2):
        for f in range(BOX_Z):
            g = f + 1 if part == 0 else f
            low = by.T.astype(ml_dtypes.bfloat16).astype(np.float64)
            at = slice(f * BOX_Y, (f + 1) * BOX_Y)
            along_y[part, 0, at, g * LANES : (g + 1) * LANES] = low
            along_y[part, 1, at, g * LANES : (g + 1) * LANES] = by.T - low
    along_y = along_y.reshape(2, 256, 7 * LANES).astype(ml_dtypes.bfloat16)
    lanes = np.zeros((2, 3, 256, LANES))
    for part in range(2):
        mz, kz = mass_and_edges(CELLS_Z, part == 0, part == 1)
        mz, kz = place_z(mz, part), place_z(kz, part)
        for kind in range(3):
            my, ky = mass_and_edges(CELLS_Y, kind == 0, kind == 2)
            used = BOX_Z * BOX_Y
            lanes[part, kind, :used, :used] = np.kron(kz, my) + np.kron(mz, ky)
            lanes[part, kind, 128 : 128 + used, :used] = np.kron(mz, my)
    return (
        stacked(rows_x.astype(np.float64)),
        stacked(expand.T / SCALE),
        along_y,
        stacked(lanes.reshape(6, 256, LANES))[..., [*range(LANES), *range(3 * LANES, 4 * LANES)]],
    )


def iotas():
    row = lax.broadcasted_iota(jnp.int32, (ROWS, LANES), 0)
    lane = lax.broadcasted_iota(jnp.int32, (ROWS, LANES), 1)
    f = jnp.zeros_like(lane)
    for k in range(1, BOX_Z + 1):
        f = f + (lane >= k * BOX_Y).astype(jnp.int32)
    return row & 7, f, lane - f * BOX_Y


def masks(where):
    (gx, nx), (gy, ny), (gz, nz) = where
    kx, f, e = iotas()
    low_x, high_x = jnp.where(gx == 0, 1, 0), jnp.where(gx == nx - 1, 4, 6)
    low_y, high_y = jnp.where(gy == 0, 1, 0), jnp.where(gy == ny - 1, 16, 18)
    high_z = jnp.where(gz == 0, 5, 4)
    inside = (kx >= low_x) & (kx <= high_x) & (e >= low_y) & (e <= high_y) & (f <= high_z)
    own_z = jnp.where(gz == 0, 0, 1)
    own = (kx >= 1) & (kx <= 4) & (e >= 1) & (e <= 16) & (f >= own_z) & (f <= own_z + 3)
    return inside.astype(jnp.float32), own.astype(jnp.float32)


def places():
    return tuple((lax.axis_index(a), lax.axis_size(a)) for a in ("gx", "gy", "gz"))


def add(a, b):
    return b if a is None else a if b is None else a + b


def split3(value):
    high = value.astype(jnp.bfloat16)
    rest = value - high.astype(jnp.float32)
    middle = rest.astype(jnp.bfloat16)
    low = (rest - middle.astype(jnp.float32)).astype(jnp.bfloat16)
    return jnp.concatenate([high, middle, low], axis=0)


def pieces6(value):
    pieces = split3(value)
    count = value.shape[0]
    return jnp.concatenate([pieces, pieces[: 2 * count], pieces[:count]], axis=0)


def dot(a, b, dims=((1,), (0,)), precision=None):
    return lax.dot_general(
        a, b, (dims, ((), ())), precision=precision, preferred_element_type=jnp.float32
    )


def kind_of(index, count):
    return jnp.where(index == 0, 0, jnp.where(index == count - 1, 2, 1))


def apply_local(vector, grad_ref, rows_ref, back_ref, along_ref, lanes_ref, field_ref, sums_ref):
    first = dot(rows_ref[...], pieces6(vector))
    pieces = split3(first[:96])[:192]
    field = dot(jnp.concatenate([pieces, pieces], axis=1), along_ref[...])
    field_ref[...] = field[:96] + field[96:192]

    def column(cx, carry):
        rows = [pl.ds(pl.multiple_of(c * 32 + cx * 8, 8), 8) for c in range(3)]
        inside = pl.ds(pl.multiple_of(cx * 8, 8), 8)
        total = [[None] * 4 for _ in range(3)]
        for cz in range(CELLS_Z):
            layer = [
                [field_ref[rows[c], (cz + k) * LANES : (cz + k + 1) * LANES] for k in range(4)]
                for c in range(3)
            ]

            def weighted(t, values):
                slope = [grad_ref[c, cz * 8 + t, inside, :] for c in range(3)]
                shade = slope[0] * values[0] + slope[1] * values[1] + slope[2] * values[2]
                return [slope[c] * shade for c in range(3)]

            edge, near = WEIGHTS[0][0], WEIGHTS[0][1]
            value = weighted(0, [edge * (v[0] + v[2]) + near * v[1] for v in layer])
            first = [edge * v for v in value]
            second = [near * v for v in value]
            outer = [v[0] + v[3] for v in layer]
            inner = [v[1] + v[2] for v in layer]
            outer_odd = [v[0] - v[3] for v in layer]
            inner_odd = [v[1] - v[2] for v in layer]
            edge, near = WEIGHTS[4][0], WEIGHTS[4][1]
            value = weighted(4, [edge * a + near * b for a, b in zip(outer, inner)])
            sums = [[edge * v, near * v, None, None] for v in value]
            for t in (1, 2, 3):
                w = WEIGHTS[t]
                a, b, p, q = (w[0] + w[3]) / 2, (w[1] + w[2]) / 2, (w[0] - w[3]) / 2, (w[1] - w[2]) / 2
                even = [a * outer[c] + b * inner[c] for c in range(3)]
                odd = [p * outer_odd[c] + q * inner_odd[c] for c in range(3)]
                one = weighted(t, [even[c] + odd[c] for c in range(3)])
                two = weighted(8 - t, [even[c] - odd[c] for c in range(3)])
                for c in range(3):
                    plus, minus = one[c] + two[c], one[c] - two[c]
                    terms = (a * plus, b * plus, p * minus, q * minus)
                    sums[c] = [add(x, y) for x, y in zip(sums[c], terms)]
            for c in range(3):
                outside, middle, outside_odd, middle_odd = sums[c]
                parts = (
                    outside + outside_odd + first[c],
                    middle + middle_odd + second[c],
                    middle - middle_odd + first[c],
                    outside - outside_odd,
                )
                total[c] = [add(x, y) for x, y in zip(total[c], parts)]
                sums_ref[rows[c], cz * LANES : (cz + 1) * LANES] = total[c][0]
                total[c] = total[c][1:] + [None]
        for c in range(3):
            for k in range(3):
                g = CELLS_Z + k
                sums_ref[rows[c], g * LANES : (g + 1) * LANES] = total[c][k]
        return carry

    lax.fori_loop(0, CELLS_X, column, 0, unroll=True)
    pieces = split3(sums_ref[...])[:192]
    back = dot(pieces, along_ref[...], ((1,), (1,)))
    back = back[:, :LANES] + back[:, LANES:]
    back = back[:96] + back[96:192]
    data = dot(back_ref[...], pieces6(back))
    relief = dot(split3(jnp.concatenate([first[96:120], first[120:144]], axis=1)), lanes_ref[...])
    relief = relief[:, :LANES] + relief[:, LANES:]
    relief = relief[:ROWS] + relief[ROWS : 2 * ROWS] + relief[2 * ROWS :]
    return data + relief


def roll(value, shift, axis):
    return pltpu.roll(value, shift, axis)


def put():
    first_f = jnp.where(lax.axis_index("gz") == 0, 0, 1)
    row = lax.broadcasted_iota(jnp.int32, (64, LANES), 0)
    lane = lax.broadcasted_iota(jnp.int32, (64, LANES), 1)
    target = ((row >> 4) + first_f) * BOX_Y + 1 + (row & 15)
    return (lane == target).astype(jnp.float32).astype(jnp.bfloat16)


def start_kernel(right_ref, out_ref):
    parts = []
    for c in range(3):
        own = jnp.concatenate([right_ref[c, z] for z in range(CELLS_Z)], axis=1)
        parts += [jnp.zeros((1, 64), jnp.float32), own, jnp.zeros((3, 64), jnp.float32)]
    value = dot(split3(jnp.concatenate(parts, axis=0)), put())
    out_ref[...] = value[:ROWS] + value[ROWS : 2 * ROWS] + value[2 * ROWS :]


def size_kernel(grad_ref, out_ref):
    def plane(z, totals):
        totals = list(totals)
        for x in range(4):
            slope = [grad_ref[c, z, x * 8 : x * 8 + 8, :] for c in range(3)]
            k = 0
            for a in range(3):
                for b in range(a, 3):
                    totals[k] = totals[k] + slope[a] * slope[b]
                    k += 1
        return tuple(totals)

    zero = jnp.zeros((8, LANES), jnp.float32)
    totals = lax.fori_loop(0, 32, plane, (zero,) * 6)
    count = 32.0 * 32.0 * 128.0
    xx, xy, xz, yy, yz, zz = [
        jnp.sum(jnp.sum(t, axis=0, keepdims=True), axis=1, keepdims=True) / count for t in totals
    ]
    aa = xx * xx + xy * xy + xz * xz
    bb = xy * xy + yy * yy + yz * yz
    cc = xz * xz + yz * yz + zz * zz
    ab = xx * xy + xy * yy + xz * yz
    ac = xx * xz + xy * yz + xz * zz
    bc = xy * xz + yy * yz + yz * zz
    norm = aa * aa + bb * bb + cc * cc + 2.0 * (ab * ab + ac * ac + bc * bc)
    size = 0.73 * jnp.sqrt(jnp.sqrt(norm)) + 0.04
    row = lax.broadcasted_iota(jnp.int32, (8, LANES), 0)
    out_ref[...] = jnp.where(row == 7, jnp.broadcast_to(size, (8, LANES)), 0.0)


def with_size(value, *others):
    row = lax.broadcasted_iota(jnp.int32, (ROWS, LANES), 0)
    return jnp.where(row == 7, functools.reduce(jnp.maximum, others), value)


def pair_sides(index, pair, other):
    even = lax.rem(index, 2) == 0
    return jnp.where(even, other, pair), jnp.where(even, pair, other)


def z_kernel(mine_ref, swap_ref, out_ref):
    gz = lax.axis_index("gz")
    _, f, _ = iotas()
    mine, swap = mine_ref[...], swap_ref[...]
    other = roll(swap, jnp.where(gz == 0, 3 * BOX_Y, LANES - 3 * BOX_Y), 1)
    first_f = jnp.where(gz == 0, 3, 0)
    value = mine + jnp.where((f >= first_f) & (f <= first_f + 2), other, 0.0)
    out_ref[...] = with_size(value, mine, swap)


def x_kernel(mine_ref, pair_ref, other_ref, *rest):
    out_ref = rest[-1]
    gx, nx = lax.axis_index("gx"), lax.axis_size("gx")
    kx, _, _ = iotas()
    mine, pair, other = mine_ref[...], pair_ref[...], other_ref[...]
    low, high = pair_sides(gx, pair, other)
    first_x, last_x = jnp.where(gx > 0, 2, -1), jnp.where(gx < nx - 1, 4, 8)
    value = mine + jnp.where(kx <= first_x, rows_rolled(low, 4), 0.0)
    value = value + jnp.where((kx >= last_x) & (kx <= 6), rows_rolled(high, 4), 0.0)
    out_ref[...] = with_size(value, mine, pair, other)


def x_first_kernel(mine_ref, size_ref, out_ref):
    out_ref[...] = mine_ref[...]
    row = lax.broadcasted_iota(jnp.int32, (8, LANES), 0)
    out_ref[0:8] = jnp.where(row == 7, size_ref[...], mine_ref[0:8])


def y_sum(mine_ref, pair_ref, other_ref):
    gy, ny = lax.axis_index("gy"), lax.axis_size("gy")
    _, _, e = iotas()
    mine, pair, other = mine_ref[...], pair_ref[...], other_ref[...]
    low, high = pair_sides(gy, pair, other)
    first_y, last_y = jnp.where(gy > 0, 2, -1), jnp.where(gy < ny - 1, 16, LANES)
    value = mine + jnp.where(e <= first_y, roll(low, LANES - 16, 1), 0.0)
    value = value + jnp.where(e >= last_y, roll(high, 16, 1), 0.0)
    return value, jnp.maximum(jnp.maximum(mine, pair), other)[7:8]


def rows_rolled(value, shift):
    return jnp.concatenate(
        [roll(value[c * 8 : c * 8 + 8], shift, 0) for c in range(3)], axis=0
    )


def middle_kernel(in_ref, out_ref):
    (gx, nx), _, (gz, nz) = places()
    kx, f, e = iotas()
    has_low = (gx > 0).astype(jnp.int32)
    has_high = (gx < nx - 1).astype(jnp.int32)
    low = jnp.maximum(gx - 1, 0)
    high = jnp.minimum(gx + 1, nx - 1)
    take_low = (kx <= 2) & (has_low == 1)
    take_high = (kx >= 4) & (kx <= 6) & (has_high == 1)

    def along_x(part):
        value = in_ref[gx * nz + part]
        below = rows_rolled(in_ref[low * nz + part], 4)
        above = rows_rolled(in_ref[high * nz + part], 4)
        value = value + jnp.where(take_low, below, 0.0)
        return value + jnp.where(take_high, above, 0.0)

    mine = along_x(gz)
    other = along_x(1 - gz)
    other = roll(other, jnp.where(gz == 0, 3 * BOX_Y, LANES - 3 * BOX_Y), 1)
    first_f = jnp.where(gz == 0, 3, 0)
    value = mine + jnp.where((f >= first_f) & (f <= first_f + 2), other, 0.0)
    everything = in_ref[0]
    for i in range(1, in_ref.shape[0]):
        everything = everything + in_ref[i]
    value = jnp.where(kx == 7, everything, value)
    for i in range(out_ref.shape[0]):
        out_ref[i] = value


def along_y_sum(in_ref):
    _, (gy, ny), _ = places()
    kx, f, e = iotas()
    has_low = (gy > 0).astype(jnp.int32)
    has_high = (gy < ny - 1).astype(jnp.int32)
    below = roll(in_ref[jnp.maximum(gy - 1, 0)], LANES - 16, 1)
    above = roll(in_ref[jnp.minimum(gy + 1, ny - 1)], 16, 1)
    value = in_ref[gy]
    value = value + jnp.where((e <= 2) & (has_low == 1), below, 0.0)
    value = value + jnp.where((e >= 16) & (has_high == 1), above, 0.0)
    everything = in_ref[0]
    for i in range(1, in_ref.shape[0]):
        everything = everything + in_ref[i]
    return value, everything


def message(vector, image, own, out_ref):
    norm = jnp.sum(own * vector * vector, axis=0, keepdims=True)
    product = jnp.sum(vector * image, axis=0, keepdims=True)
    row = lax.broadcasted_iota(jnp.int32, (ROWS, LANES), 0)
    value = jnp.where(row == 7, norm, image)
    value = jnp.where(row == 15, product, value)
    for i in range(out_ref.shape[0]):
        out_ref[i] = value


def total_of(in_ref):
    values = [in_ref[i] for i in range(in_ref.shape[0])]
    while len(values) > 1:
        values = [a + b for a, b in zip(values[::2], values[1::2])]
    return values[0]


def tile_parts():
    kx, f, e = (v[0:8] for v in iotas())
    return kx, f, e, lax.broadcasted_iota(jnp.int32, (8, LANES), 1)


def own_parts(image, line, out_ref):
    (gx, nx), (gy, ny), (gz, nz) = places()
    row, f, e, lane = tile_parts()
    parts = [image[c * 8 : c * 8 + 8] for c in range(3)]
    six = jnp.zeros((8, LANES), jnp.float32)
    before, other_z, beside_y = six, six, six
    layers = 2 * BOX_Y
    start = jnp.where(gz == 0, 4 * BOX_Y, 0)
    for c, part in enumerate(parts):
        here = (row == 2 * c) | (row == 2 * c + 1)
        six = jnp.where(here, roll(part, (2 * c + 3) % 8, 0), six)
        before = jnp.where(row == c, roll(part, c, 0), before)
        part = roll(part, 7, 0)
        packed = roll(part, lax.rem(layers * c - start + LANES, LANES), 1)
        other_z = jnp.where((lane >= layers * c) & (lane < layers * c + layers), packed, other_z)
        beside_y = jnp.where(e == c, roll(part, c, 1), beside_y)
        here = (e == 17 - 2 * c) | (e == 18 - 2 * c)
        beside_y = jnp.where(here, roll(part, (LANES - 2 * c) % LANES, 1), beside_y)
    own = roll(six, jnp.where(gz == 0, 0, LANES - BOX_Y), 1)
    after = own
    for source, target, shift in SPARE:
        moved = roll(roll(own, (target - source) % 8, 0), shift, 1)
        after = jnp.where((row == target) & (lane >= 2 * layers), moved, after)
    own = roll(six, jnp.where(gz == 0, LANES - 4 * BOX_Y, 0), 1)
    after_z = jnp.where(lane < layers, own, roll(roll(own, 4, 0), layers, 1))
    values = (after, after_z, before, other_z, beside_y)
    scalars = jnp.where(row == 0, roll(line, 114, 1), roll(line, 100, 1))
    after, after_z, before, other_z, beside_y = [
        jnp.where(lane >= BOX_Z * BOX_Y, scalars, v)[0:4] for v in values
    ]
    for x in range(nx):
        for z in range(nz):
            same = gz == z
            value = jnp.where(gx == x, jnp.where(same, beside_y, other_z), before)
            value = jnp.where(gx + 1 == x, jnp.where(same, after, after_z), value)
            for y in range(ny):
                out_ref[(x * ny + y) * nz + z] = value


def own_sum(image, in_ref):
    (gx, nx), (gy, ny), (gz, nz) = places()
    row, f, e, lane = tile_parts()
    lower_y, upper_y = gy > 0, gy < ny - 1
    below_y, above_y = jnp.maximum(gy - 1, 0), jnp.minimum(gy + 1, ny - 1)
    below_mask = ((e == 1) | (e == 2)) & lower_y
    above_mask = (e == 16) & upper_y
    first_f, last_f = jnp.where(gz == 0, 3, 1), jnp.where(gz == 0, 3, 2)
    z_mask = (f >= first_f) & (f <= last_f)
    nothing = jnp.zeros((4, LANES), jnp.float32)

    def tile(x, y, z):
        return jnp.concatenate([in_ref[(x * ny + y) * nz + z], nothing], axis=0)

    def over_y(x, z):
        value = tile(x, gy, z)
        value = value + jnp.where(below_mask, roll(tile(x, below_y, z), LANES - 16, 1), 0.0)
        return value + jnp.where(above_mask, roll(tile(x, above_y, z), 16, 1), 0.0)

    layers = 2 * BOX_Y
    z_start = jnp.where(gz == 0, 3 * BOX_Y, BOX_Y)
    packed = over_y(jnp.maximum(gx - 1, 0), gz)
    six = packed
    for source, target, shift in SPARE:
        moved = roll(roll(packed, (source - target) % 8, 0), LANES - shift, 1)
        first = 2 * layers - shift
        six = jnp.where((row == source) & (lane >= first) & (lane < first + layers), moved, six)
    six = roll(six, jnp.where(gz == 0, 0, BOX_Y), 1)
    packed = over_y(jnp.maximum(gx - 1, 0), 1 - gz)
    moved = jnp.where(row < 4, packed, roll(roll(packed, 4, 0), LANES - layers, 1))
    from_before = six + jnp.where(z_mask, roll(moved, z_start, 1), 0.0)
    above_x = jnp.minimum(gx + 1, nx - 1)
    moved = roll(over_y(above_x, 1 - gz), jnp.where(gz == 0, 3 * BOX_Y, LANES - 3 * BOX_Y), 1)
    from_after = over_y(above_x, gz) + jnp.where(z_mask, moved, 0.0)
    from_z = roll(over_y(gx, 1 - gz), 1, 0)
    from_below, from_above = roll(tile(gx, below_y, gz), 1, 0), roll(tile(gx, above_y, gz), 1, 0)
    own_rows = (row >= 1) & (row <= 4)
    sums = []
    for c in range(3):
        value = image[c * 8 : c * 8 + 8]
        here = ((row == 1) | (row == 2)) & (gx > 0)
        value = value + jnp.where(here, roll(from_before, (1 - 2 * c) % 8, 0), 0.0)
        here = (row == 4) & (gx < nx - 1)
        value = value + jnp.where(here, roll(from_after, 4 - c, 0), 0.0)
        moved = roll(from_z, lax.rem(z_start - layers * c + LANES, LANES), 1)
        value = value + jnp.where(own_rows & z_mask, moved, 0.0)
        moved = roll(from_below, LANES - 16 + 2 * c, 1)
        value = value + jnp.where(own_rows & below_mask, moved, 0.0)
        moved = roll(from_above, 16 - c, 1)
        value = value + jnp.where(own_rows & above_mask, moved, 0.0)
        sums.append(value)
    return jnp.concatenate(sums, axis=0)


def row_sums(products, rows):
    sums = [jnp.sum(p, axis=0, keepdims=True) for p in products]
    return jnp.concatenate(sums + [jnp.zeros((rows - len(sums), LANES), jnp.float32)], axis=0)


def early_kernel(*refs):
    _, own = masks(places())
    vectors = [ref[...] for ref in refs[:5]]
    products = []
    for i in range(5):
        mine = own * vectors[i]
        products += [mine * vectors[j] for j in range(i, 5)]
    refs[5][...] = row_sums(products, 16)


def basis_kernel(number, mine_ref, pair_ref, other_ref, *refs):
    past = refs[:number]
    early_ref, refs = (refs[number], refs[1:]) if number == 5 else (None, refs)
    operands = refs[number : number + 5]
    out_ref, *new_refs, field_ref, sums_ref = refs[number + 5 :]
    inside, own = masks(places())
    value, size = y_sum(mine_ref, pair_ref, other_ref)
    value = value * inside
    if number:
        value = value + DAMP * past[-1][...]
    if number == 3:
        inverse = 1.0 / size
        one, two = past[1][...], past[2][...]
        second = inverse * two - SHIFTS[1] * one
        value = inverse * (inverse * value - SHIFTS[1] * two) - SHIFTS[2] * second
        new_refs[1][...] = second
    elif number > 3:
        value = value / size - SHIFTS[number - 1] * past[-1][...]
    new_refs[0][...] = value
    image = apply_local(value, *operands, field_ref, sums_ref) * inside
    if number < 5:
        out_ref[...] = with_size(image, jnp.broadcast_to(size, (ROWS, LANES)))
        return
    new_refs[1][...] = jnp.broadcast_to(size, (8, LANES))
    mine = own * value
    late = [mine * ref[...] for ref in past] + [mine * value]
    late.append(value * image + DAMP * late[5])
    sums = jnp.concatenate([early_ref[...], row_sums(late, 8)], axis=0)
    sums = jnp.sum(sums, axis=1, keepdims=True)
    row = lax.broadcasted_iota(jnp.int32, (ROWS, LANES), 0)
    lane = lax.broadcasted_iota(jnp.int32, (ROWS, LANES), 1)
    line = jnp.sum(jnp.where(row == lane, sums, 0.0), axis=0, keepdims=True)
    own_parts(image, line, out_ref)
    new_refs[2][...] = image


def times(a, b):
    return None if a is None or b is None else a * b


def form(left, table, right):
    total = None
    for i, a in enumerate(left):
        inner = None
        for j, b in enumerate(right):
            inner = add(inner, times(table[i][j], b))
        total = add(total, times(a, inner))
    return total


def fast_kernel(in_ref, *refs):
    vectors = [ref[...] for ref in refs[:6]]
    size_ref, last_ref, solution_ref, residual_ref, good_ref = refs[6:]
    inside, _ = masks(places())
    value = own_sum(last_ref[...], in_ref)
    size = size_ref[0:1, 0:1]
    inverse = 1.0 / size
    image = (value * inside + DAMP * vectors[5]) * inverse
    total = total_of(in_ref)
    lane = lax.broadcasted_iota(jnp.int32, (1, LANES), 1)
    scalars = []
    for k in range(23):
        row, at = (0, 114 + k) if k < 14 else (1, 100 + k)
        scalars.append(jnp.sum(jnp.where(lane == at, total[row : row + 1], 0.0), axis=1, keepdims=True))
    gram = [[None] * 6 for _ in range(6)]
    k = 0
    for i in range(5):
        for j in range(i, 5):
            gram[i][j] = gram[j][i] = scalars[k]
            k += 1
    for i in range(6):
        gram[i][5] = gram[5][i] = scalars[16 + i]
    factor = [inverse] + [jnp.ones_like(inverse)] * 4
    energy = [[None] * 6 for _ in range(6)]
    for i in range(5):
        for j in range(i, 6):
            energy[i][j] = energy[j][i] = factor[i] * (gram[i + 1][j] + SHIFTS[i] * gram[i][j])
    energy[5][5] = scalars[22] * inverse
    rest = [row[:] for row in gram]
    good = jnp.ones_like(inverse)
    for k in range(6):
        good = jnp.where(rest[k][k] / gram[k][k] > WORST_PIVOT, good, 0.0)
        for i in range(k + 1, 6):
            ratio = rest[i][k] / rest[k][k]
            for j in range(i, 6):
                rest[i][j] = rest[i][j] - ratio * rest[k][j]
                rest[j][i] = rest[i][j]
    good_ref[0, 0] = jnp.sum(good).astype(jnp.int32)
    solved = [None] * 7
    residual = [jnp.ones_like(inverse)] + [None] * 6
    direction = residual[:]
    norm = gram[0][0]
    for number in range(ITERS):
        known = number + 1
        moved = [None] * 7
        for j in range(known):
            if j == 5:
                moved[6] = add(moved[6], direction[5])
            else:
                part = factor[j] * direction[j]
                moved[j + 1] = add(moved[j + 1], part)
                moved[j] = add(moved[j], SHIFTS[j] * part)
        step = norm / form(direction[:known], energy, direction[:known])
        solved = [add(a, times(step, b)) for a, b in zip(solved, direction)]
        residual = [add(a, times(-step, b)) for a, b in zip(residual, moved)]
        if number < ITERS - 1:
            known += 1
            later = form(residual[:known], gram, residual[:known])
            ratio = later / norm
            direction = [add(a, times(ratio, b)) for a, b in zip(residual, direction)]
            norm = later
    vectors = vectors + [image]
    first, second = None, None
    for j in range(7):
        if solved[j] is not None:
            first = add(first, solved[j] * vectors[j])
        second = add(second, residual[j] * vectors[j])
    write_out(first * (inverse / SCALE), second, solution_ref, residual_ref)


def write_out(solved, residual, solution_ref, residual_ref):
    both = jnp.concatenate([solved, residual], axis=0)
    value = dot(split3(both), put(), ((1,), (1,)))
    value = value[:48] + value[48:96] + value[96:]
    for z in range(CELLS_Z):
        for c in range(3):
            solution_ref[c, z] = value[c * 8 + 1 : c * 8 + 5, z * 16 : z * 16 + 16]
            residual_ref[c, z] = value[ROWS + c * 8 + 1 : ROWS + c * 8 + 5, z * 16 : z * 16 + 16]


def slow_kernel(vector_ref, grad_ref, rows_ref, back_ref, along_ref, lanes_ref, out_ref, field_ref, sums_ref):
    inside, own = masks(places())
    vector = vector_ref[...]
    image = apply_local(vector, grad_ref, rows_ref, back_ref, along_ref, lanes_ref, field_ref, sums_ref)
    message(vector, image * inside, own, out_ref)


def update(in_ref, old_ref, number):
    inside, own = masks(places())
    value, everything = along_y_sum(in_ref)
    residual = old_ref[ROWS : 2 * ROWS] if number else old_ref[...]
    image = value * inside + DAMP * residual
    norm = jnp.sum(everything[7:8], axis=1, keepdims=True)
    product = jnp.sum(everything[15:16], axis=1, keepdims=True) + DAMP * norm
    if number:
        ratio = norm / old_ref[4 * ROWS : 4 * ROWS + 1, 0:1]
        step = norm / (product - ratio * norm / old_ref[4 * ROWS + 1 : 4 * ROWS + 2, 0:1])
        direction = residual + ratio * old_ref[2 * ROWS : 3 * ROWS]
        image = image + ratio * old_ref[3 * ROWS : 4 * ROWS]
        solved = old_ref[0:ROWS] + step * direction
    else:
        step = norm / product
        direction = residual
        solved = step * direction
    residual = residual - step * image
    return own, inside, solved, residual, direction, image, norm, step


def step_kernel(number, in_ref, old_ref, grad_ref, rows_ref, back_ref, along_ref, lanes_ref, out_ref, new_ref, field_ref, sums_ref):
    own, inside, solved, residual, direction, image, norm, step = update(in_ref, old_ref, number)
    new_ref[0:ROWS] = solved
    new_ref[ROWS : 2 * ROWS] = residual
    new_ref[2 * ROWS : 3 * ROWS] = direction
    new_ref[3 * ROWS : 4 * ROWS] = image
    row = lax.broadcasted_iota(jnp.int32, (8, LANES), 0)
    new_ref[4 * ROWS : 4 * ROWS + 8] = jnp.where(row == 0, norm, step)
    image = apply_local(residual, grad_ref, rows_ref, back_ref, along_ref, lanes_ref, field_ref, sums_ref)
    message(residual, image * inside, own, out_ref)


def last_kernel(in_ref, old_ref, solution_ref, residual_ref):
    _, _, solved, residual, _, _, _, _ = update(in_ref, old_ref, ITERS - 1)
    write_out(solved / SCALE, residual, solution_ref, residual_ref)


def call(body, outs, *args, scratch=False):
    shapes = [
        jax.ShapeDtypeStruct(s, jnp.float32) if s else jax.ShapeDtypeStruct((1, 1), jnp.int32)
        for s in outs
    ]
    scratch_shapes = [pltpu.VMEM((96, 7 * LANES), jnp.float32)] * 2 if scratch else []
    vmem = pl.BlockSpec(memory_space=pltpu.VMEM)
    return pl.pallas_call(
        body,
        out_shape=shapes,
        in_specs=[vmem] * len(args),
        out_specs=[vmem if s else pl.BlockSpec(memory_space=pltpu.SMEM) for s in outs],
        scratch_shapes=scratch_shapes,
        compiler_params=pltpu.CompilerParams(vmem_limit_bytes=24 * 1024 * 1024),
    )(*args)


def swaps(axis):
    count = lax.axis_size(axis)
    pair = [(i, i ^ 1) for i in range(count)]
    other = [(i, (i + 1 if i % 2 else i - 1) % count) for i in range(count)]
    return pair, other


def shards(gradient, right_side):
    (gx, nx), (gy, ny), (gz, nz) = places()
    rows_x, back_x, along_y, lanes = [jnp.asarray(t) for t in tables()]
    rows_x = lax.dynamic_index_in_dim(rows_x, kind_of(gx, nx), 0, keepdims=False)
    along_y = lax.dynamic_index_in_dim(along_y, gz, 0, keepdims=False)
    lanes = lax.dynamic_index_in_dim(lanes, gz * 3 + kind_of(gy, ny), 0, keepdims=False)
    operands = (gradient, rows_x, back_x, along_y, lanes)
    group, line, box = (nx * nz, ROWS, LANES), (ny, ROWS, LANES), (ROWS, LANES)
    everyone = (nx * ny * nz, 4, LANES)
    tile, state, shape = (8, LANES), (4 * ROWS + 8, LANES), right_side.shape

    def exchange_all(sent):
        near = lax.all_to_all(sent, ("gx", "gz"), 0, 0)
        (sent,) = call(middle_kernel, [line], near)
        return lax.all_to_all(sent, "gy", 0, 0)

    def exchange_near(sent, size=None):
        swapped = lax.ppermute(sent, "gz", swaps("gz")[0])
        (sent,) = call(z_kernel, [box], sent, swapped)
        if size is not None:
            (sent,) = call(x_first_kernel, [box], sent, size)
        pair, other = [lax.ppermute(sent, "gx", s) for s in swaps("gx")]
        (sent,) = call(x_kernel, [box], sent, pair, other)
        pair, other = swaps("gy")
        other = lax.ppermute(sent, "gy", other)
        pair = lax.ppermute(sent, "gy", pair)
        return sent, pair, other

    def slow(first):
        (sent,) = call(slow_kernel, [group], first, *operands, scratch=True)
        old = first
        for number in range(ITERS - 1):
            body = functools.partial(step_kernel, number)
            sent, old = call(body, [group, state], exchange_all(sent), old, *operands, scratch=True)
        return tuple(call(last_kernel, [shape, shape], exchange_all(sent), old))

    (sent,) = call(start_kernel, [box], right_side)
    (size,) = call(size_kernel, [tile], gradient)
    vectors = []
    for number in range(6):
        near = exchange_near(sent, size if number == 0 else None)
        outs = [everyone if number == 5 else box, box] + [[], [], [], [box], [], [tile, box]][number]
        body = functools.partial(basis_kernel, number)
        early = call(early_kernel, [(16, LANES)], *vectors) if number == 5 else []
        sent, vector, *extra = call(
            body, outs, *near, *vectors, *early, *operands, scratch=True
        )
        if number == 3:
            vectors[2] = extra[0]
        vectors.append(vector)
    arrived = lax.all_to_all(sent, ("gx", "gy", "gz"), 0, 0)
    *fast, good = call(fast_kernel, [shape, shape, None], arrived, *vectors, *extra)
    return lax.cond(good[0, 0] > 0, lambda first: tuple(fast), slow, vectors[0])


def solution(mesh):
    placed = P(None, "gz", "gx", "gy")
    return jax.shard_map(
        shards,
        mesh=mesh,
        in_specs=(placed, placed),
        out_specs=(placed, placed),
        check_vma=False,
    )
```

```python
import functools

import jax
import jax.numpy as jnp
import ml_dtypes
import numpy as np
from jax import lax
from jax.experimental import pallas as pl
from jax.experimental.pallas import tpu as pltpu
from jax.sharding import PartitionSpec as P

ITERS = 6
SMOOTHING = 0.5
DAMPING = 0.05
HIGHEST = lax.Precision.HIGHEST

CELLS_Z, CELLS_X, CELLS_Y = 4, 4, 16
BOX_X, BOX_Y, BOX_Z = 7, 19, 6
LANES = 128
ROWS = 24
DENOMINATOR = 3072.0
SCALE = 512.0
DAMP = DAMPING / SCALE
SHIFTS = (0.0, 0.171, 0.452, 0.776, 0.114)
WORST_PIVOT = 0.05
SPARE = ((4, 0, 76), (4, 1, 38), (5, 2, 76), (5, 3, 38))


def numerators(t):
    return (
        (8 - t) ** 3,
        3 * t**3 - 48 * t**2 + 2048,
        -3 * t**3 + 24 * t**2 + 192 * t + 512,
        t**3,
    )


WEIGHTS = [[n / DENOMINATOR for n in numerators(t)] for t in range(8)]


def basis(cells):
    table = np.zeros((8 * cells + 1, cells + 3 + 1))
    for voxel in range(8 * cells + 1):
        for k, n in enumerate(numerators(voxel % 8)):
            table[voxel, voxel // 8 + k] = n
    return table[:, :-1]


def mass_and_edges(cells, first, last):
    table = basis(cells) / DENOMINATOR
    own = table[:-1]
    steps = table[1:] - table[:-1]
    if last:
        steps[-1] = -table[-2]
    edges = steps.T @ steps
    if first:
        edges = edges + np.outer(table[0], table[0])
    return own.T @ own, edges


def place_z(matrix, part):
    return matrix[1:7, 1:7] if part == 0 else matrix[0:6, 0:6]


def stacked(table):
    high = table.astype(ml_dtypes.bfloat16)
    rest = table - high.astype(table.dtype)
    middle = rest.astype(ml_dtypes.bfloat16)
    low = (rest - middle.astype(table.dtype)).astype(ml_dtypes.bfloat16)
    return np.concatenate([high, high, high, middle, middle, low], axis=-1)


@functools.lru_cache(None)
def tables():
    bx = basis(CELLS_X)[:-1]
    expand = np.zeros((96, ROWS))
    for c in range(3):
        expand[c * 32 : c * 32 + 32, c * 8 : c * 8 + BOX_X] = bx / DENOMINATOR / DENOMINATOR
    rows_x = np.zeros((3, 144, ROWS), np.float32)
    for kind in range(3):
        mass, edges = mass_and_edges(CELLS_X, kind == 0, kind == 2)
        rows_x[kind, :96] = expand
        for c in range(3):
            at = slice(c * 8, c * 8 + BOX_X)
            rows_x[kind, 96 + c * 8 : 96 + c * 8 + BOX_X, at] = SMOOTHING / SCALE * mass
            rows_x[kind, 120 + c * 8 : 120 + c * 8 + BOX_X, at] = SMOOTHING / SCALE * edges
    by = basis(CELLS_Y)[:-1]
    along_y = np.zeros((2, 2, LANES, 7 * LANES))
    for part in range(2):
        for f in range(BOX_Z):
            g = f + 1 if part == 0 else f
            low = by.T.astype(ml_dtypes.bfloat16).astype(np.float64)
            at = slice(f * BOX_Y, (f + 1) * BOX_Y)
            along_y[part, 0, at, g * LANES : (g + 1) * LANES] = low
            along_y[part, 1, at, g * LANES : (g + 1) * LANES] = by.T - low
    along_y = along_y.reshape(2, 256, 7 * LANES).astype(ml_dtypes.bfloat16)
    lanes = np.zeros((2, 3, 256, LANES))
    for part in range(2):
        mz, kz = mass_and_edges(CELLS_Z, part == 0, part == 1)
        mz, kz = place_z(mz, part), place_z(kz, part)
        for kind in range(3):
            my, ky = mass_and_edges(CELLS_Y, kind == 0, kind == 2)
            used = BOX_Z * BOX_Y
            lanes[part, kind, :used, :used] = np.kron(kz, my) + np.kron(mz, ky)
            lanes[part, kind, 128 : 128 + used, :used] = np.kron(mz, my)
    return (
        stacked(rows_x.astype(np.float64)),
        stacked(expand.T / SCALE),
        along_y,
        stacked(lanes.reshape(6, 256, LANES))[..., [*range(LANES), *range(3 * LANES, 4 * LANES)]],
    )


def iotas():
    row = lax.broadcasted_iota(jnp.int32, (ROWS, LANES), 0)
    lane = lax.broadcasted_iota(jnp.int32, (ROWS, LANES), 1)
    f = jnp.zeros_like(lane)
    for k in range(1, BOX_Z + 1):
        f = f + (lane >= k * BOX_Y).astype(jnp.int32)
    return row & 7, f, lane - f * BOX_Y


def masks(where):
    (gx, nx), (gy, ny), (gz, nz) = where
    kx, f, e = iotas()
    low_x, high_x = jnp.where(gx == 0, 1, 0), jnp.where(gx == nx - 1, 4, 6)
    low_y, high_y = jnp.where(gy == 0, 1, 0), jnp.where(gy == ny - 1, 16, 18)
    high_z = jnp.where(gz == 0, 5, 4)
    inside = (kx >= low_x) & (kx <= high_x) & (e >= low_y) & (e <= high_y) & (f <= high_z)
    own_z = jnp.where(gz == 0, 0, 1)
    own = (kx >= 1) & (kx <= 4) & (e >= 1) & (e <= 16) & (f >= own_z) & (f <= own_z + 3)
    return inside.astype(jnp.float32), own.astype(jnp.float32)


def places():
    return tuple((lax.axis_index(a), lax.axis_size(a)) for a in ("gx", "gy", "gz"))


def add(a, b):
    return b if a is None else a if b is None else a + b


def split3(value):
    high = value.astype(jnp.bfloat16)
    rest = value - high.astype(jnp.float32)
    middle = rest.astype(jnp.bfloat16)
    low = (rest - middle.astype(jnp.float32)).astype(jnp.bfloat16)
    return jnp.concatenate([high, middle, low], axis=0)


def pieces6(value):
    pieces = split3(value)
    count = value.shape[0]
    return jnp.concatenate([pieces, pieces[: 2 * count], pieces[:count]], axis=0)


def dot(a, b, dims=((1,), (0,)), precision=None):
    return lax.dot_general(
        a, b, (dims, ((), ())), precision=precision, preferred_element_type=jnp.float32
    )


def kind_of(index, count):
    return jnp.where(index == 0, 0, jnp.where(index == count - 1, 2, 1))


def apply_local(vector, grad_ref, rows_ref, back_ref, along_ref, lanes_ref, field_ref, sums_ref):
    first = dot(rows_ref[...], pieces6(vector))
    pieces = split3(first[:96])[:192]
    field = dot(jnp.concatenate([pieces, pieces], axis=1), along_ref[...])
    field_ref[...] = field[:96] + field[96:192]

    def column(cx, carry):
        rows = [pl.ds(pl.multiple_of(c * 32 + cx * 8, 8), 8) for c in range(3)]
        inside = pl.ds(pl.multiple_of(cx * 8, 8), 8)
        total = [[None] * 4 for _ in range(3)]
        for cz in range(CELLS_Z):
            layer = [
                [field_ref[rows[c], (cz + k) * LANES : (cz + k + 1) * LANES] for k in range(4)]
                for c in range(3)
            ]

            def weighted(t, values):
                slope = [grad_ref[c, cz * 8 + t, inside, :] for c in range(3)]
                shade = slope[0] * values[0] + slope[1] * values[1] + slope[2] * values[2]
                return [slope[c] * shade for c in range(3)]

            edge, near = WEIGHTS[0][0], WEIGHTS[0][1]
            value = weighted(0, [edge * (v[0] + v[2]) + near * v[1] for v in layer])
            first = [edge * v for v in value]
            second = [near * v for v in value]
            outer = [v[0] + v[3] for v in layer]
            inner = [v[1] + v[2] for v in layer]
            outer_odd = [v[0] - v[3] for v in layer]
            inner_odd = [v[1] - v[2] for v in layer]
            edge, near = WEIGHTS[4][0], WEIGHTS[4][1]
            value = weighted(4, [edge * a + near * b for a, b in zip(outer, inner)])
            sums = [[edge * v, near * v, None, None] for v in value]
            for t in (1, 2, 3):
                w = WEIGHTS[t]
                a, b, p, q = (w[0] + w[3]) / 2, (w[1] + w[2]) / 2, (w[0] - w[3]) / 2, (w[1] - w[2]) / 2
                even = [a * outer[c] + b * inner[c] for c in range(3)]
                odd = [p * outer_odd[c] + q * inner_odd[c] for c in range(3)]
                one = weighted(t, [even[c] + odd[c] for c in range(3)])
                two = weighted(8 - t, [even[c] - odd[c] for c in range(3)])
                for c in range(3):
                    plus, minus = one[c] + two[c], one[c] - two[c]
                    terms = (a * plus, b * plus, p * minus, q * minus)
                    sums[c] = [add(x, y) for x, y in zip(sums[c], terms)]
            for c in range(3):
                outside, middle, outside_odd, middle_odd = sums[c]
                parts = (
                    outside + outside_odd + first[c],
                    middle + middle_odd + second[c],
                    middle - middle_odd + first[c],
                    outside - outside_odd,
                )
                total[c] = [add(x, y) for x, y in zip(total[c], parts)]
                sums_ref[rows[c], cz * LANES : (cz + 1) * LANES] = total[c][0]
                total[c] = total[c][1:] + [None]
        for c in range(3):
            for k in range(3):
                g = CELLS_Z + k
                sums_ref[rows[c], g * LANES : (g + 1) * LANES] = total[c][k]
        return carry

    lax.fori_loop(0, CELLS_X, column, 0, unroll=True)
    pieces = split3(sums_ref[...])[:192]
    back = dot(pieces, along_ref[...], ((1,), (1,)))
    back = back[:, :LANES] + back[:, LANES:]
    back = back[:96] + back[96:192]
    data = dot(back_ref[...], pieces6(back))
    relief = dot(split3(jnp.concatenate([first[96:120], first[120:144]], axis=1)), lanes_ref[...])
    relief = relief[:, :LANES] + relief[:, LANES:]
    relief = relief[:ROWS] + relief[ROWS : 2 * ROWS] + relief[2 * ROWS :]
    return data + relief


def roll(value, shift, axis):
    return pltpu.roll(value, shift, axis)


def put():
    first_f = jnp.where(lax.axis_index("gz") == 0, 0, 1)
    row = lax.broadcasted_iota(jnp.int32, (64, LANES), 0)
    lane = lax.broadcasted_iota(jnp.int32, (64, LANES), 1)
    target = ((row >> 4) + first_f) * BOX_Y + 1 + (row & 15)
    return (lane == target).astype(jnp.float32).astype(jnp.bfloat16)


def start_kernel(right_ref, out_ref):
    parts = []
    for c in range(3):
        own = jnp.concatenate([right_ref[c, z] for z in range(CELLS_Z)], axis=1)
        parts += [jnp.zeros((1, 64), jnp.float32), own, jnp.zeros((3, 64), jnp.float32)]
    value = dot(split3(jnp.concatenate(parts, axis=0)), put())
    out_ref[...] = value[:ROWS] + value[ROWS : 2 * ROWS] + value[2 * ROWS :]


def size_kernel(grad_ref, out_ref):
    def plane(z, totals):
        totals = list(totals)
        for x in range(4):
            slope = [grad_ref[c, z, x * 8 : x * 8 + 8, :] for c in range(3)]
            k = 0
            for a in range(3):
                for b in range(a, 3):
                    totals[k] = totals[k] + slope[a] * slope[b]
                    k += 1
        return tuple(totals)

    zero = jnp.zeros((8, LANES), jnp.float32)
    totals = lax.fori_loop(0, 32, plane, (zero,) * 6)
    count = 32.0 * 32.0 * 128.0
    xx, xy, xz, yy, yz, zz = [
        jnp.sum(jnp.sum(t, axis=0, keepdims=True), axis=1, keepdims=True) / count for t in totals
    ]
    aa = xx * xx + xy * xy + xz * xz
    bb = xy * xy + yy * yy + yz * yz
    cc = xz * xz + yz * yz + zz * zz
    ab = xx * xy + xy * yy + xz * yz
    ac = xx * xz + xy * yz + xz * zz
    bc = xy * xz + yy * yz + yz * zz
    norm = aa * aa + bb * bb + cc * cc + 2.0 * (ab * ab + ac * ac + bc * bc)
    size = 0.73 * jnp.sqrt(jnp.sqrt(norm)) + 0.04
    row = lax.broadcasted_iota(jnp.int32, (8, LANES), 0)
    out_ref[...] = jnp.where(row == 7, jnp.broadcast_to(size, (8, LANES)), 0.0)


def with_size(value, *others):
    row = lax.broadcasted_iota(jnp.int32, (ROWS, LANES), 0)
    return jnp.where(row == 7, functools.reduce(jnp.maximum, others), value)


def pair_sides(index, pair, other):
    even = lax.rem(index, 2) == 0
    return jnp.where(even, other, pair), jnp.where(even, pair, other)


def z_kernel(mine_ref, swap_ref, out_ref):
    gz = lax.axis_index("gz")
    _, f, _ = iotas()
    mine, swap = mine_ref[...], swap_ref[...]
    other = roll(swap, jnp.where(gz == 0, 3 * BOX_Y, LANES - 3 * BOX_Y), 1)
    first_f = jnp.where(gz == 0, 3, 0)
    value = mine + jnp.where((f >= first_f) & (f <= first_f + 2), other, 0.0)
    out_ref[...] = with_size(value, mine, swap)


def x_kernel(mine_ref, pair_ref, other_ref, *rest):
    out_ref = rest[-1]
    gx, nx = lax.axis_index("gx"), lax.axis_size("gx")
    kx, _, _ = iotas()
    mine, pair, other = mine_ref[...], pair_ref[...], other_ref[...]
    low, high = pair_sides(gx, pair, other)
    first_x, last_x = jnp.where(gx > 0, 2, -1), jnp.where(gx < nx - 1, 4, 8)
    value = mine + jnp.where(kx <= first_x, rows_rolled(low, 4), 0.0)
    value = value + jnp.where((kx >= last_x) & (kx <= 6), rows_rolled(high, 4), 0.0)
    out_ref[...] = with_size(value, mine, pair, other)


def x_first_kernel(mine_ref, size_ref, out_ref):
    out_ref[...] = mine_ref[...]
    row = lax.broadcasted_iota(jnp.int32, (8, LANES), 0)
    out_ref[0:8] = jnp.where(row == 7, size_ref[...], mine_ref[0:8])


def y_sum(mine_ref, pair_ref, other_ref):
    gy, ny = lax.axis_index("gy"), lax.axis_size("gy")
    _, _, e = iotas()
    mine, pair, other = mine_ref[...], pair_ref[...], other_ref[...]
    low, high = pair_sides(gy, pair, other)
    first_y, last_y = jnp.where(gy > 0, 2, -1), jnp.where(gy < ny - 1, 16, LANES)
    value = mine + jnp.where(e <= first_y, roll(low, LANES - 16, 1), 0.0)
    value = value + jnp.where(e >= last_y, roll(high, 16, 1), 0.0)
    return value, jnp.maximum(jnp.maximum(mine, pair), other)[7:8]


def rows_rolled(value, shift):
    return jnp.concatenate(
        [roll(value[c * 8 : c * 8 + 8], shift, 0) for c in range(3)], axis=0
    )


def middle_kernel(in_ref, out_ref):
    (gx, nx), _, (gz, nz) = places()
    kx, f, e = iotas()
    has_low = (gx > 0).astype(jnp.int32)
    has_high = (gx < nx - 1).astype(jnp.int32)
    low = jnp.maximum(gx - 1, 0)
    high = jnp.minimum(gx + 1, nx - 1)
    take_low = (kx <= 2) & (has_low == 1)
    take_high = (kx >= 4) & (kx <= 6) & (has_high == 1)

    def along_x(part):
        value = in_ref[gx * nz + part]
        below = rows_rolled(in_ref[low * nz + part], 4)
        above = rows_rolled(in_ref[high * nz + part], 4)
        value = value + jnp.where(take_low, below, 0.0)
        return value + jnp.where(take_high, above, 0.0)

    mine = along_x(gz)
    other = along_x(1 - gz)
    other = roll(other, jnp.where(gz == 0, 3 * BOX_Y, LANES - 3 * BOX_Y), 1)
    first_f = jnp.where(gz == 0, 3, 0)
    value = mine + jnp.where((f >= first_f) & (f <= first_f + 2), other, 0.0)
    everything = in_ref[0]
    for i in range(1, in_ref.shape[0]):
        everything = everything + in_ref[i]
    value = jnp.where(kx == 7, everything, value)
    for i in range(out_ref.shape[0]):
        out_ref[i] = value


def along_y_sum(in_ref):
    _, (gy, ny), _ = places()
    kx, f, e = iotas()
    has_low = (gy > 0).astype(jnp.int32)
    has_high = (gy < ny - 1).astype(jnp.int32)
    below = roll(in_ref[jnp.maximum(gy - 1, 0)], LANES - 16, 1)
    above = roll(in_ref[jnp.minimum(gy + 1, ny - 1)], 16, 1)
    value = in_ref[gy]
    value = value + jnp.where((e <= 2) & (has_low == 1), below, 0.0)
    value = value + jnp.where((e >= 16) & (has_high == 1), above, 0.0)
    everything = in_ref[0]
    for i in range(1, in_ref.shape[0]):
        everything = everything + in_ref[i]
    return value, everything


def message(vector, image, own, out_ref):
    norm = jnp.sum(own * vector * vector, axis=0, keepdims=True)
    product = jnp.sum(vector * image, axis=0, keepdims=True)
    row = lax.broadcasted_iota(jnp.int32, (ROWS, LANES), 0)
    value = jnp.where(row == 7, norm, image)
    value = jnp.where(row == 15, product, value)
    for i in range(out_ref.shape[0]):
        out_ref[i] = value


def total_of(in_ref):
    values = [in_ref[i] for i in range(in_ref.shape[0])]
    while len(values) > 1:
        values = [a + b for a, b in zip(values[::2], values[1::2])]
    return values[0]


def tile_parts():
    kx, f, e = (v[0:8] for v in iotas())
    return kx, f, e, lax.broadcasted_iota(jnp.int32, (8, LANES), 1)


def own_parts(image, line, out_ref):
    (gx, nx), (gy, ny), (gz, nz) = places()
    row, f, e, lane = tile_parts()
    parts = [image[c * 8 : c * 8 + 8] for c in range(3)]
    six = jnp.zeros((8, LANES), jnp.float32)
    before, other_z, beside_y = six, six, six
    layers = 2 * BOX_Y
    start = jnp.where(gz == 0, 4 * BOX_Y, 0)
    for c, part in enumerate(parts):
        here = (row == 2 * c) | (row == 2 * c + 1)
        six = jnp.where(here, roll(part, (2 * c + 3) % 8, 0), six)
        before = jnp.where(row == c, roll(part, c, 0), before)
        part = roll(part, 7, 0)
        packed = roll(part, lax.rem(layers * c - start + LANES, LANES), 1)
        other_z = jnp.where((lane >= layers * c) & (lane < layers * c + layers), packed, other_z)
        beside_y = jnp.where(e == c, roll(part, c, 1), beside_y)
        here = (e == 17 - 2 * c) | (e == 18 - 2 * c)
        beside_y = jnp.where(here, roll(part, (LANES - 2 * c) % LANES, 1), beside_y)
    own = roll(six, jnp.where(gz == 0, 0, LANES - BOX_Y), 1)
    after = own
    for source, target, shift in SPARE:
        moved = roll(roll(own, (target - source) % 8, 0), shift, 1)
        after = jnp.where((row == target) & (lane >= 2 * layers), moved, after)
    own = roll(six, jnp.where(gz == 0, LANES - 4 * BOX_Y, 0), 1)
    after_z = jnp.where(lane < layers, own, roll(roll(own, 4, 0), layers, 1))
    values = (after, after_z, before, other_z, beside_y)
    scalars = jnp.where(row == 0, roll(line, 114, 1), roll(line, 100, 1))
    after, after_z, before, other_z, beside_y = [
        jnp.where(lane >= BOX_Z * BOX_Y, scalars, v)[0:4] for v in values
    ]
    for x in range(nx):
        for z in range(nz):
            same = gz == z
            value = jnp.where(gx == x, jnp.where(same, beside_y, other_z), before)
            value = jnp.where(gx + 1 == x, jnp.where(same, after, after_z), value)
            for y in range(ny):
                out_ref[(x * ny + y) * nz + z] = value


def own_sum(image, in_ref):
    (gx, nx), (gy, ny), (gz, nz) = places()
    row, f, e, lane = tile_parts()
    lower_y, upper_y = gy > 0, gy < ny - 1
    below_y, above_y = jnp.maximum(gy - 1, 0), jnp.minimum(gy + 1, ny - 1)
    below_mask = ((e == 1) | (e == 2)) & lower_y
    above_mask = (e == 16) & upper_y
    first_f, last_f = jnp.where(gz == 0, 3, 1), jnp.where(gz == 0, 3, 2)
    z_mask = (f >= first_f) & (f <= last_f)
    nothing = jnp.zeros((4, LANES), jnp.float32)

    def tile(x, y, z):
        return jnp.concatenate([in_ref[(x * ny + y) * nz + z], nothing], axis=0)

    def over_y(x, z):
        value = tile(x, gy, z)
        value = value + jnp.where(below_mask, roll(tile(x, below_y, z), LANES - 16, 1), 0.0)
        return value + jnp.where(above_mask, roll(tile(x, above_y, z), 16, 1), 0.0)

    layers = 2 * BOX_Y
    z_start = jnp.where(gz == 0, 3 * BOX_Y, BOX_Y)
    packed = over_y(jnp.maximum(gx - 1, 0), gz)
    six = packed
    for source, target, shift in SPARE:
        moved = roll(roll(packed, (source - target) % 8, 0), LANES - shift, 1)
        first = 2 * layers - shift
        six = jnp.where((row == source) & (lane >= first) & (lane < first + layers), moved, six)
    six = roll(six, jnp.where(gz == 0, 0, BOX_Y), 1)
    packed = over_y(jnp.maximum(gx - 1, 0), 1 - gz)
    moved = jnp.where(row < 4, packed, roll(roll(packed, 4, 0), LANES - layers, 1))
    from_before = six + jnp.where(z_mask, roll(moved, z_start, 1), 0.0)
    above_x = jnp.minimum(gx + 1, nx - 1)
    moved = roll(over_y(above_x, 1 - gz), jnp.where(gz == 0, 3 * BOX_Y, LANES - 3 * BOX_Y), 1)
    from_after = over_y(above_x, gz) + jnp.where(z_mask, moved, 0.0)
    from_z = roll(over_y(gx, 1 - gz), 1, 0)
    from_below, from_above = roll(tile(gx, below_y, gz), 1, 0), roll(tile(gx, above_y, gz), 1, 0)
    own_rows = (row >= 1) & (row <= 4)
    sums = []
    for c in range(3):
        value = image[c * 8 : c * 8 + 8]
        here = ((row == 1) | (row == 2)) & (gx > 0)
        value = value + jnp.where(here, roll(from_before, (1 - 2 * c) % 8, 0), 0.0)
        here = (row == 4) & (gx < nx - 1)
        value = value + jnp.where(here, roll(from_after, 4 - c, 0), 0.0)
        moved = roll(from_z, lax.rem(z_start - layers * c + LANES, LANES), 1)
        value = value + jnp.where(own_rows & z_mask, moved, 0.0)
        moved = roll(from_below, LANES - 16 + 2 * c, 1)
        value = value + jnp.where(own_rows & below_mask, moved, 0.0)
        moved = roll(from_above, 16 - c, 1)
        value = value + jnp.where(own_rows & above_mask, moved, 0.0)
        sums.append(value)
    return jnp.concatenate(sums, axis=0)


def row_sums(products, rows):
    sums = [jnp.sum(p, axis=0, keepdims=True) for p in products]
    return jnp.concatenate(sums + [jnp.zeros((rows - len(sums), LANES), jnp.float32)], axis=0)


def early_kernel(*refs):
    _, own = masks(places())
    vectors = [ref[...] for ref in refs[:5]]
    products = []
    for i in range(5):
        mine = own * vectors[i]
        products += [mine * vectors[j] for j in range(i, 5)]
    refs[5][...] = row_sums(products, 16)


def basis_kernel(number, mine_ref, pair_ref, other_ref, *refs):
    past = refs[:number]
    early_ref, refs = (refs[number], refs[1:]) if number == 5 else (None, refs)
    operands = refs[number : number + 5]
    out_ref, *new_refs, field_ref, sums_ref = refs[number + 5 :]
    inside, own = masks(places())
    value, size = y_sum(mine_ref, pair_ref, other_ref)
    value = value * inside
    if number:
        value = value + DAMP * past[-1][...]
    if number == 3:
        inverse = 1.0 / size
        one, two = past[1][...], past[2][...]
        second = inverse * two - SHIFTS[1] * one
        value = inverse * (inverse * value - SHIFTS[1] * two) - SHIFTS[2] * second
        new_refs[1][...] = second
    elif number > 3:
        value = value / size - SHIFTS[number - 1] * past[-1][...]
    new_refs[0][...] = value
    image = apply_local(value, *operands, field_ref, sums_ref) * inside
    if number < 5:
        out_ref[...] = with_size(image, jnp.broadcast_to(size, (ROWS, LANES)))
        return
    new_refs[1][...] = jnp.broadcast_to(size, (8, LANES))
    mine = own * value
    late = [mine * ref[...] for ref in past] + [mine * value]
    late.append(value * image + DAMP * late[5])
    sums = jnp.concatenate([early_ref[...], row_sums(late, 8)], axis=0)
    sums = jnp.sum(sums, axis=1, keepdims=True)
    row = lax.broadcasted_iota(jnp.int32, (ROWS, LANES), 0)
    lane = lax.broadcasted_iota(jnp.int32, (ROWS, LANES), 1)
    line = jnp.sum(jnp.where(row == lane, sums, 0.0), axis=0, keepdims=True)
    own_parts(image, line, out_ref)
    new_refs[2][...] = image


def times(a, b):
    return None if a is None or b is None else a * b


def form(left, table, right):
    total = None
    for i, a in enumerate(left):
        inner = None
        for j, b in enumerate(right):
            inner = add(inner, times(table[i][j], b))
        total = add(total, times(a, inner))
    return total


def fast_kernel(in_ref, *refs):
    vectors = [ref[...] for ref in refs[:6]]
    size_ref, last_ref, solution_ref, residual_ref, good_ref = refs[6:]
    inside, _ = masks(places())
    value = own_sum(last_ref[...], in_ref)
    size = size_ref[0:1, 0:1]
    inverse = 1.0 / size
    image = (value * inside + DAMP * vectors[5]) * inverse
    total = total_of(in_ref)
    lane = lax.broadcasted_iota(jnp.int32, (1, LANES), 1)
    scalars = []
    for k in range(23):
        row, at = (0, 114 + k) if k < 14 else (1, 100 + k)
        scalars.append(jnp.sum(jnp.where(lane == at, total[row : row + 1], 0.0), axis=1, keepdims=True))
    gram = [[None] * 6 for _ in range(6)]
    k = 0
    for i in range(5):
        for j in range(i, 5):
            gram[i][j] = gram[j][i] = scalars[k]
            k += 1
    for i in range(6):
        gram[i][5] = gram[5][i] = scalars[16 + i]
    factor = [inverse] + [jnp.ones_like(inverse)] * 4
    energy = [[None] * 6 for _ in range(6)]
    for i in range(5):
        for j in range(i, 6):
            energy[i][j] = energy[j][i] = factor[i] * (gram[i + 1][j] + SHIFTS[i] * gram[i][j])
    energy[5][5] = scalars[22] * inverse
    rest = [row[:] for row in gram]
    good = jnp.ones_like(inverse)
    for k in range(6):
        good = jnp.where(rest[k][k] / gram[k][k] > WORST_PIVOT, good, 0.0)
        for i in range(k + 1, 6):
            ratio = rest[i][k] / rest[k][k]
            for j in range(i, 6):
                rest[i][j] = rest[i][j] - ratio * rest[k][j]
                rest[j][i] = rest[i][j]
    good_ref[0, 0] = jnp.sum(good).astype(jnp.int32)
    solved = [None] * 7
    residual = [jnp.ones_like(inverse)] + [None] * 6
    direction = residual[:]
    norm = gram[0][0]
    for number in range(ITERS):
        known = number + 1
        moved = [None] * 7
        for j in range(known):
            if j == 5:
                moved[6] = add(moved[6], direction[5])
            else:
                part = factor[j] * direction[j]
                moved[j + 1] = add(moved[j + 1], part)
                moved[j] = add(moved[j], SHIFTS[j] * part)
        step = norm / form(direction[:known], energy, direction[:known])
        solved = [add(a, times(step, b)) for a, b in zip(solved, direction)]
        residual = [add(a, times(-step, b)) for a, b in zip(residual, moved)]
        if number < ITERS - 1:
            known += 1
            later = form(residual[:known], gram, residual[:known])
            ratio = later / norm
            direction = [add(a, times(ratio, b)) for a, b in zip(residual, direction)]
            norm = later
    vectors = vectors + [image]
    first, second = None, None
    for j in range(7):
        if solved[j] is not None:
            first = add(first, solved[j] * vectors[j])
        second = add(second, residual[j] * vectors[j])
    write_out(first * (inverse / SCALE), second, solution_ref, residual_ref)


def write_out(solved, residual, solution_ref, residual_ref):
    both = jnp.concatenate([solved, residual], axis=0)
    value = dot(split3(both), put(), ((1,), (1,)))
    value = value[:48] + value[48:96] + value[96:]
    for z in range(CELLS_Z):
        for c in range(3):
            solution_ref[c, z] = value[c * 8 + 1 : c * 8 + 5, z * 16 : z * 16 + 16]
            residual_ref[c, z] = value[ROWS + c * 8 + 1 : ROWS + c * 8 + 5, z * 16 : z * 16 + 16]


def slow_kernel(vector_ref, grad_ref, rows_ref, back_ref, along_ref, lanes_ref, out_ref, field_ref, sums_ref):
    inside, own = masks(places())
    vector = vector_ref[...]
    image = apply_local(vector, grad_ref, rows_ref, back_ref, along_ref, lanes_ref, field_ref, sums_ref)
    message(vector, image * inside, own, out_ref)


def update(in_ref, old_ref, number):
    inside, own = masks(places())
    value, everything = along_y_sum(in_ref)
    residual = old_ref[ROWS : 2 * ROWS] if number else old_ref[...]
    image = value * inside + DAMP * residual
    norm = jnp.sum(everything[7:8], axis=1, keepdims=True)
    product = jnp.sum(everything[15:16], axis=1, keepdims=True) + DAMP * norm
    if number:
        ratio = norm / old_ref[4 * ROWS : 4 * ROWS + 1, 0:1]
        step = norm / (product - ratio * norm / old_ref[4 * ROWS + 1 : 4 * ROWS + 2, 0:1])
        direction = residual + ratio * old_ref[2 * ROWS : 3 * ROWS]
        image = image + ratio * old_ref[3 * ROWS : 4 * ROWS]
        solved = old_ref[0:ROWS] + step * direction
    else:
        step = norm / product
        direction = residual
        solved = step * direction
    residual = residual - step * image
    return own, inside, solved, residual, direction, image, norm, step


def step_kernel(number, in_ref, old_ref, grad_ref, rows_ref, back_ref, along_ref, lanes_ref, out_ref, new_ref, field_ref, sums_ref):
    own, inside, solved, residual, direction, image, norm, step = update(in_ref, old_ref, number)
    new_ref[0:ROWS] = solved
    new_ref[ROWS : 2 * ROWS] = residual
    new_ref[2 * ROWS : 3 * ROWS] = direction
    new_ref[3 * ROWS : 4 * ROWS] = image
    row = lax.broadcasted_iota(jnp.int32, (8, LANES), 0)
    new_ref[4 * ROWS : 4 * ROWS + 8] = jnp.where(row == 0, norm, step)
    image = apply_local(residual, grad_ref, rows_ref, back_ref, along_ref, lanes_ref, field_ref, sums_ref)
    message(residual, image * inside, own, out_ref)


def last_kernel(in_ref, old_ref, solution_ref, residual_ref):
    _, _, solved, residual, _, _, _, _ = update(in_ref, old_ref, ITERS - 1)
    write_out(solved / SCALE, residual, solution_ref, residual_ref)


def call(body, outs, *args, scratch=False):
    shapes = [
        jax.ShapeDtypeStruct(s, jnp.float32) if s else jax.ShapeDtypeStruct((1, 1), jnp.int32)
        for s in outs
    ]
    scratch_shapes = [pltpu.VMEM((96, 7 * LANES), jnp.float32)] * 2 if scratch else []
    vmem = pl.BlockSpec(memory_space=pltpu.VMEM)
    return pl.pallas_call(
        body,
        out_shape=shapes,
        in_specs=[vmem] * len(args),
        out_specs=[vmem if s else pl.BlockSpec(memory_space=pltpu.SMEM) for s in outs],
        scratch_shapes=scratch_shapes,
        compiler_params=pltpu.CompilerParams(vmem_limit_bytes=24 * 1024 * 1024),
    )(*args)


def swaps(axis):
    count = lax.axis_size(axis)
    pair = [(i, i ^ 1) for i in range(count)]
    other = [(i, (i + 1 if i % 2 else i - 1) % count) for i in range(count)]
    return pair, other


def shards(gradient, right_side):
    (gx, nx), (gy, ny), (gz, nz) = places()
    rows_x, back_x, along_y, lanes = [jnp.asarray(t) for t in tables()]
    rows_x = lax.dynamic_index_in_dim(rows_x, kind_of(gx, nx), 0, keepdims=False)
    lanes = lax.dynamic_index_in_dim(lanes, gz * 3 + kind_of(gy, ny), 0, keepdims=False)
    group, line, box = (nx * nz, ROWS, LANES), (ny, ROWS, LANES), (ROWS, LANES)
    everyone = (nx * ny * nz, 4, LANES)
    tile, state, shape = (8, LANES), (4 * ROWS + 8, LANES), right_side.shape

    def exchange_all(sent):
        near = lax.all_to_all(sent, ("gx", "gz"), 0, 0)
        (sent,) = call(middle_kernel, [line], near)
        return lax.all_to_all(sent, "gy", 0, 0)

    def exchange_near(sent, size=None):
        swapped = lax.ppermute(sent, "gz", swaps("gz")[0])
        (sent,) = call(z_kernel, [box], sent, swapped)
        if size is not None:
            (sent,) = call(x_first_kernel, [box], sent, size)
            sent, part = lax.optimization_barrier((sent, gz))
            picked.append(lax.dynamic_index_in_dim(along_y, part, 0, keepdims=False))
        pair, other = [lax.ppermute(sent, "gx", s) for s in swaps("gx")]
        (sent,) = call(x_kernel, [box], sent, pair, other)
        pair, other = swaps("gy")
        other = lax.ppermute(sent, "gy", other)
        pair = lax.ppermute(sent, "gy", pair)
        return sent, pair, other

    (sent,) = call(start_kernel, [box], right_side)
    (size,) = call(size_kernel, [tile], gradient)
    picked = []
    near = exchange_near(sent, size)
    operands = (gradient, rows_x, back_x, picked[0], lanes)

    def slow(first):
        (sent,) = call(slow_kernel, [group], first, *operands, scratch=True)
        old = first
        for number in range(ITERS - 1):
            body = functools.partial(step_kernel, number)
            sent, old = call(body, [group, state], exchange_all(sent), old, *operands, scratch=True)
        return tuple(call(last_kernel, [shape, shape], exchange_all(sent), old))

    vectors = []
    for number in range(6):
        if number:
            near = exchange_near(sent)
        outs = [everyone if number == 5 else box, box] + [[], [], [], [box], [], [tile, box]][number]
        body = functools.partial(basis_kernel, number)
        early = call(early_kernel, [(16, LANES)], *vectors) if number == 5 else []
        sent, vector, *extra = call(
            body, outs, *near, *vectors, *early, *operands, scratch=True
        )
        if number == 3:
            vectors[2] = extra[0]
        vectors.append(vector)
    arrived = lax.all_to_all(sent, ("gx", "gy", "gz"), 0, 0)
    *fast, good = call(fast_kernel, [shape, shape, None], arrived, *vectors, *extra)
    return lax.cond(good[0, 0] > 0, lambda first: tuple(fast), slow, vectors[0])


def solution(mesh):
    placed = P(None, "gz", "gx", "gy")
    return jax.shard_map(
        shards,
        mesh=mesh,
        in_specs=(placed, placed),
        out_specs=(placed, placed),
        check_vma=False,
    )
```
